32 devices in a mesh: dp: 4 (over x, core), seq: 8 (over z, y).
Axes of the slice: x: 2, y: 2, z: 4, core: 2. Of those that a mesh axis runs over, the one named last changes fastest.
Arguments:
- tokens: bfloat16 [16384, 1024], P(('dp', 'seq')), may hold values from -6 to 6
- ln_gain: bfloat16 [2, 1024], P(None, ('dp', 'seq')), may hold values from 0.5 to 1.5
- ln_shift: bfloat16 [2, 1024], P(None, ('dp', 'seq')), may hold values from -1.75 to 1.75
- w_gate: bfloat16 [2, 1024, 3072], P(None, None, ('dp', 'seq')), may hold values from -0.1875 to 0.1875
- w_reduce: bfloat16 [2, 1024, 512], P(None, None, ('dp', 'seq')), may hold values from -0.1875 to 0.1875
- decay_rate: bfloat16 [2, 512], P(None, ('dp', 'seq')), may hold values from 4.6386719e-05 to 0.034
- state_scale: bfloat16 [2, 512], P(None, ('dp', 'seq')), may hold values from -8 to 8
- skip_scale: bfloat16 [2, 512], P(None, ('dp', 'seq')), may hold values from -6 to 6
- w_expand: bfloat16 [2, 512, 3072], P(None, None, ('dp', 'seq')), may hold values from -0.25 to 0.25
- w_out: bfloat16 [2, 3072, 1024], P(None, ('dp', 'seq')), may hold values from -0.21875 to 0.21875
- prev_state: float32 [2, 4, 512], P(None, 'dp'), may hold values from -6 to 6
- item_lengths: int32 [4, 4], P('dp'), may hold values from 1 to 3840, 4096 in all within a row
- cotangent: bfloat16 [16384, 1024], P(('dp', 'seq')), may hold values from -6 to 6
Outputs:
- output: bfloat16 [16384, 1024], P(('dp', 'seq'))
- input_grad: bfloat16 [16384, 1024], P(('dp', 'seq'))
- grad_ln_gain: float32 [2, 1024], P(None, ('dp', 'seq'))
- grad_ln_shift: float32 [2, 1024], P(None, ('dp', 'seq'))
- grad_w_gate: float32 [2, 1024, 3072], P(None, None, ('dp', 'seq'))
- grad_w_reduce: float32 [2, 1024, 512], P(None, None, ('dp', 'seq'))
- grad_decay_rate: float32 [2, 512], P(None, ('dp', 'seq'))
- grad_state_scale: float32 [2, 512], P(None, ('dp', 'seq'))
- grad_skip_scale: float32 [2, 512], P(None, ('dp', 'seq'))
- grad_w_expand: float32 [2, 512, 3072], P(None, None, ('dp', 'seq'))
- grad_w_out: float32 [2, 3072, 1024], P(None, ('dp', 'seq'))
The draws below stay inside these ranges and needn't reach their ends.
Inputs may be any that keep to these rules, and one draw needn't show every extreme that they name: `item_lengths`: each row sums to 4096.
All inputs are finite; a program needn't handle non-finite values.
Results may differ from the reference program's by a relative error of at most 0.017.
Values may be sent and summed in bfloat16 or wider, within the bound.
No kernel may reach another device: no remote copies, remote signals or barrier semaphores. Data moves between devices by JAX's collectives and lax.ppermute only.
A program may use at most 256 MiB of HBM per device.

```python
import math
import jax
import jax.numpy as jnp
import numpy as np
from jax import lax

D = 1024
FF = 3072
R = 512
LAYERS = 2
ITEMS = 4
TOK_DEV = 512
GROUPS = 4
GROUP_TOK = 4096
TOKENS = 16384


def draw_decay_rate(key, part):
    key = jax.random.fold_in(key, 7)
    pick_key, slow_key, fast_key = jax.random.split(key, 3)
    share = 0.5
    chooser = jax.random.uniform(pick_key, (LAYERS, R), dtype=jnp.float32)
    slow_rate = jnp.exp(jax.random.uniform(slow_key, (LAYERS, R), dtype=jnp.float32, minval=jnp.log(0.2 / GROUP_TOK), maxval=jnp.log(2.0 / GROUP_TOK)))
    fast_rate = jnp.exp(jax.random.uniform(fast_key, (LAYERS, R), dtype=jnp.float32, minval=jnp.log(1.0 / 50.0), maxval=jnp.log(1.0 / 30.0)))
    return jnp.where(chooser < share, slow_rate, fast_rate).astype(jnp.bfloat16)


def shard_levels(rng, shape, cuts, smallest, top_value):
    loudness, own = 1.0, jax.random.fold_in(rng, 6)
    for dim, parts in cuts:
        draws = jnp.exp(jax.random.uniform(jax.random.fold_in(own, dim), (parts,), jnp.float32, smallest / len(cuts), top_value / len(cuts)))
        loudness = loudness * jnp.repeat(draws, shape[dim] // parts).reshape([-1 if axis == dim else 1 for axis in range(len(shape))])
    return loudness


def length_profile(count, total, bound, lean):
    weights = [(1 << 20) // math.isqrt(standing ** lean) + 1 for standing in range(2, count + 1)]
    surplus, holding = total - bound - (count - 1), [1] * (count - 1)
    while surplus > 0:
        candidates = [i for i in range(count - 1) if holding[i] < bound]
        mass, left = sum([weights[i] for i in candidates]), surplus
        for i in candidates:
            more = min(bound - holding[i], max(1, left * weights[i] // mass), surplus)
            holding[i] = holding[i] + more
            surplus = surplus - more
    return np.array([bound] + holding)


def ragged(stream_key, number_of, total, bound, lean):
    if number_of == 2:
        one = jax.random.randint(stream_key, (), max(1, total - bound), min(bound, total - 1) + 1)
        return jnp.stack([one, total - one])
    sizes = jnp.asarray(length_profile(number_of, total, bound, lean), jnp.int32)
    twos = (number_of - 1) // 2
    donor, taker = sizes[1:1 + 2 * twos:2], sizes[2:2 + 2 * twos:2]
    slack = jnp.minimum(donor - 1, bound - taker)
    passed = jax.random.randint(jax.random.fold_in(stream_key, 1), (twos,), 0, 1 << 20) % (slack + 1)
    sizes = sizes.at[1:1 + 2 * twos:2].set(donor - passed).at[2:2 + 2 * twos:2].set(taker + passed)
    return sizes[jax.random.permutation(jax.random.fold_in(stream_key, 2), number_of)]


def bell_draw(rng, extent, width, limit, pieces=(), kind=jnp.bfloat16):
    array = width * jax.random.normal(rng, extent, jnp.float32)
    if pieces:
        array = array * shard_levels(rng, extent, pieces, -0.22, 0.18)
    return jnp.clip(array, -limit, limit).astype(kind)


def setup_inputs(seed: int = 0) -> dict:
    key_list = jax.random.split(jax.random.key(seed), 14)
    return {
        "tokens": bell_draw(key_list[0], (TOKENS, D), 1.0, 6.0, ((0, 32),)),
        "ln_gain": jnp.clip(1.0 + 0.1 * jax.random.normal(key_list[1], (LAYERS, D), jnp.float32), 0.5, 1.5).astype(jnp.bfloat16),
        "ln_shift": bell_draw(key_list[2], (LAYERS, D), 0.3, 1.75, ((1, 32),)),
        "w_gate": bell_draw(key_list[3], (LAYERS, D, FF), D ** -0.5, 0.1875, ((2, 32),)),
        "w_reduce": bell_draw(key_list[4], (LAYERS, D, R), D ** -0.5, 0.1875, ((2, 32),)),
        "decay_rate": draw_decay_rate(jax.random.fold_in(key_list[13], 71), 0),
        "state_scale": bell_draw(key_list[6], (LAYERS, R), 1.5, 8.0, ((1, 32),)),
        "skip_scale": bell_draw(key_list[7], (LAYERS, R), 1.0, 6.0, ((1, 32),)),
        "w_expand": bell_draw(key_list[8], (LAYERS, R, FF), R ** -0.5, 0.25, ((2, 32),)),
        "w_out": bell_draw(key_list[9], (LAYERS, FF, D), (FF // 4) ** -0.5, 0.21875, ((1, 32),)),
        "prev_state": bell_draw(key_list[10], (LAYERS, GROUPS, R), 1.0, 6.0, ((1, 4),), jnp.float32),
        "item_lengths": jax.vmap(lambda own: ragged(own, ITEMS, GROUP_TOK, GROUP_TOK - TOK_DEV // 2, 2))(jax.random.split(key_list[11], GROUPS)).reshape((GROUPS, ITEMS)).astype(jnp.int32),
        "cotangent": bell_draw(key_list[12], (TOKENS, D), 1.0, 6.0, ((0, 32),)),
    }


@jax.custom_vjp
def low(v):
    return lax.optimization_barrier(v.astype(jnp.bfloat16)).astype(jnp.float32)

@jax.custom_vjp
def low_back(v):
    return v

def low_keep(v):
    return (low(v), None)

def low_pass(kept, grad):
    return (grad,)

def back_keep(v):
    return (v, None)

def back_low(kept, grad):
    return (low(grad),)
low.defvjp(low_keep, low_pass)
low_back.defvjp(back_keep, back_low)

def combine_pair(earlier, latter):
    return (earlier[0] * latter[0], latter[0] * earlier[1] + latter[1])

def normalize(stream, gain_vec, shift_vec):
    centre = lax.optimization_barrier(jnp.mean(stream, axis=-1, keepdims=True))
    centred = stream - centre
    spread = lax.optimization_barrier(jnp.mean(centred * centred, axis=-1, keepdims=True))
    return centred * lax.rsqrt(spread + 1e-05) * gain_vec + shift_vec

def product(left, right):
    return jnp.dot(left, right, precision=lax.Precision.HIGHEST)

def keep_mask(lengths):
    starts = jnp.cumsum(lengths)[:-1].astype(jnp.int32)
    positions = jnp.arange(GROUP_TOK, dtype=jnp.int32)
    hits = jnp.any(positions[:, None] == starts[None, :], axis=1)
    return 1.0 - hits.astype(jnp.float32)[:, None]

def gss_layer(stream, params, keep_rows, start_state):
    gain_vec, shift_vec, w_gate, w_reduce, rate_vec, scale_vec, skip_vec, w_expand, w_out = params
    normed = low(normalize(stream, gain_vec, shift_vec))
    pre_gate = low_back(product(normed, w_gate))
    pre_reduce = low_back(product(normed, w_reduce))
    gate_act = jax.nn.gelu(pre_gate)
    reduced = jax.nn.gelu(pre_reduce)
    decay_vec = jnp.exp(-rate_vec)
    multiplier = jnp.broadcast_to(decay_vec * keep_rows, reduced.shape)
    running, states = lax.associative_scan(combine_pair, (multiplier, (1.0 - decay_vec) * reduced), axis=0)
    states = states + running * start_state
    mixed = low(scale_vec * states + skip_vec * reduced)
    expanded = low_back(product(mixed, w_expand))
    joined = low(expanded * gate_act)
    branch = low_back(product(joined, w_out))
    return stream + branch

def reference(tokens, ln_gain, ln_shift, w_gate, w_reduce, decay_rate, state_scale, skip_scale, w_expand, w_out, prev_state, item_lengths, cotangent):
    weights = tuple((argument.astype(jnp.float32) for argument in (ln_gain, ln_shift, w_gate, w_reduce, decay_rate, state_scale, skip_scale, w_expand, w_out)))
    group_rows = tokens.reshape(GROUPS, GROUP_TOK, D)
    group_backs = cotangent.reshape(GROUPS, GROUP_TOK, D)
    group_states = jnp.swapaxes(prev_state, 0, 1).astype(jnp.float32)

    def group_pass(totals, inputs):
        rows_in, backs_in, lengths, start_states = inputs
        keep_rows = keep_mask(lengths)

        def forward(stream, *stacks):
            for layer_index in range(LAYERS):
                layer_params = tuple((stacked[layer_index] for stacked in stacks))
                stream = gss_layer(stream, layer_params, keep_rows, start_states[layer_index][None, :])
            return stream
        result, pullback = jax.vjp(forward, rows_in.astype(jnp.float32), *weights)
        gradients = pullback(backs_in.astype(jnp.float32))
        totals = tuple((running_sum + gradient for running_sum, gradient in zip(totals, gradients[1:])))
        return (totals, (result.astype(jnp.bfloat16), gradients[0].astype(jnp.bfloat16)))
    zero_grads = tuple((jnp.zeros_like(weight) for weight in weights))
    totals, outputs = lax.scan(group_pass, zero_grads, (group_rows, group_backs, item_lengths, group_states))
    results, input_grads = outputs
    grad_gain, grad_shift, grad_gate, grad_reduce, grad_rate, grad_scale, grad_skip, grad_expand, grad_out = totals
    return (results.reshape(TOKENS, D), input_grads.reshape(TOKENS, D), grad_gain, grad_shift, grad_gate, grad_reduce, grad_rate, grad_scale, grad_skip, grad_expand, grad_out)
```

```python
import functools
import itertools
import math

import jax
import jax.numpy as jnp
from jax import lax
from jax.experimental import pallas as pl
from jax.experimental.pallas import tpu as pltpu
from jax.sharding import PartitionSpec as P

LAYERS = 2
JOBS = 2
AXES = ("dp", "seq")
BF = jnp.bfloat16
F32 = jnp.float32
VMEM_LIMIT = 60 << 20
C0 = math.sqrt(2.0 / math.pi)
C1 = 0.044715
SMALL = 7
PAD = 128


class Layout:
    def __init__(self, mesh):
        self.dp, self.seq = mesh.shape["dp"], mesh.shape["seq"]
        self.x, self.c = self.dp // 2, 2
        self.s1 = 4
        self.s0 = self.seq // 4
        self.count = self.dp * self.seq
        self.alt_minor = self.s0 == self.x
        self.swap = self.s0 == self.x or self.s1 == self.x
        if self.alt_minor or not self.swap:
            self.alt, self.nq = self.s0, self.s1
        else:
            self.alt, self.nq = self.s1, self.s0
        self.n1, self.n2 = self.alt, self.x
        self.q = [self.pairs(self.move_q, k) for k in range(self.nq)]
        self.p1 = [self.pairs(self.move_1, k) for k in range(self.n1)]
        self.p2 = [self.pairs(self.move_2, k) for k in range(self.n2)]
        self.core = self.pairs(lambda x, c, a, q, k: (x, c ^ 1, a, q), 0)

    def place(self, x, c, a, q):
        s1, s0 = (q, a) if (self.alt_minor or not self.swap) else (a, q)
        return ((x * 2 + c) * self.s1 + s1) * self.s0 + s0

    def pairs(self, move, k):
        spots = itertools.product(range(self.x), range(2), range(self.alt), range(self.nq))
        return [(self.place(*spot), self.place(*move(*spot, k))) for spot in spots]

    def move_q(self, x, c, a, q, k):
        return (x, c, a, q ^ k)

    def move_1(self, x, c, a, q, k):
        return (x ^ k, c, a, q) if (self.swap and c == 1) else (x, c, a ^ k, q)

    def move_2(self, x, c, a, q, k):
        return (x, c, a ^ k, q) if (self.swap and c == 1) else (x ^ k, c, a, q)

    def natural_rows(self, rows):
        me_dp, me_seq = lax.axis_index("dp"), lax.axis_index("seq")
        mx, mc = me_dp // 2, me_dp % 2
        m1, m0 = me_seq // self.s0, me_seq % self.s0
        minor = self.alt_minor or not self.swap
        ma, mq = (m0, m1) if minor else (m1, m0)
        at = jnp.arange(self.count * rows, dtype=jnp.int32)
        row, at = at % rows, at // rows
        kq, at = at % self.nq, at // self.nq
        k1, at = at % self.n1, at // self.n1
        k2, half = at % self.n2, at // self.n2
        core = mc ^ half
        turned = (core == 1) if self.swap else (core > 1)
        kx = jnp.where(turned, k1, k2)
        ka = jnp.where(turned, k2, k1)
        x, a, q = mx ^ kx, ma ^ ka, mq ^ kq
        s1, s0 = (q, a) if minor else (a, q)
        return (((x * 2 + core) * self.s1 + s1) * self.s0 + s0) * rows + row


def permute(array, pairs):
    return lax.ppermute(array, AXES, pairs)


def cat(*arrays):
    return jnp.concatenate(arrays, axis=0)


def after(array, *others):
    return lax.optimization_barrier((array,) + others)[0]


def gather_job(lay, shard):
    line = cat(shard, *[permute(shard, lay.q[k]) for k in range(1, lay.nq)])
    plane = cat(line, *[permute(line, lay.p1[k]) for k in range(1, lay.n1)])
    own = cat(plane, *[permute(plane, lay.p2[k]) for k in range(1, lay.n2)])
    return own, permute(own, lay.core), line


def add_parts(parts, dtype):
    total = parts[0].astype(F32)
    for part in parts[1:]:
        total = total + part.astype(F32)
    return total.astype(dtype)


def scatter_job(lay, own, other):
    dtype = own.dtype
    held = add_parts([own, permute(other, lay.core)], dtype)
    for pairs, count, kind in ((lay.p2, lay.n2, dtype), (lay.p1, lay.n1, dtype), (lay.q, lay.nq, F32)):
        rows = held.shape[0] // count
        parts = [held[:rows]]
        for k in range(1, count):
            parts.append(permute(held[k * rows : (k + 1) * rows], pairs[k]))
        held = add_parts(parts, kind)
    return held


def dot_nn(a, b):
    return jnp.dot(a, b, preferred_element_type=F32)


def dot_nt(a, b):
    return lax.dot_general(a, b, (((1,), (1,)), ((), ())), preferred_element_type=F32)


def dot_tn(a, b):
    return lax.dot_general(a, b, (((0,), (0,)), ((), ())), preferred_element_type=F32)


def gelu(v):
    return 0.5 * v * (1.0 + jnp.tanh(C0 * (v + C1 * v * v * v)))


def gelu_both(v):
    square = v * v
    t = jnp.tanh(C0 * (v + C1 * v * square))
    half = 0.5 * (1.0 + t)
    slope = half + 0.5 * v * (1.0 - t * t) * (C0 * (1.0 + 3.0 * C1 * square))
    return v * half, slope


def full_spec(shape):
    return pl.BlockSpec(shape, lambda *_: (0,) * len(shape))


SCALARS = pl.BlockSpec(memory_space=pltpu.SMEM)


def enter_kernel(starts_n, scal, x_ref, gain_ref, shift_ref, wr_ref, rate_ref, normed_ref, pre_ref, local_ref):
    x = x_ref[...].astype(F32)
    centred = x - jnp.mean(x, axis=-1, keepdims=True)
    spread = jnp.mean(centred * centred, axis=-1, keepdims=True)
    normed = (centred * lax.rsqrt(spread + 1e-05) * gain_ref[...] + shift_ref[...]).astype(BF)
    normed_ref[...] = normed
    pre = dot_nt(normed, wr_ref[...])
    pre_ref[...] = pre
    rate = rate_ref[...]
    state = (1.0 - jnp.exp(-rate)) * gelu(pre)
    rows = state.shape[0]
    row = lax.broadcasted_iota(jnp.int32, (rows, 1), 0)
    k = 1
    while k < rows:
        open_rows = row >= k
        for s in range(starts_n):
            open_rows = open_rows & ~((row >= scal[s]) & (row < scal[s] + k))
        factor = jnp.where(open_rows, jnp.exp(-float(k) * rate), 0.0)
        state = state + factor * pltpu.roll(state, k, 0)
        k *= 2
    local_ref[...] = state


def enter_call(starts, x, gain, shift, wr, rate):
    rows, width = x.shape
    chan = wr.shape[0]
    return pl.pallas_call(
        functools.partial(enter_kernel, starts.shape[0]),
        out_shape=(
            jax.ShapeDtypeStruct((rows, width), BF),
            jax.ShapeDtypeStruct((rows, chan), F32),
            jax.ShapeDtypeStruct((rows, chan), F32),
        ),
        in_specs=[SCALARS] + [pl.BlockSpec(memory_space=pltpu.VMEM)] * 5,
        out_specs=(pl.BlockSpec(memory_space=pltpu.VMEM),) * 3,
        compiler_params=pltpu.CompilerParams(vmem_limit_bytes=VMEM_LIMIT),
        cost_estimate=pl.CostEstimate(
            flops=2 * rows * width * chan, bytes_accessed=10 * rows * width, transcendentals=rows * chan
        ),
        name="enter",
    )(starts, x, gain, shift, wr, rate)


def back_scan_kernel(starts_n, scal, dmix_ref, rate_ref, scale_ref, local_ref):
    rate = rate_ref[...]
    grad = scale_ref[...] * dmix_ref[...]
    rows = grad.shape[0]
    row = lax.broadcasted_iota(jnp.int32, (rows, 1), 0)
    k = 1
    while k < rows:
        open_rows = row < rows - k
        for s in range(starts_n):
            open_rows = open_rows & ~((row < scal[s]) & (row >= scal[s] - k))
        factor = jnp.where(open_rows, jnp.exp(-float(k) * rate), 0.0)
        grad = grad + factor * pltpu.roll(grad, rows - k, 0)
        k *= 2
    local_ref[...] = grad


def back_scan_call(starts, dmix, rate, scale):
    rows, chan = dmix.shape
    return pl.pallas_call(
        functools.partial(back_scan_kernel, starts.shape[0]),
        out_shape=jax.ShapeDtypeStruct((rows, chan), F32),
        in_specs=[SCALARS] + [pl.BlockSpec(memory_space=pltpu.VMEM)] * 3,
        out_specs=pl.BlockSpec(memory_space=pltpu.VMEM),
        compiler_params=pltpu.CompilerParams(vmem_limit_bytes=VMEM_LIMIT),
        cost_estimate=pl.CostEstimate(flops=40 * rows * chan, bytes_accessed=8 * rows * chan, transcendentals=0),
        name="back_scan",
    )(starts, dmix, rate, scale)


def leave_kernel(
    starts_n,
    scal,
    dmix_ref,
    local_ref,
    arriving_ref,
    states_ref,
    state_in_ref,
    pre_ref,
    normed_ref,
    x_ref,
    gain_ref,
    wr_ref,
    dnorm_ref,
    up_ref,
    rate_ref,
    scale_ref,
    skip_ref,
    up_out_ref,
    low_ref,
    grad_ref,
    small_ref,
):
    rate = rate_ref[...]
    decay = jnp.exp(-rate)
    dmix = dmix_ref[...]
    rows, chan = dmix.shape
    row = lax.broadcasted_iota(jnp.int32, (rows, 1), 0)
    later = row >= 0
    first = row < 0
    for s in range(starts_n):
        later = later & ~((row < scal[s]) & (scal[s] < rows))
        first = first | (row == scal[s])
    left = (rows - 1 - row).astype(F32)
    running = jnp.where(later, jnp.exp(-left * rate), 0.0)
    grad = local_ref[...] + running * arriving_ref[...]
    reduced, slope = gelu_both(pre_ref[...])
    states = states_ref[...]
    before = jnp.where(row == 0, state_in_ref[...], pltpu.roll(states, 1, 0))
    before = jnp.where(first, 0.0, before)
    small_ref[...] = jnp.zeros_like(small_ref)
    small_ref[2:3, :chan] = -decay * jnp.sum(grad * (before - reduced), axis=0, keepdims=True)
    small_ref[3:4, :chan] = jnp.sum(dmix * states, axis=0, keepdims=True)
    small_ref[4:5, :chan] = jnp.sum(dmix * reduced, axis=0, keepdims=True)
    d_reduced = (1.0 - decay) * grad + skip_ref[...] * dmix
    d_pre = (d_reduced * slope).astype(BF)
    grad_ref[...] = dot_tn(d_pre, normed_ref[...])
    d_normed = dnorm_ref[...] + dot_nn(d_pre, wr_ref[...])
    x = x_ref[...].astype(F32)
    centred = x - jnp.mean(x, axis=-1, keepdims=True)
    spread = jnp.mean(centred * centred, axis=-1, keepdims=True)
    rs = lax.rsqrt(spread + 1e-05)
    xhat = centred * rs
    small_ref[0:1, :] = jnp.sum(d_normed * xhat, axis=0, keepdims=True)
    small_ref[1:2, :] = jnp.sum(d_normed, axis=0, keepdims=True)
    e = d_normed * gain_ref[...]
    mean_e = jnp.mean(e, axis=-1, keepdims=True)
    mean_ex = jnp.mean(e * xhat, axis=-1, keepdims=True)
    up = up_ref[...].astype(F32) + rs * (e - mean_e - xhat * mean_ex)
    up_out_ref[...] = up
    low_ref[...] = up.astype(BF)


def leave_call(starts, dmix, local, arriving, states, state_in, pre, normed, x, gain, wr, dnorm, up, rate, scale, skip):
    rows, width = x.shape
    chan = dmix.shape[1]
    return pl.pallas_call(
        functools.partial(leave_kernel, starts.shape[0]),
        out_shape=(
            jax.ShapeDtypeStruct((rows, width), F32),
            jax.ShapeDtypeStruct((rows, width), BF),
            jax.ShapeDtypeStruct((chan, width), F32),
            jax.ShapeDtypeStruct((8, width), F32),
        ),
        in_specs=[SCALARS] + [pl.BlockSpec(memory_space=pltpu.VMEM)] * 15,
        out_specs=(pl.BlockSpec(memory_space=pltpu.VMEM),) * 4,
        compiler_params=pltpu.CompilerParams(vmem_limit_bytes=VMEM_LIMIT),
        cost_estimate=pl.CostEstimate(
            flops=4 * rows * width * chan, bytes_accessed=24 * rows * width, transcendentals=rows * chan
        ),
        name="leave",
    )(starts, dmix, local, arriving, states, state_in, pre, normed, x, gain, wr, dnorm, up, rate, scale, skip)


def wide_kernel(names, mode, blocks, dims, *refs):
    r = dict(zip(names, refs))
    width, chan = dims
    step = pl.program_id(0)
    forward, backward = mode != "back", mode != "fore"
    weights = r["weights"]

    @pl.when(step == 0)
    def _():
        if forward:
            r["acc"][...] = r["base"][...].astype(F32)
        if backward:
            r["d_normed"][...] = r["d_normed_in"][...] if "d_normed_in" in r else jnp.zeros_like(r["d_normed"])
            r["d_mixed"][...] = r["d_mixed_in"][...] if "d_mixed_in" in r else jnp.zeros_like(r["d_mixed"])

    @pl.when(step < blocks)
    def _():
        weights[...] = r["own"][...]

    @pl.when(step >= blocks)
    def _():
        weights[...] = r["other"][...]

    normed, mixed = r["normed"][...], r["mixed"][...]
    if forward:
        pre = dot_nt(normed, weights[:, :width])
        expanded = dot_nt(mixed, weights[:, 2 * width :])
        if mode == "fore":
            r["pre"][...] = pre
            r["expanded"][...] = expanded
    else:
        pre, expanded = r["pre"][...], r["expanded"][...]
    if backward:
        gate, slope = gelu_both(pre)
    else:
        gate = gelu(pre)
    joined = (expanded * gate).astype(BF)
    if forward:
        r["acc"][...] += dot_nn(joined, weights[:, width : 2 * width])
    if backward:
        low = r["low"][...]
        d_joined = dot_nt(low, weights[:, width : 2 * width])
        d_expanded = (d_joined * gate).astype(BF)
        d_pre = (d_joined * expanded * slope).astype(BF)
        r["d_mixed"][...] += dot_nn(d_expanded, weights[:, 2 * width :])
        r["d_normed"][...] += dot_nn(d_pre, weights[:, :width])

        def store(out):
            out[:, :width] = dot_tn(d_pre, normed).astype(BF)
            out[:, width : 2 * width] = dot_tn(joined, low).astype(BF)
            out[:, 2 * width :] = dot_tn(d_expanded, mixed).astype(BF)

        grads = r["grads"]
        store(grads)

        @pl.when(step < blocks)
        def _():
            r["grad_own"][...] = grads[...]

        @pl.when(step >= blocks)
        def _():
            r["grad_other"][...] = grads[...]

    if "out" in r:

        @pl.when(step == 2 * blocks - 1)
        def _():
            r["out"][...] = r["acc"][...].astype(r["out"].dtype)


def wide_call(mode, own, other, normed, mixed, base=None, low=None, pre=None, expanded=None, sums=None, out_dtype=None):
    rows, width = normed.shape
    chan = mixed.shape[1]
    span = own.shape[0]
    block = span // 2 if span % 32 == 0 else span
    blocks = span // block
    lanes = own.shape[1]
    forward, backward = mode != "back", mode != "fore"
    ins, outs, scratch = [], [], []
    ins.append(("own", own, pl.BlockSpec((block, lanes), lambda i: (jnp.minimum(i, blocks - 1), 0))))
    ins.append(("other", other, pl.BlockSpec((block, lanes), lambda i: (jnp.maximum(i - blocks, 0), 0))))
    ins.append(("normed", normed, full_spec(normed.shape)))
    ins.append(("mixed", mixed, full_spec(mixed.shape)))
    saved = pl.BlockSpec((rows, block), lambda i: (0, i))
    saved_shape = jax.ShapeDtypeStruct((rows, 2 * span), F32)
    if forward:
        ins.append(("base", base, full_spec(base.shape)))
    if backward:
        ins.append(("low", low, full_spec(low.shape)))
        if sums is not None:
            ins.append(("d_normed_in", sums[0], full_spec(sums[0].shape)))
            ins.append(("d_mixed_in", sums[1], full_spec(sums[1].shape)))
    if mode == "back":
        ins.append(("pre", pre, saved))
        ins.append(("expanded", expanded, saved))
    if mode == "fore":
        outs.append(("pre", saved_shape, saved))
        outs.append(("expanded", saved_shape, saved))
    if forward:
        if out_dtype == F32:
            outs.append(("acc", jax.ShapeDtypeStruct((rows, width), F32), full_spec((rows, width))))
        else:
            outs.append(("out", jax.ShapeDtypeStruct((rows, width), out_dtype), full_spec((rows, width))))
            scratch.append(("acc", pltpu.VMEM((rows, width), F32)))
    if backward:
        outs.append(("d_normed", jax.ShapeDtypeStruct((rows, width), F32), full_spec((rows, width))))
        outs.append(("d_mixed", jax.ShapeDtypeStruct((rows, chan), F32), full_spec((rows, chan))))
        grad = jax.ShapeDtypeStruct((span, lanes), BF)
        outs.append(("grad_own", grad, pl.BlockSpec((block, lanes), lambda i: (jnp.minimum(i, blocks - 1), 0))))
        outs.append(("grad_other", grad, pl.BlockSpec((block, lanes), lambda i: (jnp.maximum(i - blocks, 0), 0))))
        scratch.append(("grads", pltpu.VMEM((block, lanes), BF)))
    scratch.append(("weights", pltpu.VMEM((block, lanes), BF)))
    names = [name for name, _, _ in ins + outs] + [name for name, _ in scratch]
    passes = (1 if forward else 0) + (2 if backward else 0)
    return pl.pallas_call(
        functools.partial(wide_kernel, names, mode, blocks, (width, chan)),
        grid=(2 * blocks,),
        out_shape=tuple(shape for _, shape, _ in outs),
        in_specs=[spec for _, _, spec in ins],
        out_specs=tuple(spec for _, _, spec in outs),
        scratch_shapes=[shape for _, shape in scratch],
        compiler_params=pltpu.CompilerParams(vmem_limit_bytes=VMEM_LIMIT),
        cost_estimate=pl.CostEstimate(
            flops=2 * passes * rows * 2 * span * lanes,
            bytes_accessed=8 * span * lanes,
            transcendentals=rows * 2 * span,
        ),
        name="wide_" + mode,
    )(*[array for _, array, _ in ins])


def seq_gather(lay, vector):
    held, k = vector, 1
    while k < lay.seq:
        pairs = [
            (d * lay.seq + s, d * lay.seq + (s ^ k)) for d in range(lay.dp) for s in range(lay.seq)
        ]
        held = cat(held, permute(held, pairs))
        k *= 2
    return held


def clear_between(starts, low, high):
    hit = (starts[None, :] >= low[:, None]) & (starts[None, :] < high[:, None])
    return ~jnp.any(hit, axis=1)


def carry_forward(lay, lasts, start_state, rate, starts, rows):
    me = lax.axis_index("seq")
    source = me ^ jnp.arange(lay.seq, dtype=jnp.int32)
    hops = me - 1 - source
    live = (hops >= 0) & clear_between(starts, (source + 1) * rows, jnp.full_like(source, me * rows))
    weight = jnp.where(live[:, None], jnp.exp(-(jnp.maximum(hops, 0) * rows).astype(F32)[:, None] * rate), 0.0)
    open_start = ~jnp.any(starts < me * rows)
    start_weight = jnp.where(open_start, jnp.exp(-(me * rows).astype(F32) * rate), 0.0)
    return jnp.sum(weight * lasts, axis=0, keepdims=True) + start_weight * start_state


def carry_backward(lay, firsts, rate, starts, rows):
    me = lax.axis_index("seq")
    source = me ^ jnp.arange(lay.seq, dtype=jnp.int32)
    hops = source - me - 1
    live = (hops >= 0) & clear_between(starts, jnp.full_like(source, (me + 1) * rows), source * rows)
    weight = jnp.where(live[:, None], jnp.exp(-(jnp.maximum(hops, 0) * rows).astype(F32)[:, None] * rate), 0.0)
    return jnp.sum(weight * firsts, axis=0, keepdims=True)


def local(
    lay,
    tokens,
    ln_gain,
    ln_shift,
    w_gate,
    w_reduce,
    decay_rate,
    state_scale,
    skip_scale,
    w_expand,
    w_out,
    prev_state,
    item_lengths,
    cotangent,
):
    rows, width = tokens.shape
    chan = w_expand.shape[1]
    small_rows = w_reduce.shape[2]
    ff_rows = w_gate.shape[2]
    job_rows = ff_rows // JOBS
    me_seq = lax.axis_index("seq")
    starts = jnp.cumsum(item_lengths[0])[:-1].astype(jnp.int32)
    near = starts - me_seq * rows
    pos = jnp.arange(rows, dtype=jnp.int32)

    def vectors(layer):
        return jnp.concatenate(
            [
                ln_gain[layer].reshape(small_rows, 2),
                ln_shift[layer].reshape(small_rows, 2),
                decay_rate[layer][:, None],
                state_scale[layer][:, None],
                skip_scale[layer][:, None],
                jnp.zeros((small_rows, PAD - SMALL), BF),
            ],
            axis=1,
        )

    head = cat(*[jnp.concatenate([w_reduce[i].T, vectors(i)], axis=1) for i in range(LAYERS)])
    head_own, head_other, tie = gather_job(lay, head)
    relative = cat(head_own, head_other).reshape(lay.count, LAYERS, small_rows, width + PAD)
    relative = jnp.swapaxes(relative, 0, 1).reshape(LAYERS, chan, width + PAD)
    nature = lay.natural_rows(small_rows)
    turn = (nature[None, :] == jnp.arange(chan, dtype=jnp.int32)[:, None])
    turn_low = turn.astype(BF)

    params = []
    for layer in range(LAYERS):
        whole = dot_nn(turn_low, relative[layer]).astype(BF)
        vec = whole[:, width : width + SMALL].astype(F32)
        params.append(
            dict(
                wr=whole[:, :width],
                gain=vec[:, 0:2].reshape(1, width),
                shift=vec[:, 2:4].reshape(1, width),
                rate=vec[:, 4].reshape(1, chan),
                scale=vec[:, 5].reshape(1, chan),
                skip=vec[:, 6].reshape(1, chan),
            )
        )

    weights = []
    for layer in range(LAYERS):
        bundle = jnp.concatenate([w_gate[layer].T, w_out[layer], w_expand[layer].T], axis=1)
        jobs = []
        for job in range(JOBS):
            shard = after(bundle[job * job_rows : (job + 1) * job_rows], tie)
            own, other, tie = gather_job(lay, shard)
            jobs.append((own, other))
        weights.append(jobs)

    def enter(layer, stream):
        p = params[layer]
        normed, pre_reduce, local_states = enter_call(near, stream, p["gain"], p["shift"], p["wr"], p["rate"])
        lasts = seq_gather(lay, local_states[rows - 1 :])
        state_in = carry_forward(lay, lasts, prev_state[layer], p["rate"], starts, rows)
        closed = jnp.any((near[None, :] >= 0) & (near[None, :] <= pos[:, None]), axis=1)[:, None]
        running = jnp.where(closed, 0.0, jnp.exp(-(pos + 1).astype(F32)[:, None] * p["rate"]))
        states = local_states + running * state_in
        mixed = (p["scale"] * states + p["skip"] * jax.nn.gelu(pre_reduce)).astype(BF)
        return dict(stream=stream, normed=normed, pre_reduce=pre_reduce, states=states, state_in=state_in, mixed=mixed)

    def leave(layer, kept, sums, upstream):
        p = params[layer]
        d_normed, d_mixed = sums
        back_local = back_scan_call(near, d_mixed, p["rate"], p["scale"])
        keep_first = jnp.where(jnp.any(near == 0), 0.0, 1.0)
        firsts = seq_gather(lay, keep_first * jnp.exp(-p["rate"]) * back_local[:1])
        arriving = carry_backward(lay, firsts, p["rate"], starts, rows)
        upstream, low, grad_reduce, small = leave_call(
            near,
            d_mixed,
            back_local,
            arriving,
            kept["states"],
            kept["state_in"],
            kept["pre_reduce"],
            kept["normed"],
            kept["stream"],
            p["gain"],
            p["wr"],
            d_normed,
            upstream,
            p["rate"],
            p["scale"],
            p["skip"],
        )
        vec = jnp.concatenate(
            [
                small[0].reshape(chan, 2),
                small[1].reshape(chan, 2),
                small[2:5, :chan].T,
                jnp.zeros((chan, PAD - SMALL), F32),
            ],
            axis=1,
        )
        bundle = jnp.concatenate([grad_reduce, vec], axis=1)
        moved = jnp.dot(turn.astype(F32).T, bundle, precision=lax.Precision.HIGHEST)
        half = chan // 2
        return upstream, low, scatter_job(lay, moved[:half], moved[half:])

    kept, stream = [], tokens
    saved = []
    for layer in range(LAYERS - 1):
        k = enter(layer, stream)
        acc, done = stream, []
        for own, other in weights[layer]:
            pre, expanded, acc = wide_call("fore", own, other, k["normed"], k["mixed"], base=acc, out_dtype=F32)
            done.append((pre, expanded))
        stream = acc
        kept.append(k)
        saved.append(done)

    top = LAYERS - 1
    k = enter(top, stream)
    kept.append(k)
    acc, sums = stream, None
    scattered = [[None] * JOBS for _ in range(LAYERS)]
    low = cotangent
    for job, (own, other) in enumerate(weights[top]):
        last = job == JOBS - 1
        acc, d_normed, d_mixed, grad_own, grad_other = wide_call(
            "both", own, other, k["normed"], k["mixed"], base=acc, low=low, sums=sums, out_dtype=BF if last else F32
        )
        sums = (d_normed, d_mixed)
        scattered[top][job] = scatter_job(lay, grad_own, grad_other)
    output = acc
    heads = [None] * LAYERS
    upstream, low, heads[top] = leave(top, k, sums, cotangent)

    for layer in reversed(range(top)):
        k, sums = kept[layer], None
        for job, (own, other) in enumerate(weights[layer]):
            pre, expanded = saved[layer][job]
            d_normed, d_mixed, grad_own, grad_other = wide_call(
                "back", own, other, k["normed"], k["mixed"], low=low, pre=pre, expanded=expanded, sums=sums
            )
            sums = (d_normed, d_mixed)
            scattered[layer][job] = scatter_job(lay, grad_own, grad_other)
        upstream, low, heads[layer] = leave(layer, k, sums, upstream)

    whole = [cat(*scattered[layer]) for layer in range(LAYERS)]
    vecs = [heads[layer][:, width : width + SMALL] for layer in range(LAYERS)]
    return (
        output,
        low,
        jnp.stack([v[:, 0:2].reshape(-1) for v in vecs]),
        jnp.stack([v[:, 2:4].reshape(-1) for v in vecs]),
        jnp.stack([g[:, :width].T for g in whole]),
        jnp.stack([h[:, :width].T for h in heads]),
        jnp.stack([v[:, 4] for v in vecs]),
        jnp.stack([v[:, 5] for v in vecs]),
        jnp.stack([v[:, 6] for v in vecs]),
        jnp.stack([g[:, 2 * width :].T for g in whole]),
        jnp.stack([g[:, width : 2 * width] for g in whole]),
    )


def solution(mesh):
    lay = Layout(mesh)
    both = ("dp", "seq")
    return jax.shard_map(
        functools.partial(local, lay),
        mesh=mesh,
        in_specs=(
            P(both, None),
            P(None, both),
            P(None, both),
            P(None, None, both),
            P(None, None, both),
            P(None, both),
            P(None, both),
            P(None, both),
            P(None, None, both),
            P(None, both, None),
            P(None, "dp", None),
            P("dp", None),
            P(both, None),
        ),
        out_specs=(
            P(both, None),
            P(both, None),
            P(None, both),
            P(None, both),
            P(None, None, both),
            P(None, None, both),
            P(None, both),
            P(None, both),
            P(None, both),
            P(None, None, both),
            P(None, both, None),
        ),
        check_vma=False,
    )
```

```python
import functools
import itertools
import math

import jax
import jax.numpy as jnp
from jax import lax
from jax.experimental import pallas as pl
from jax.experimental.pallas import tpu as pltpu
from jax.sharding import PartitionSpec as P

LAYERS = 2
JOBS = 2
AXES = ("dp", "seq")
BF = jnp.bfloat16
F32 = jnp.float32
VMEM_LIMIT = 60 << 20
C0 = math.sqrt(2.0 / math.pi)
C1 = 0.044715
SMALL = 7
PAD = 128


class Layout:
    def __init__(self, mesh):
        self.dp, self.seq = mesh.shape["dp"], mesh.shape["seq"]
        self.x, self.c = self.dp // 2, 2
        self.s1 = 4
        self.s0 = self.seq // 4
        self.count = self.dp * self.seq
        self.alt_minor = self.s0 == self.x
        self.swap = self.s0 == self.x or self.s1 == self.x
        if self.alt_minor or not self.swap:
            self.alt, self.nq = self.s0, self.s1
        else:
            self.alt, self.nq = self.s1, self.s0
        self.n1, self.n2 = self.alt, self.x
        self.q = [self.pairs(self.move_q, k) for k in range(self.nq)]
        self.p1 = [self.pairs(self.move_1, k) for k in range(self.n1)]
        self.p2 = [self.pairs(self.move_2, k) for k in range(self.n2)]
        self.core = self.pairs(lambda x, c, a, q, k: (x, c ^ 1, a, q), 0)

    def place(self, x, c, a, q):
        s1, s0 = (q, a) if (self.alt_minor or not self.swap) else (a, q)
        return ((x * 2 + c) * self.s1 + s1) * self.s0 + s0

    def pairs(self, move, k):
        spots = itertools.product(range(self.x), range(2), range(self.alt), range(self.nq))
        return [(self.place(*spot), self.place(*move(*spot, k))) for spot in spots]

    def move_q(self, x, c, a, q, k):
        return (x, c, a, q ^ k)

    def move_1(self, x, c, a, q, k):
        return (x ^ k, c, a, q) if (self.swap and c == 1) else (x, c, a ^ k, q)

    def move_2(self, x, c, a, q, k):
        return (x, c, a ^ k, q) if (self.swap and c == 1) else (x ^ k, c, a, q)

    def natural_rows(self, rows):
        me_dp, me_seq = lax.axis_index("dp"), lax.axis_index("seq")
        mx, mc = me_dp // 2, me_dp % 2
        m1, m0 = me_seq // self.s0, me_seq % self.s0
        minor = self.alt_minor or not self.swap
        ma, mq = (m0, m1) if minor else (m1, m0)
        at = jnp.arange(self.count * rows, dtype=jnp.int32)
        row, at = at % rows, at // rows
        kq, at = at % self.nq, at // self.nq
        k1, at = at % self.n1, at // self.n1
        k2, half = at % self.n2, at // self.n2
        core = mc ^ half
        turned = (core == 1) if self.swap else (core > 1)
        kx = jnp.where(turned, k1, k2)
        ka = jnp.where(turned, k2, k1)
        x, a, q = mx ^ kx, ma ^ ka, mq ^ kq
        s1, s0 = (q, a) if minor else (a, q)
        return (((x * 2 + core) * self.s1 + s1) * self.s0 + s0) * rows + row


def permute(array, pairs):
    return lax.ppermute(array, AXES, pairs)


def cat(*arrays):
    return jnp.concatenate(arrays, axis=0)


def after(array, *others):
    return lax.optimization_barrier((array,) + others)[0]


def fence(*arrays):
    return lax.optimization_barrier(arrays)


def spread_lanes(block):
    third = block.shape[1] // 3
    return cat(*[block[:, i * third : (i + 1) * third] for i in range(3)])


def close_lanes(block, rows):
    parts = block.reshape(-1, 3, rows, block.shape[1])
    return jnp.concatenate([parts[:, i] for i in range(3)], axis=-1).reshape(-1, 3 * block.shape[1])


def stage(array, pairs):
    return cat(array, *[permute(array, pairs[k]) for k in range(1, len(pairs))])


def add_parts(parts, dtype):
    total = parts[0].astype(F32)
    for part in parts[1:]:
        total = total + part.astype(F32)
    return total.astype(dtype)


def fold(array, pairs, dtype=None):
    count = len(pairs)
    rows = array.shape[0] // count
    parts = [array[:rows]]
    for k in range(1, count):
        parts.append(permute(array[k * rows : (k + 1) * rows], pairs[k]))
    return add_parts(parts, dtype or array.dtype)


def dot_nn(a, b):
    return jnp.dot(a, b, preferred_element_type=F32)


def dot_nt(a, b):
    return lax.dot_general(a, b, (((1,), (1,)), ((), ())), preferred_element_type=F32)


def dot_tn(a, b):
    return lax.dot_general(a, b, (((0,), (0,)), ((), ())), preferred_element_type=F32)


def gelu(v):
    return 0.5 * v * (1.0 + jnp.tanh(C0 * (v + C1 * v * v * v)))


def gelu_both(v):
    square = v * v
    t = jnp.tanh(C0 * (v + C1 * v * square))
    half = 0.5 * (1.0 + t)
    slope = half + 0.5 * v * (1.0 - t * t) * (C0 * (1.0 + 3.0 * C1 * square))
    return v * half, slope


def full_spec(shape):
    return pl.BlockSpec(shape, lambda *_: (0,) * len(shape))


COST = pl.CostEstimate(flops=1000, bytes_accessed=1000, transcendentals=0)
SCALARS = pl.BlockSpec(memory_space=pltpu.SMEM)
VMEM = pl.BlockSpec(memory_space=pltpu.VMEM)


def one_hot(left, right):
    return jnp.where(left == right, 1.0, 0.0).astype(BF)


def column(count):
    return lax.broadcasted_iota(jnp.int32, (count, 1), 0)


def lane(count):
    return lax.broadcasted_iota(jnp.int32, (1, count), 1)


GAIN, SHIFT, RATE, SCALE, SKIP = range(5)


def params_kernel(lanes, dims, key_ref, own_hbm, other_hbm, wr_ref, rows_ref, own, other, sem):
    width, chan = dims
    span = own.shape[1] // LAYERS
    half = own.shape[0]
    pull_own = pltpu.make_async_copy(own_hbm.at[:, pl.ds(lanes, LAYERS * span)], own, sem.at[0])
    pull_other = pltpu.make_async_copy(other_hbm.at[:, pl.ds(lanes, LAYERS * span)], other, sem.at[1])
    pull_own.start()
    pull_other.start()
    pull_own.wait()
    pull_other.wait()
    rows_ref[...] = jnp.zeros_like(rows_ref)
    turns = []
    for g in range(3):
        key = key_ref[...] - g * chan
        turns.append((one_hot(key[:, :half], column(chan)), one_hot(key[:, half:], column(chan))))
    even = one_hot(2 * column(chan), lane(width))
    odd = one_hot(2 * column(chan) + 1, lane(width))
    same = one_hot(column(chan), lane(chan))
    for layer in range(LAYERS):
        at = layer * span
        for g, (turn_own, turn_other) in enumerate(turns):
            part = dot_nn(turn_own, own[:, at : at + span]) + dot_nn(turn_other, other[:, at : at + span])
            part = part.astype(BF)
            low, high = g * span, min((g + 1) * span, width)
            wr_ref[layer, :, low:high] = part[:, : high - low]
        vec = part[:, width - 2 * span :]
        evens, odds = dot_tn(vec, even), dot_tn(vec, odd)
        turned = dot_tn(vec, same)
        rows_ref[layer, GAIN : GAIN + 1, :] = evens[0:1] + odds[1:2]
        rows_ref[layer, SHIFT : SHIFT + 1, :] = evens[2:3] + odds[3:4]
        for name, k in ((RATE, 4), (SCALE, 5), (SKIP, 6)):
            rows_ref[layer, name : name + 1, :chan] = turned[k : k + 1]


def params_call(key, own, other, lanes, width, chan):
    half = own.shape[0]
    span = (own.shape[1] - lanes) // LAYERS
    return pl.pallas_call(
        functools.partial(params_kernel, lanes, (width, chan)),
        out_shape=(
            jax.ShapeDtypeStruct((LAYERS, chan, width), BF),
            jax.ShapeDtypeStruct((LAYERS, 8, width), F32),
        ),
        in_specs=[VMEM, pl.BlockSpec(memory_space=pl.ANY), pl.BlockSpec(memory_space=pl.ANY)],
        out_specs=(VMEM,) * 2,
        scratch_shapes=[
            pltpu.VMEM((half, LAYERS * span), BF),
            pltpu.VMEM((half, LAYERS * span), BF),
            pltpu.SemaphoreType.DMA((2,)),
        ],
        compiler_params=pltpu.CompilerParams(vmem_limit_bytes=VMEM_LIMIT),
        cost_estimate=COST,
        name="params",
    )(key, own, other)


def enter_kernel(starts_n, layer, scal, x_ref, rows_ref, wr_ref, normed_ref, pre_ref, local_ref, last_ref):
    x = x_ref[...].astype(F32)
    centred = x - jnp.mean(x, axis=-1, keepdims=True)
    spread = jnp.mean(centred * centred, axis=-1, keepdims=True)
    gain, shift = rows_ref[layer, GAIN : GAIN + 1, :], rows_ref[layer, SHIFT : SHIFT + 1, :]
    normed = (centred * lax.rsqrt(spread + 1e-05) * gain + shift).astype(BF)
    normed_ref[...] = normed
    pre = dot_nt(normed, wr_ref[layer])
    pre_ref[...] = pre
    rows, chan = pre.shape
    rate = rows_ref[layer, RATE : RATE + 1, :chan]
    state = (1.0 - jnp.exp(-rate)) * gelu(pre)
    row = column(rows)
    k = 1
    while k < rows:
        open_rows = row >= k
        for s in range(starts_n):
            open_rows = open_rows & ~((row >= scal[s]) & (row < scal[s] + k))
        factor = jnp.where(open_rows, jnp.exp(-float(k) * rate), 0.0)
        state = state + factor * pltpu.roll(state, k, 0)
        k *= 2
    local_ref[...] = state
    last_ref[...] = state[rows - 1 :]


def enter_call(layer, starts, x, rows_all, wr_all):
    rows, width = x.shape
    chan = wr_all.shape[1]
    return pl.pallas_call(
        functools.partial(enter_kernel, starts.shape[0], layer),
        out_shape=(
            jax.ShapeDtypeStruct((rows, width), BF),
            jax.ShapeDtypeStruct((rows, chan), F32),
            jax.ShapeDtypeStruct((rows, chan), F32),
            jax.ShapeDtypeStruct((1, chan), F32),
        ),
        in_specs=[SCALARS] + [VMEM] * 3,
        out_specs=(VMEM,) * 4,
        compiler_params=pltpu.CompilerParams(vmem_limit_bytes=VMEM_LIMIT),
        cost_estimate=COST,
        name="enter",
    )(starts, x, rows_all, wr_all)


def mix_kernel(starts_n, layer, scal, hops_ref, lasts_ref, start_ref, rows_ref, pre_ref, local_ref, states_ref, in_ref, mixed_ref):
    rows, chan = pre_ref.shape
    rate = rows_ref[layer, RATE : RATE + 1, :chan]
    hops = hops_ref[...]
    weight = jnp.where(hops >= 0.0, jnp.exp(-jnp.maximum(hops, 0.0) * rate), 0.0)
    many = lasts_ref.shape[0]
    entered = jnp.sum(weight[:many] * lasts_ref[...], axis=0, keepdims=True) + weight[many:] * start_ref[...]
    in_ref[...] = entered
    row = column(rows)
    open_rows = row >= 0
    for s in range(starts_n):
        open_rows = open_rows & ~((row >= scal[s]) & (scal[s] >= 0))
    running = jnp.where(open_rows, jnp.exp(-(row + 1).astype(F32) * rate), 0.0)
    states = local_ref[...] + running * entered
    states_ref[...] = states
    scale, skip = rows_ref[layer, SCALE : SCALE + 1, :chan], rows_ref[layer, SKIP : SKIP + 1, :chan]
    mixed_ref[...] = (scale * states + skip * gelu(pre_ref[...])).astype(BF)


def mix_call(layer, starts, hops, lasts, start_state, rows_all, pre, local_states):
    rows, chan = pre.shape
    return pl.pallas_call(
        functools.partial(mix_kernel, starts.shape[0], layer),
        out_shape=(
            jax.ShapeDtypeStruct((rows, chan), F32),
            jax.ShapeDtypeStruct((1, chan), F32),
            jax.ShapeDtypeStruct((rows, chan), BF),
        ),
        in_specs=[SCALARS] + [VMEM] * 6,
        out_specs=(VMEM,) * 3,
        compiler_params=pltpu.CompilerParams(vmem_limit_bytes=VMEM_LIMIT),
        cost_estimate=COST,
        name="mix",
    )(starts, hops, lasts, start_state, rows_all, pre, local_states)


def back_scan_kernel(starts_n, layer, scal, dmix_ref, rows_ref, local_ref, first_ref):
    rows, chan = dmix_ref.shape
    rate = rows_ref[layer, RATE : RATE + 1, :chan]
    grad = rows_ref[layer, SCALE : SCALE + 1, :chan] * dmix_ref[...]
    row = column(rows)
    k = 1
    while k < rows:
        open_rows = row < rows - k
        for s in range(starts_n):
            open_rows = open_rows & ~((row < scal[s]) & (row >= scal[s] - k))
        factor = jnp.where(open_rows, jnp.exp(-float(k) * rate), 0.0)
        grad = grad + factor * pltpu.roll(grad, rows - k, 0)
        k *= 2
    local_ref[...] = grad
    keep = 1.0
    for s in range(starts_n):
        keep = jnp.where(scal[s] == 0, 0.0, keep)
    first_ref[...] = keep * jnp.exp(-rate) * grad[:1]


def back_scan_call(layer, starts, dmix, rows_all):
    rows, chan = dmix.shape
    return pl.pallas_call(
        functools.partial(back_scan_kernel, starts.shape[0], layer),
        out_shape=(jax.ShapeDtypeStruct((rows, chan), F32), jax.ShapeDtypeStruct((1, chan), F32)),
        in_specs=[SCALARS] + [VMEM] * 2,
        out_specs=(VMEM,) * 2,
        compiler_params=pltpu.CompilerParams(vmem_limit_bytes=VMEM_LIMIT),
        cost_estimate=COST,
        name="back_scan",
    )(starts, dmix, rows_all)


def leave_kernel(
    starts_n,
    layer,
    scal,
    hops_ref,
    firsts_ref,
    key_ref,
    key_col_ref,
    dmix_ref,
    local_ref,
    states_ref,
    in_ref,
    pre_ref,
    normed_ref,
    x_ref,
    rows_ref,
    wr_ref,
    dnorm_ref,
    up_ref,
    up_out_ref,
    low_ref,
    own_ref,
    other_ref,
    small,
):
    rows, chan = dmix_ref.shape
    width = x_ref.shape[1]
    rate = rows_ref[layer, RATE : RATE + 1, :chan]
    decay = jnp.exp(-rate)
    hops = hops_ref[...]
    weight = jnp.where(hops >= 0.0, jnp.exp(-jnp.maximum(hops, 0.0) * rate), 0.0)
    arriving = jnp.sum(weight * firsts_ref[...], axis=0, keepdims=True)
    dmix = dmix_ref[...]
    row = column(rows)
    later = row >= 0
    first = row < 0
    for s in range(starts_n):
        later = later & ~((row < scal[s]) & (scal[s] < rows))
        first = first | (row == scal[s])
    running = jnp.where(later, jnp.exp(-(rows - 1 - row).astype(F32) * rate), 0.0)
    grad = local_ref[...] + running * arriving
    reduced, slope = gelu_both(pre_ref[...])
    states = states_ref[...]
    before = jnp.where(row == 0, in_ref[...], pltpu.roll(states, 1, 0))
    before = jnp.where(first, 0.0, before)
    small[...] = jnp.zeros_like(small)
    small[4:5, :chan] = -decay * jnp.sum(grad * (before - reduced), axis=0, keepdims=True)
    small[5:6, :chan] = jnp.sum(dmix * states, axis=0, keepdims=True)
    small[6:7, :chan] = jnp.sum(dmix * reduced, axis=0, keepdims=True)
    d_reduced = (1.0 - decay) * grad + rows_ref[layer, SKIP : SKIP + 1, :chan] * dmix
    d_pre = (d_reduced * slope).astype(BF)
    d_normed = dnorm_ref[...] + dot_nn(d_pre, wr_ref[layer])
    x = x_ref[...].astype(F32)
    centred = x - jnp.mean(x, axis=-1, keepdims=True)
    spread = jnp.mean(centred * centred, axis=-1, keepdims=True)
    rs = lax.rsqrt(spread + 1e-05)
    xhat = centred * rs
    small[0:1, :] = jnp.sum(d_normed * xhat, axis=0, keepdims=True)
    small[2:3, :] = jnp.sum(d_normed, axis=0, keepdims=True)
    e = d_normed * rows_ref[layer, GAIN : GAIN + 1, :]
    mean_e = jnp.mean(e, axis=-1, keepdims=True)
    mean_ex = jnp.mean(e * xhat, axis=-1, keepdims=True)
    up = up_ref[...].astype(F32) + rs * (e - mean_e - xhat * mean_ex)
    up_out_ref[...] = up
    low_ref[...] = up.astype(BF)
    key = key_ref[...]
    turned = dot_nn(d_pre, one_hot(column(chan), key)).astype(BF)
    grads = dot_tn(turned, normed_ref[...]).astype(BF)
    vecs = small[...].astype(BF)
    key_col = key_col_ref[...]
    pick = column(small.shape[0])
    tail = jnp.zeros((chan, PAD), F32)
    for source, at, spot in ((vecs, 2 * key_col, (0, 2)), (vecs, 2 * key_col + 1, (1, 3))):
        wide = dot_nt(one_hot(at, lane(width)), source)
        tail += dot_nn(wide.astype(BF), one_hot(jnp.where(pick == 0, spot[0], jnp.where(pick == 2, spot[1], -1)), lane(PAD)))
    thin = dot_nt(one_hot(key_col, lane(chan)), vecs[:, :chan])
    tail += dot_nn(thin.astype(BF), one_hot(jnp.where((pick >= 4) & (pick < 7), pick, -1), lane(PAD)))
    half = chan // 2
    own_ref[:, :width] = grads[:half]
    other_ref[:, :width] = grads[half:]
    own_ref[:, width:] = tail[:half].astype(BF)
    other_ref[:, width:] = tail[half:].astype(BF)


def leave_call(layer, starts, hops, firsts, key, dmix, local_grad, kept, rows_all, wr_all, dnorm, up):
    rows, width = kept["stream"].shape
    chan = dmix.shape[1]
    head = jax.ShapeDtypeStruct((chan // 2, width + PAD), BF)
    return pl.pallas_call(
        functools.partial(leave_kernel, starts.shape[0], layer),
        out_shape=(
            jax.ShapeDtypeStruct((rows, width), F32),
            jax.ShapeDtypeStruct((rows, width), BF),
            head,
            head,
        ),
        in_specs=[SCALARS] + [VMEM] * 15,
        out_specs=(VMEM,) * 4,
        scratch_shapes=[pltpu.VMEM((16, width), F32)],
        compiler_params=pltpu.CompilerParams(vmem_limit_bytes=VMEM_LIMIT),
        cost_estimate=COST,
        name="leave",
    )(
        starts,
        hops,
        firsts,
        key.reshape(1, chan),
        key.reshape(chan, 1),
        dmix,
        local_grad,
        kept["states"],
        kept["state_in"],
        kept["pre_reduce"],
        kept["normed"],
        kept["stream"],
        rows_all,
        wr_all,
        dnorm,
        up,
    )


def spread_block(head, count, rows, block):
    at = block * count + column(count)
    slot, group, row = at // (3 * rows), (at // rows) % 3, at % rows
    span = head.shape[1] // 3
    total = None
    for g in range(3):
        source = jnp.where(group == g, slot * rows + row, -1)
        part = dot_nn(one_hot(source, lane(head.shape[0])), head[:, g * span : (g + 1) * span])
        total = part if total is None else total + part
    return total.astype(BF)


def wide_kernel(names, mode, blocks, dims, head_rows, *refs):
    r = dict(zip(names, refs), head_rows=head_rows)
    width, chan = dims
    step = pl.program_id(0)
    forward, backward = mode != "back", mode != "fore"
    pair = "other" in r
    weights = r["weights"] if pair else r["own"]

    @pl.when(step == 0)
    def _():
        if forward:
            r["acc"][...] = r["base"][...].astype(F32)
        if backward:
            r["d_normed"][...] = r["d_normed_in"][...] if "d_normed_in" in r else jnp.zeros_like(r["d_normed"])
            r["d_mixed"][...] = r["d_mixed_in"][...] if "d_mixed_in" in r else jnp.zeros_like(r["d_mixed"])

    if pair:

        @pl.when(step < blocks)
        def _():
            weights[...] = r["own"][...]

        @pl.when(step >= blocks)
        def _():
            weights[...] = r["other"][...]

    normed, mixed = r["normed"][...], r["mixed"][...]
    if forward:
        pre = dot_nt(normed, weights[:, :width])
        expanded = dot_nt(mixed, weights[:, 2 * width :])
        if mode == "fore":
            r["pre"][...] = pre
            r["expanded"][...] = expanded
    else:
        pre, expanded = r["pre"][...], r["expanded"][...]
    if backward:
        gate, slope = gelu_both(pre)
    else:
        gate = gelu(pre)
    joined = (expanded * gate).astype(BF)
    if forward:
        r["acc"][...] += dot_nn(joined, weights[:, width : 2 * width])
    if backward:
        low = r["low"][...]
        d_joined = dot_nt(low, weights[:, width : 2 * width])
        d_expanded = (d_joined * gate).astype(BF)
        d_pre = (d_joined * expanded * slope).astype(BF)
        r["d_mixed"][...] += dot_nn(d_expanded, weights[:, 2 * width :])
        r["d_normed"][...] += dot_nn(d_pre, weights[:, :width])

        def store(out):
            out[:, :width] = dot_tn(d_pre, normed).astype(BF)
            out[:, width : 2 * width] = dot_tn(joined, low).astype(BF)
            out[:, 2 * width :] = dot_tn(d_expanded, mixed).astype(BF)

        if not pair:
            store(r["grad_own"])
        else:
            grads = r["grads"]
            store(grads)
            lanes = 2 * width + chan

            def put(out, head):
                out[:, :lanes] = grads[...]
                if head in r:
                    out[:, lanes:] = spread_block(r[head], out.shape[0], r["head_rows"], step % blocks)

            @pl.when(step < blocks)
            def _():
                put(r["grad_own"], "head_own")

            @pl.when(step >= blocks)
            def _():
                put(r["grad_other"], "head_other")

    if "out" in r:

        @pl.when(step == pl.num_programs(0) - 1)
        def _():
            r["out"][...] = r["acc"][...].astype(r["out"].dtype)


def wide_call(mode, own, other, normed, mixed, base=None, low=None, pre=None, expanded=None, sums=None, heads=None, head_rows=0, out_dtype=None):
    rows, width = normed.shape
    chan = mixed.shape[1]
    span = own.shape[0]
    pair = other is not None
    block = span // 2 if pair else span // 4
    blocks = span // block
    steps = blocks * (2 if pair else 1)
    lanes = 2 * width + chan
    forward, backward = mode != "back", mode != "fore"
    ins, outs, scratch = [], [], []

    def half_spec(which, count):
        if which == "own":
            return pl.BlockSpec((block, count), lambda i: (jnp.minimum(i, blocks - 1), 0))
        return pl.BlockSpec((block, count), lambda i: (jnp.maximum(i - blocks, 0), 0))

    ins.append(("own", own, half_spec("own", lanes)))
    more = 0
    if pair:
        ins.append(("other", other, half_spec("other", lanes)))
    if heads is not None:
        more = heads[0].shape[1] // 3
        ins.append(("head_own", heads[0], full_spec(heads[0].shape)))
        ins.append(("head_other", heads[1], full_spec(heads[1].shape)))
    ins.append(("normed", normed, full_spec(normed.shape)))
    ins.append(("mixed", mixed, full_spec(mixed.shape)))
    saved = pl.BlockSpec((rows, block), lambda i: (0, i))
    saved_shape = jax.ShapeDtypeStruct((rows, steps * block), F32)
    if forward:
        ins.append(("base", base, full_spec(base.shape)))
    if backward:
        ins.append(("low", low, full_spec(low.shape)))
        if sums is not None:
            ins.append(("d_normed_in", sums[0], full_spec(sums[0].shape)))
            ins.append(("d_mixed_in", sums[1], full_spec(sums[1].shape)))
    if mode == "back":
        ins.append(("pre", pre, saved))
        ins.append(("expanded", expanded, saved))
    if mode == "fore":
        outs.append(("pre", saved_shape, saved))
        outs.append(("expanded", saved_shape, saved))
    if forward:
        if out_dtype == F32:
            outs.append(("acc", jax.ShapeDtypeStruct((rows, width), F32), full_spec((rows, width))))
        else:
            outs.append(("out", jax.ShapeDtypeStruct((rows, width), out_dtype), full_spec((rows, width))))
            scratch.append(("acc", pltpu.VMEM((rows, width), F32)))
    if backward:
        outs.append(("d_normed", jax.ShapeDtypeStruct((rows, width), F32), full_spec((rows, width))))
        outs.append(("d_mixed", jax.ShapeDtypeStruct((rows, chan), F32), full_spec((rows, chan))))
        grad = jax.ShapeDtypeStruct((span, lanes + more), BF)
        outs.append(("grad_own", grad, half_spec("own", lanes + more)))
        if pair:
            outs.append(("grad_other", grad, half_spec("other", lanes + more)))
            scratch.append(("grads", pltpu.VMEM((block, lanes), BF)))
    if pair:
        scratch.append(("weights", pltpu.VMEM((block, lanes), BF)))
    names = [name for name, _, _ in ins + outs] + [name for name, _ in scratch]
    return pl.pallas_call(
        functools.partial(wide_kernel, names, mode, blocks, (width, chan), head_rows),
        grid=(steps,),
        out_shape=tuple(shape for _, shape, _ in outs),
        in_specs=[spec for _, _, spec in ins],
        out_specs=tuple(spec for _, _, spec in outs),
        scratch_shapes=[shape for _, shape in scratch],
        compiler_params=pltpu.CompilerParams(vmem_limit_bytes=VMEM_LIMIT),
        cost_estimate=COST,
        name="wide_" + mode,
    )(*[array for _, array, _ in ins])


def seq_gather(lay, vector):
    held, k = vector, 1
    while k < lay.seq:
        pairs = [
            (d * lay.seq + s, d * lay.seq + (s ^ k)) for d in range(lay.dp) for s in range(lay.seq)
        ]
        held = cat(held, permute(held, pairs))
        k *= 2
    return held


def hops_forward(lay, starts, rows):
    me = lax.axis_index("seq")
    source = jnp.concatenate([me ^ jnp.arange(lay.seq, dtype=jnp.int32), jnp.full((1,), -1, jnp.int32)])
    hops = me - 1 - source
    low, high = (source + 1) * rows, me * rows
    hit = jnp.any((starts[None, :] >= low[:, None]) & (starts[None, :] < high), axis=1)
    return jnp.where((hops >= 0) & ~hit, (hops * rows).astype(F32), -1.0)[:, None]


def hops_backward(lay, starts, rows):
    me = lax.axis_index("seq")
    source = me ^ jnp.arange(lay.seq, dtype=jnp.int32)
    hops = source - me - 1
    low, high = (me + 1) * rows, source * rows
    hit = jnp.any((starts[None, :] >= low) & (starts[None, :] < high[:, None]), axis=1)
    return jnp.where((hops >= 0) & ~hit, (hops * rows).astype(F32), -1.0)[:, None]


def local(
    lay,
    tokens,
    ln_gain,
    ln_shift,
    w_gate,
    w_reduce,
    decay_rate,
    state_scale,
    skip_scale,
    w_expand,
    w_out,
    prev_state,
    item_lengths,
    cotangent,
):
    rows, width = tokens.shape
    chan = w_expand.shape[1]
    small_rows = w_reduce.shape[2]
    ff_rows = w_gate.shape[2]
    job_rows = ff_rows // JOBS
    me_seq = lax.axis_index("seq")
    starts = jnp.cumsum(item_lengths[0])[:-1].astype(jnp.int32)
    near = starts - me_seq * rows
    hops_fore, hops_back = hops_forward(lay, starts, rows), hops_backward(lay, starts, rows)

    def vectors(layer):
        return jnp.concatenate(
            [
                ln_gain[layer].reshape(small_rows, 2),
                ln_shift[layer].reshape(small_rows, 2),
                decay_rate[layer][:, None],
                state_scale[layer][:, None],
                skip_scale[layer][:, None],
                jnp.zeros((small_rows, PAD - SMALL), BF),
            ],
            axis=1,
        )

    heads = [jnp.concatenate([w_reduce[i].T, vectors(i)], axis=1) for i in range(LAYERS)]
    bundles = [
        jnp.concatenate([w_gate[i].T, w_out[i], w_expand[i].T], axis=1).reshape(JOBS, job_rows, -1)
        for i in range(LAYERS)
    ]
    nature = lay.natural_rows(small_rows)
    lanes = bundles[0].shape[2]
    group = jnp.arange(3, dtype=jnp.int32)[None, :, None] * chan
    key = (nature.reshape(lay.count, 1, small_rows) + group).reshape(1, -1)

    def relative_order(gathered):
        order = lay.natural_rows(1)
        half = lay.count // 2
        return [
            gathered.at[at].get(mode="promise_in_bounds", unique_indices=True).reshape(half * job_rows, -1)
            for at in (order[:half], order[half:])
        ]

    first = jnp.concatenate([bundles[0][0]] + [spread_lanes(h) for h in heads], axis=1)
    third = bundles[0][1]
    gathered_a = lax.all_gather(bundles[1][0], AXES, axis=0)
    gathered_b = lax.all_gather(after(bundles[1][1], gathered_a), AXES, axis=0, tiled=True)

    line_a = stage(first, lay.q)
    line_a, third = fence(line_a, third)
    plane_a = stage(line_a, lay.p1)
    cut = max(1, (lay.nq * 2) // 3) + 1
    early = [permute(third, lay.q[k]) for k in range(1, cut)]
    plane_a, third, *early = fence(plane_a, third, *early)
    a_own = stage(plane_a, lay.p2)
    line_b = cat(third, *early, *[permute(third, lay.q[k]) for k in range(cut, lay.nq)])
    a_own, line_b = fence(a_own, line_b)
    a_other = permute(a_own, lay.core)
    plane_b = stage(line_b, lay.p1)
    a_own, a_other, plane_b, gathered_a = fence(a_own, a_other, plane_b, gathered_a)
    b_own = stage(plane_b, lay.p2)
    wr_all, rows_all = params_call(key, a_own, a_other, lanes, width, chan)

    def enter(layer, stream):
        normed, pre_reduce, local_states, last = enter_call(layer, near, stream, rows_all, wr_all)
        lasts = seq_gather(lay, last)
        states, state_in, mixed = mix_call(
            layer, near, hops_fore, lasts, prev_state[layer], rows_all, pre_reduce, local_states
        )
        return dict(stream=stream, normed=normed, pre_reduce=pre_reduce, states=states, state_in=state_in, mixed=mixed)

    def leave(layer, kept, sums, upstream):
        d_normed, d_mixed = sums
        back_local, first_row = back_scan_call(layer, near, d_mixed, rows_all)
        firsts = seq_gather(lay, first_row)
        upstream, low, *head = leave_call(
            layer, near, hops_back, firsts, nature, d_mixed, back_local, kept, rows_all, wr_all, d_normed, upstream
        )
        return upstream, low, head

    k0 = enter(0, tokens)
    top_a = relative_order(gathered_a)
    b_own, k0["mixed"], *top_a = fence(b_own, k0["mixed"], *top_a)
    b_other = permute(b_own, lay.core)
    pre_a, exp_a, acc = wide_call("fore", a_own, a_other, k0["normed"], k0["mixed"], base=tokens, out_dtype=F32)
    b_own, b_other, acc = fence(b_own, b_other, acc)
    pre_b, exp_b, acc = wide_call("fore", b_own, b_other, k0["normed"], k0["mixed"], base=acc, out_dtype=F32)

    k1 = enter(1, acc)
    acc, d_normed, d_mixed, a1_own, a1_other = wide_call(
        "both", *top_a, k1["normed"], k1["mixed"], base=k1["stream"], low=cotangent, out_dtype=F32
    )
    acc, d_normed, d_mixed, a1_own, a1_other = fence(acc, d_normed, d_mixed, a1_own, a1_other)
    a1 = add_parts([a1_own, permute(a1_other, lay.core)], BF)
    output, d_normed, d_mixed, b1 = wide_call(
        "both",
        gathered_b,
        None,
        k1["normed"],
        k1["mixed"],
        base=acc,
        low=cotangent,
        sums=(d_normed, d_mixed),
        out_dtype=BF,
    )
    a1, d_normed, d_mixed, b1 = fence(a1, d_normed, d_mixed, b1)
    b1_done = lax.psum_scatter(b1, AXES, scatter_dimension=0, tiled=True)

    a1 = fold(a1, lay.p2)
    upstream, low, head_1 = leave(1, k1, (d_normed, d_mixed), cotangent)
    a1, low, upstream, *head_1 = fence(a1, low, upstream, *head_1)

    a1 = fold(a1, lay.p1)
    d_normed, d_mixed, a0_own, a0_other = wide_call(
        "back",
        a_own,
        a_other,
        k0["normed"],
        k0["mixed"],
        low=low,
        pre=pre_a,
        expanded=exp_a,
        heads=head_1,
        head_rows=small_rows,
    )
    a1, d_normed, d_mixed, a0_own, a0_other = fence(a1, d_normed, d_mixed, a0_own, a0_other)

    a1_done = fold(a1, lay.q, F32)
    a0 = add_parts([a0_own, permute(a0_other, lay.core)], BF)
    d_normed, d_mixed, b0_own, b0_other = wide_call(
        "back",
        b_own,
        b_other,
        k0["normed"],
        k0["mixed"],
        low=low,
        pre=pre_b,
        expanded=exp_b,
        sums=(d_normed, d_mixed),
    )
    a1_done, a0, d_normed, d_mixed, b0_own, b0_other = fence(a1_done, a0, d_normed, d_mixed, b0_own, b0_other)

    b0 = add_parts([b0_own, permute(b0_other, lay.core)], BF)
    a0 = fold(a0, lay.p2)
    _, input_grad, (head_own, head_other) = leave(0, k0, (d_normed, d_mixed), upstream)
    a0, b0, head_own, head_other = fence(a0, b0, head_own, head_other)

    a0 = fold(a0, lay.p1)
    b0 = fold(b0, lay.p2)
    h0 = fold(add_parts([head_own, permute(head_other, lay.core)], BF), lay.p2)
    a0, b0, h0, b1_done = fence(a0, b0, h0, b1_done)

    a0_done = fold(a0, lay.q, F32)
    b0 = fold(b0, lay.p1)
    h0 = fold(h0, lay.p1)
    a0_done, b0, h0 = fence(a0_done, b0, h0)
    b0_done = fold(b0, lay.q, F32)
    h0_done = fold(h0, lay.q, F32)

    h1_done = close_lanes(a0_done[:, lanes:], small_rows)
    b1_done = b1_done.astype(F32)
    grads = [cat(a0_done[:, :lanes], b0_done), cat(a1_done, b1_done)]
    heads_done = [h0_done, h1_done]
    vecs = [h[:, width : width + SMALL] for h in heads_done]
    return (
        output,
        input_grad,
        jnp.stack([v[:, 0:2].reshape(-1) for v in vecs]),
        jnp.stack([v[:, 2:4].reshape(-1) for v in vecs]),
        jnp.stack([g[:, :width].T for g in grads]),
        jnp.stack([h[:, :width].T for h in heads_done]),
        jnp.stack([v[:, 4] for v in vecs]),
        jnp.stack([v[:, 5] for v in vecs]),
        jnp.stack([v[:, 6] for v in vecs]),
        jnp.stack([g[:, 2 * width :].T for g in grads]),
        jnp.stack([g[:, width : 2 * width] for g in grads]),
    )


def solution(mesh):
    lay = Layout(mesh)
    both = ("dp", "seq")
    return jax.shard_map(
        functools.partial(local, lay),
        mesh=mesh,
        in_specs=(
            P(both, None),
            P(None, both),
            P(None, both),
            P(None, None, both),
            P(None, None, both),
            P(None, both),
            P(None, both),
            P(None, both),
            P(None, None, both),
            P(None, both, None),
            P(None, "dp", None),
            P("dp", None),
            P(both, None),
        ),
        out_specs=(
            P(both, None),
            P(both, None),
            P(None, both),
            P(None, both),
            P(None, None, both),
            P(None, None, both),
            P(None, both),
            P(None, both),
            P(None, both),
            P(None, None, both),
            P(None, both, None),
        ),
        check_vma=False,
    )
```

```python
import functools
import itertools
import math

import jax
import jax.numpy as jnp
from jax import lax
from jax.experimental import pallas as pl
from jax.experimental.pallas import tpu as pltpu
from jax.sharding import PartitionSpec as P

LAYERS = 2
JOBS = 2
AXES = ("dp", "seq")
BF = jnp.bfloat16
F32 = jnp.float32
VMEM_LIMIT = 30 << 20
C0 = math.sqrt(2.0 / math.pi)
C1 = 0.044715
SMALL = 7
PAD = 128


class Layout:
    def __init__(self, mesh):
        self.dp, self.seq = mesh.shape["dp"], mesh.shape["seq"]
        self.x, self.c = self.dp // 2, 2
        self.s1 = 4
        self.s0 = self.seq // 4
        self.count = self.dp * self.seq
        self.alt_minor = self.s0 == self.x
        self.swap = self.s0 == self.x or self.s1 == self.x
        if self.alt_minor or not self.swap:
            self.alt, self.nq = self.s0, self.s1
        else:
            self.alt, self.nq = self.s1, self.s0
        self.n1, self.n2 = self.alt, self.x
        self.q = [self.pairs(self.move_q, k) for k in range(self.nq)]
        self.p1 = [self.pairs(self.move_1, k) for k in range(self.n1)]
        self.p2 = [self.pairs(self.move_2, k) for k in range(self.n2)]
        self.core = self.pairs(lambda x, c, a, q, k: (x, c ^ 1, a, q), 0)

    def place(self, x, c, a, q):
        s1, s0 = (q, a) if (self.alt_minor or not self.swap) else (a, q)
        return ((x * 2 + c) * self.s1 + s1) * self.s0 + s0

    def pairs(self, move, k):
        spots = itertools.product(range(self.x), range(2), range(self.alt), range(self.nq))
        return [(self.place(*spot), self.place(*move(*spot, k))) for spot in spots]

    def move_q(self, x, c, a, q, k):
        return (x, c, a, q ^ k)

    def move_1(self, x, c, a, q, k):
        return (x ^ k, c, a, q) if (self.swap and c == 1) else (x, c, a ^ k, q)

    def move_2(self, x, c, a, q, k):
        return (x, c, a ^ k, q) if (self.swap and c == 1) else (x ^ k, c, a, q)

    def natural_rows(self, rows):
        me_dp, me_seq = lax.axis_index("dp"), lax.axis_index("seq")
        mx, mc = me_dp // 2, me_dp % 2
        m1, m0 = me_seq // self.s0, me_seq % self.s0
        minor = self.alt_minor or not self.swap
        ma, mq = (m0, m1) if minor else (m1, m0)
        at = jnp.arange(self.count * rows, dtype=jnp.int32)
        row, at = at % rows, at // rows
        kq, at = at % self.nq, at // self.nq
        k1, at = at % self.n1, at // self.n1
        k2, half = at % self.n2, at // self.n2
        core = mc ^ half
        turned = (core == 1) if self.swap else (core > 1)
        kx = jnp.where(turned, k1, k2)
        ka = jnp.where(turned, k2, k1)
        x, a, q = mx ^ kx, ma ^ ka, mq ^ kq
        s1, s0 = (q, a) if minor else (a, q)
        return (((x * 2 + core) * self.s1 + s1) * self.s0 + s0) * rows + row


def permute(array, pairs):
    return lax.ppermute(array, AXES, pairs)


def cat(*arrays):
    return jnp.concatenate(arrays, axis=0)


def after(array, *others):
    return lax.optimization_barrier((array,) + others)[0]


def fence(*arrays):
    return lax.optimization_barrier(arrays)


def close_lanes(block, rows):
    parts = block.reshape(-1, 3, rows, block.shape[1])
    return jnp.concatenate([parts[:, i] for i in range(3)], axis=-1).reshape(-1, 3 * block.shape[1])


def stage(array, pairs):
    return cat(array, *[permute(array, pairs[k]) for k in range(1, len(pairs))])


def add_parts(parts, dtype):
    total = parts[0].astype(F32)
    for part in parts[1:]:
        total = total + part.astype(F32)
    return total.astype(dtype)


def fold(array, pairs, dtype=None):
    count = len(pairs)
    rows = array.shape[0] // count
    parts = [array[:rows]]
    for k in range(1, count):
        parts.append(permute(array[k * rows : (k + 1) * rows], pairs[k]))
    return add_parts(parts, dtype or array.dtype)


def dot_nn(a, b):
    return jnp.dot(a, b, preferred_element_type=F32)


def dot_nt(a, b):
    return lax.dot_general(a, b, (((1,), (1,)), ((), ())), preferred_element_type=F32)


def dot_tn(a, b):
    return lax.dot_general(a, b, (((0,), (0,)), ((), ())), preferred_element_type=F32)


def gelu(v):
    return 0.5 * v * (1.0 + jnp.tanh(C0 * (v + C1 * v * v * v)))


def gelu_both(v):
    square = v * v
    t = jnp.tanh(C0 * (v + C1 * v * square))
    half = 0.5 * (1.0 + t)
    slope = half + 0.5 * v * (1.0 - t * t) * (C0 * (1.0 + 3.0 * C1 * square))
    return v * half, slope


def full_spec(shape):
    return pl.BlockSpec(memory_space=pltpu.VMEM)


COST = pl.CostEstimate(flops=1000, bytes_accessed=1000, transcendentals=0)
SCALARS = pl.BlockSpec(memory_space=pltpu.SMEM)
VMEM = pl.BlockSpec(memory_space=pltpu.VMEM)


def one_hot(left, right):
    return jnp.where(left == right, 1.0, 0.0).astype(BF)


def column(count):
    return lax.broadcasted_iota(jnp.int32, (count, 1), 0)


def lane(count):
    return lax.broadcasted_iota(jnp.int32, (1, count), 1)


GAIN, SHIFT, RATE, SCALE, SKIP = range(5)


def params_kernel(key_ref, own_ref, other_ref, wr_ref, rows_ref):
    chan, width = wr_ref.shape[1:]
    half = own_ref.shape[0]
    rows_ref[...] = jnp.zeros_like(rows_ref)
    even = one_hot(2 * column(chan), lane(width))
    odd = one_hot(2 * column(chan) + 1, lane(width))
    same = one_hot(column(chan), lane(chan))
    for layer in range(LAYERS):
        key = key_ref[...] - layer * chan
        whole = dot_nn(one_hot(key[:, :half], column(chan)), own_ref[...])
        whole += dot_nn(one_hot(key[:, half:], column(chan)), other_ref[...])
        whole = whole.astype(BF)
        wr_ref[layer] = whole[:, :width]
        vec = whole[:, width:]
        evens, odds = dot_tn(vec, even), dot_tn(vec, odd)
        turned = dot_tn(vec, same)
        rows_ref[layer, GAIN : GAIN + 1, :] = evens[0:1] + odds[1:2]
        rows_ref[layer, SHIFT : SHIFT + 1, :] = evens[2:3] + odds[3:4]
        for name, k in ((RATE, 4), (SCALE, 5), (SKIP, 6)):
            rows_ref[layer, name : name + 1, :chan] = turned[k : k + 1]


def params_call(key, own, other, width, chan):
    return pl.pallas_call(
        params_kernel,
        out_shape=(
            jax.ShapeDtypeStruct((LAYERS, chan, width), BF),
            jax.ShapeDtypeStruct((LAYERS, 8, width), F32),
        ),
        in_specs=[VMEM] * 3,
        out_specs=(VMEM,) * 2,
        compiler_params=pltpu.CompilerParams(vmem_limit_bytes=VMEM_LIMIT),
        cost_estimate=COST,
        name="params",
    )(key, own, other)


def enter_kernel(starts_n, layer, scal, x_ref, rows_ref, wr_ref, normed_ref, pre_ref, local_ref, last_ref):
    x = x_ref[...].astype(F32)
    centred = x - jnp.mean(x, axis=-1, keepdims=True)
    spread = jnp.mean(centred * centred, axis=-1, keepdims=True)
    gain, shift = rows_ref[layer, GAIN : GAIN + 1, :], rows_ref[layer, SHIFT : SHIFT + 1, :]
    normed = (centred * lax.rsqrt(spread + 1e-05) * gain + shift).astype(BF)
    normed_ref[...] = normed
    pre = dot_nt(normed, wr_ref[layer])
    pre_ref[...] = pre
    rows, chan = pre.shape
    rate = rows_ref[layer, RATE : RATE + 1, :chan]
    state = (1.0 - jnp.exp(-rate)) * gelu(pre)
    row = column(rows)
    k = 1
    while k < rows:
        open_rows = row >= k
        for s in range(starts_n):
            open_rows = open_rows & ~((row >= scal[s]) & (row < scal[s] + k))
        factor = jnp.where(open_rows, jnp.exp(-float(k) * rate), 0.0)
        state = state + factor * pltpu.roll(state, k, 0)
        k *= 2
    local_ref[...] = state
    last_ref[...] = state[rows - 1 :]


def enter_call(layer, starts, x, rows_all, wr_all):
    rows, width = x.shape
    chan = wr_all.shape[1]
    return pl.pallas_call(
        functools.partial(enter_kernel, starts.shape[0], layer),
        out_shape=(
            jax.ShapeDtypeStruct((rows, width), BF),
            jax.ShapeDtypeStruct((rows, chan), F32),
            jax.ShapeDtypeStruct((rows, chan), F32),
            jax.ShapeDtypeStruct((1, chan), F32),
        ),
        in_specs=[SCALARS] + [VMEM] * 3,
        out_specs=(VMEM,) * 4,
        compiler_params=pltpu.CompilerParams(vmem_limit_bytes=VMEM_LIMIT),
        cost_estimate=COST,
        name="enter",
    )(starts, x, rows_all, wr_all)


def mix_kernel(starts_n, layer, scal, hops_ref, lasts_ref, start_ref, rows_ref, pre_ref, local_ref, states_ref, in_ref, mixed_ref):
    rows, chan = pre_ref.shape
    rate = rows_ref[layer, RATE : RATE + 1, :chan]
    hops = hops_ref[...]
    weight = jnp.where(hops >= 0.0, jnp.exp(-jnp.maximum(hops, 0.0) * rate), 0.0)
    many = lasts_ref.shape[0]
    entered = jnp.sum(weight[:many] * lasts_ref[...], axis=0, keepdims=True) + weight[many:] * start_ref[...]
    in_ref[...] = entered
    row = column(rows)
    open_rows = row >= 0
    for s in range(starts_n):
        open_rows = open_rows & ~((row >= scal[s]) & (scal[s] >= 0))
    running = jnp.where(open_rows, jnp.exp(-(row + 1).astype(F32) * rate), 0.0)
    states = local_ref[...] + running * entered
    states_ref[...] = states
    scale, skip = rows_ref[layer, SCALE : SCALE + 1, :chan], rows_ref[layer, SKIP : SKIP + 1, :chan]
    mixed_ref[...] = (scale * states + skip * gelu(pre_ref[...])).astype(BF)


def mix_call(layer, starts, hops, lasts, start_state, rows_all, pre, local_states):
    rows, chan = pre.shape
    return pl.pallas_call(
        functools.partial(mix_kernel, starts.shape[0], layer),
        out_shape=(
            jax.ShapeDtypeStruct((rows, chan), F32),
            jax.ShapeDtypeStruct((1, chan), F32),
            jax.ShapeDtypeStruct((rows, chan), BF),
        ),
        in_specs=[SCALARS] + [VMEM] * 6,
        out_specs=(VMEM,) * 3,
        compiler_params=pltpu.CompilerParams(vmem_limit_bytes=VMEM_LIMIT),
        cost_estimate=COST,
        name="mix",
    )(starts, hops, lasts, start_state, rows_all, pre, local_states)


def back_scan_kernel(starts_n, layer, scal, dmix_ref, rows_ref, local_ref, first_ref):
    rows, chan = dmix_ref.shape
    rate = rows_ref[layer, RATE : RATE + 1, :chan]
    grad = rows_ref[layer, SCALE : SCALE + 1, :chan] * dmix_ref[...]
    row = column(rows)
    k = 1
    while k < rows:
        open_rows = row < rows - k
        for s in range(starts_n):
            open_rows = open_rows & ~((row < scal[s]) & (row >= scal[s] - k))
        factor = jnp.where(open_rows, jnp.exp(-float(k) * rate), 0.0)
        grad = grad + factor * pltpu.roll(grad, rows - k, 0)
        k *= 2
    local_ref[...] = grad
    keep = 1.0
    for s in range(starts_n):
        keep = jnp.where(scal[s] == 0, 0.0, keep)
    first_ref[...] = keep * jnp.exp(-rate) * grad[:1]


def back_scan_call(layer, starts, dmix, rows_all):
    rows, chan = dmix.shape
    return pl.pallas_call(
        functools.partial(back_scan_kernel, starts.shape[0], layer),
        out_shape=(jax.ShapeDtypeStruct((rows, chan), F32), jax.ShapeDtypeStruct((1, chan), F32)),
        in_specs=[SCALARS] + [VMEM] * 2,
        out_specs=(VMEM,) * 2,
        compiler_params=pltpu.CompilerParams(vmem_limit_bytes=VMEM_LIMIT),
        cost_estimate=COST,
        name="back_scan",
    )(starts, dmix, rows_all)


def leave_kernel(
    starts_n,
    layer,
    scal,
    hops_ref,
    firsts_ref,
    key_ref,
    key_col_ref,
    dmix_ref,
    local_ref,
    states_ref,
    in_ref,
    pre_ref,
    normed_ref,
    x_ref,
    rows_ref,
    wr_ref,
    dnorm_ref,
    up_ref,
    up_out_ref,
    low_ref,
    own_ref,
    other_ref,
    small,
):
    rows, chan = dmix_ref.shape
    width = x_ref.shape[1]
    rate = rows_ref[layer, RATE : RATE + 1, :chan]
    decay = jnp.exp(-rate)
    hops = hops_ref[...]
    weight = jnp.where(hops >= 0.0, jnp.exp(-jnp.maximum(hops, 0.0) * rate), 0.0)
    arriving = jnp.sum(weight * firsts_ref[...], axis=0, keepdims=True)
    dmix = dmix_ref[...]
    row = column(rows)
    later = row >= 0
    first = row < 0
    for s in range(starts_n):
        later = later & ~((row < scal[s]) & (scal[s] < rows))
        first = first | (row == scal[s])
    running = jnp.where(later, jnp.exp(-(rows - 1 - row).astype(F32) * rate), 0.0)
    grad = local_ref[...] + running * arriving
    reduced, slope = gelu_both(pre_ref[...])
    states = states_ref[...]
    before = jnp.where(row == 0, in_ref[...], pltpu.roll(states, 1, 0))
    before = jnp.where(first, 0.0, before)
    small[...] = jnp.zeros_like(small)
    small[4:5, :chan] = -decay * jnp.sum(grad * (before - reduced), axis=0, keepdims=True)
    small[5:6, :chan] = jnp.sum(dmix * states, axis=0, keepdims=True)
    small[6:7, :chan] = jnp.sum(dmix * reduced, axis=0, keepdims=True)
    d_reduced = (1.0 - decay) * grad + rows_ref[layer, SKIP : SKIP + 1, :chan] * dmix
    d_pre = (d_reduced * slope).astype(BF)
    d_normed = dnorm_ref[...] + dot_nn(d_pre, wr_ref[layer])
    x = x_ref[...].astype(F32)
    centred = x - jnp.mean(x, axis=-1, keepdims=True)
    spread = jnp.mean(centred * centred, axis=-1, keepdims=True)
    rs = lax.rsqrt(spread + 1e-05)
    xhat = centred * rs
    small[0:1, :] = jnp.sum(d_normed * xhat, axis=0, keepdims=True)
    small[2:3, :] = jnp.sum(d_normed, axis=0, keepdims=True)
    e = d_normed * rows_ref[layer, GAIN : GAIN + 1, :]
    mean_e = jnp.mean(e, axis=-1, keepdims=True)
    mean_ex = jnp.mean(e * xhat, axis=-1, keepdims=True)
    up = up_ref[...].astype(F32) + rs * (e - mean_e - xhat * mean_ex)
    up_out_ref[...] = up
    low_ref[...] = up.astype(BF)
    key = key_ref[...]
    turned = dot_nn(d_pre, one_hot(column(chan), key)).astype(BF)
    grads = dot_tn(turned, normed_ref[...]).astype(BF)
    vecs = small[...].astype(BF)
    key_col = key_col_ref[...]
    pick = column(small.shape[0])
    tail = jnp.zeros((chan, PAD), F32)
    for source, at, spot in ((vecs, 2 * key_col, (0, 2)), (vecs, 2 * key_col + 1, (1, 3))):
        wide = dot_nt(one_hot(at, lane(width)), source)
        tail += dot_nn(wide.astype(BF), one_hot(jnp.where(pick == 0, spot[0], jnp.where(pick == 2, spot[1], -1)), lane(PAD)))
    thin = dot_nt(one_hot(key_col, lane(chan)), vecs[:, :chan])
    tail += dot_nn(thin.astype(BF), one_hot(jnp.where((pick >= 4) & (pick < 7), pick, -1), lane(PAD)))
    half = chan // 2
    own_ref[:, :width] = grads[:half]
    other_ref[:, :width] = grads[half:]
    own_ref[:, width:] = tail[:half].astype(BF)
    other_ref[:, width:] = tail[half:].astype(BF)


def leave_call(layer, starts, hops, firsts, key, dmix, local_grad, kept, rows_all, wr_all, dnorm, up):
    rows, width = kept["stream"].shape
    chan = dmix.shape[1]
    head = jax.ShapeDtypeStruct((chan // 2, width + PAD), BF)
    return pl.pallas_call(
        functools.partial(leave_kernel, starts.shape[0], layer),
        out_shape=(
            jax.ShapeDtypeStruct((rows, width), F32),
            jax.ShapeDtypeStruct((rows, width), BF),
            head,
            head,
        ),
        in_specs=[SCALARS] + [VMEM] * 15,
        out_specs=(VMEM,) * 4,
        scratch_shapes=[pltpu.VMEM((16, width), F32)],
        compiler_params=pltpu.CompilerParams(vmem_limit_bytes=VMEM_LIMIT),
        cost_estimate=COST,
        name="leave",
    )(
        starts,
        hops,
        firsts,
        key.reshape(1, chan),
        key.reshape(chan, 1),
        dmix,
        local_grad,
        kept["states"],
        kept["state_in"],
        kept["pre_reduce"],
        kept["normed"],
        kept["stream"],
        rows_all,
        wr_all,
        dnorm,
        up,
    )


def spread_block(head, count, rows, block):
    at = block * count + column(count)
    slot, group, row = at // (3 * rows), (at // rows) % 3, at % rows
    span = head.shape[1] // 3
    total = None
    for g in range(3):
        source = jnp.where(group == g, slot * rows + row, -1)
        part = dot_nn(one_hot(source, lane(head.shape[0])), head[:, g * span : (g + 1) * span])
        total = part if total is None else total + part
    return total.astype(BF)


def wide_kernel(names, mode, blocks, dims, groups, *refs):
    r = dict(zip(names, (groups,) + refs))
    width, chan = dims
    step = pl.program_id(0)
    forward, backward = mode != "back", mode != "fore"
    pair = "other" in r
    weights = r["weights"] if pair else r["own"]

    def part(low, high):
        if len(weights.shape) == 4:
            return weights[:, 0, :, low:high].reshape(-1, high - low)
        return weights[:, low:high]

    w_gate, w_out, w_expand = [functools.partial(part, *at) for at in ((0, width), (width, 2 * width), (2 * width, 2 * width + chan))]

    @pl.when(step == 0)
    def _():
        if forward:
            r["acc"][...] = r["base"][...].astype(F32)
        if backward:
            r["d_normed"][...] = r["d_normed_in"][...] if "d_normed_in" in r else jnp.zeros_like(r["d_normed"])
            r["d_mixed"][...] = r["d_mixed_in"][...] if "d_mixed_in" in r else jnp.zeros_like(r["d_mixed"])

    if pair:

        @pl.when(step < blocks)
        def _():
            weights[...] = r["own"][...]

        @pl.when(step >= blocks)
        def _():
            weights[...] = r["other"][...]

    normed, mixed = r["normed"][...], r["mixed"][...]
    if forward:
        pre = dot_nt(normed, w_gate())
        expanded = dot_nt(mixed, w_expand())
        if mode == "fore":
            r["pre"][...] = pre
            r["expanded"][...] = expanded
    else:
        pre, expanded = r["pre"][...], r["expanded"][...]
    if backward:
        gate, slope = gelu_both(pre)
    else:
        gate = gelu(pre)
    joined = (expanded * gate).astype(BF)
    if forward:
        r["acc"][...] += dot_nn(joined, w_out())
    if backward:
        low = r["low"][...]
        d_joined = dot_nt(low, w_out())
        d_expanded = (d_joined * gate).astype(BF)
        d_pre = (d_joined * expanded * slope).astype(BF)
        r["d_mixed"][...] += dot_nn(d_expanded, w_expand())
        r["d_normed"][...] += dot_nn(d_pre, w_gate())

        def keep(out):
            out[0], out[1], out[2] = d_pre, joined, d_expanded

        @pl.when(step < blocks)
        def _():
            keep(r["acts_first"])

        @pl.when(step >= blocks)
        def _():
            keep(r["acts_last"])

    if "out" in r:

        @pl.when(step == pl.num_programs(0) - 1)
        def _():
            r["out"][...] = r["acc"][...].astype(r["out"].dtype)


def wide_call(mode, own, other, normed, mixed, base=None, low=None, saved=None, sums=None, out_dtype=F32, job=0, groups=None):
    rows, width = normed.shape
    chan = mixed.shape[1]
    pair = groups is None
    if pair:
        groups = jnp.zeros((1,), jnp.int32)
        blocks, block = 2, own.shape[0] // 2
    else:
        blocks = groups.shape[0] // 2
        block = own.shape[0] * own.shape[2] // groups.shape[0]
    lanes = 2 * width + chan
    forward, backward = mode != "back", mode != "fore"
    ins, outs, scratch = [], [], []
    early = lambda i, _: (jnp.minimum(i, blocks - 1), 0)
    late = lambda i, _: (jnp.maximum(i - blocks, 0), 0)
    if pair:
        ins.append(("own", own, pl.BlockSpec((block, lanes), early)))
        ins.append(("other", other, pl.BlockSpec((block, lanes), late)))
    else:
        deep = (block // own.shape[2], 1, own.shape[2], lanes)
        ins.append(("own", own, pl.BlockSpec(deep, lambda i, at: (at[i], job, 0, 0))))
    ins.append(("normed", normed, full_spec(normed.shape)))
    ins.append(("mixed", mixed, full_spec(mixed.shape)))
    side = pl.BlockSpec((rows, block), lambda i, _: (0, i))
    if forward:
        ins.append(("base", base, full_spec(base.shape)))
    if backward:
        ins.append(("low", low, full_spec(low.shape)))
        if sums is not None:
            ins.append(("d_normed_in", sums[0], full_spec(sums[0].shape)))
            ins.append(("d_mixed_in", sums[1], full_spec(sums[1].shape)))
    if mode == "back":
        ins.append(("pre", saved[0], side))
        ins.append(("expanded", saved[1], side))
    if mode == "fore":
        for name in ("pre", "expanded"):
            outs.append((name, jax.ShapeDtypeStruct((rows, 2 * blocks * block), F32), side))
    if forward:
        if out_dtype == F32:
            outs.append(("acc", jax.ShapeDtypeStruct((rows, width), F32), full_spec((rows, width))))
        else:
            outs.append(("out", jax.ShapeDtypeStruct((rows, width), out_dtype), full_spec((rows, width))))
            scratch.append(("acc", pltpu.VMEM((rows, width), F32)))
    if backward:
        outs.append(("d_normed", jax.ShapeDtypeStruct((rows, width), F32), full_spec((rows, width))))
        outs.append(("d_mixed", jax.ShapeDtypeStruct((rows, chan), F32), full_spec((rows, chan))))
        acts = jax.ShapeDtypeStruct((3, rows, blocks * block), BF)
        for name, at in (("acts_first", early), ("acts_last", late)):
            outs.append((name, acts, pl.BlockSpec((3, rows, block), lambda i, _, at=at: (0, 0, at(i, _)[0]))))
    if pair:
        scratch.append(("weights", pltpu.VMEM((block, lanes), BF)))
    names = ["groups"] + [name for name, _, _ in ins + outs] + [name for name, _ in scratch]
    return pl.pallas_call(
        functools.partial(wide_kernel, names, mode, blocks, (width, chan)),
        grid_spec=pltpu.PrefetchScalarGridSpec(
            num_scalar_prefetch=1,
            grid=(2 * blocks,),
            in_specs=[spec for _, _, spec in ins],
            out_specs=tuple(spec for _, _, spec in outs),
            scratch_shapes=[shape for _, shape in scratch],
        ),
        out_shape=tuple(shape for _, shape, _ in outs),
        compiler_params=pltpu.CompilerParams(vmem_limit_bytes=VMEM_LIMIT),
        cost_estimate=COST,
        name="wide_" + mode,
    )(groups, *[array for _, array, _ in ins])


def grads_kernel(names, head_rows, sub, places, *refs):
    r = dict(zip(names, refs))
    step = pl.program_id(0)
    out = r["grads"] if sub else r["out"]
    at = 0
    for k, name in enumerate(("normed", "low", "mixed")):
        span = r[name].shape[1]
        total = dot_tn(r["acts"][k], r[name][...]) + dot_tn(r["peer_acts"][k], r["peer_" + name][...])
        out[:, at : at + span] = total.astype(BF)
        at += span
    if "head" in r:
        head = (r["head"][...].astype(F32) + r["peer_head"][...].astype(F32)).astype(BF)
        out[:, at:] = spread_block(head, out.shape[0], head_rows, step)
    if sub:
        count = out.shape[0] // sub
        for j in range(count):
            to = pl.multiple_of(places[step * count + j] * sub, 16)
            r["out"][pl.ds(to, sub), :] = out[j * sub : (j + 1) * sub, :]


def grads_call(acts, peer_acts, inputs, peer_inputs, places=None, sub=0, heads=None, head_rows=0):
    rows, span = acts.shape[1:]
    steps = 2
    block = span // steps
    ins = []
    for prefix, array, sides in (("", acts, inputs), ("peer_", peer_acts, peer_inputs)):
        ins.append((prefix + "acts", array, pl.BlockSpec((3, rows, block), lambda i, _: (0, 0, i))))
        for name, side in zip(("normed", "low", "mixed"), sides):
            ins.append((prefix + name, side, full_spec(side.shape)))
    lanes = sum(side.shape[1] for side in inputs)
    if heads is not None:
        ins.append(("head", heads[0], full_spec(heads[0].shape)))
        ins.append(("peer_head", heads[1], full_spec(heads[1].shape)))
        lanes += heads[0].shape[1] // 3
    out_spec = full_spec((span, lanes)) if sub else pl.BlockSpec((block, lanes), lambda i, _: (i, 0))
    names = [name for name, _, _ in ins] + ["out"] + (["grads"] if sub else [])
    return pl.pallas_call(
        functools.partial(grads_kernel, names, head_rows, sub),
        grid_spec=pltpu.PrefetchScalarGridSpec(
            num_scalar_prefetch=1,
            grid=(steps,),
            in_specs=[spec for _, _, spec in ins],
            out_specs=out_spec,
            scratch_shapes=[pltpu.VMEM((block, lanes), BF)] if sub else [],
        ),
        out_shape=jax.ShapeDtypeStruct((span, lanes), BF),
        compiler_params=pltpu.CompilerParams(vmem_limit_bytes=VMEM_LIMIT),
        cost_estimate=COST,
        name="grads",
    )(jnp.zeros((1,), jnp.int32) if places is None else places, *[array for _, array, _ in ins])


def seq_gather(lay, vector):
    held, k = vector, 1
    while k < lay.seq:
        pairs = [
            (d * lay.seq + s, d * lay.seq + (s ^ k)) for d in range(lay.dp) for s in range(lay.seq)
        ]
        held = cat(held, permute(held, pairs))
        k *= 2
    return held


def hops_forward(lay, starts, rows):
    me = lax.axis_index("seq")
    source = jnp.concatenate([me ^ jnp.arange(lay.seq, dtype=jnp.int32), jnp.full((1,), -1, jnp.int32)])
    hops = me - 1 - source
    low, high = (source + 1) * rows, me * rows
    hit = jnp.any((starts[None, :] >= low[:, None]) & (starts[None, :] < high), axis=1)
    return jnp.where((hops >= 0) & ~hit, (hops * rows).astype(F32), -1.0)[:, None]


def hops_backward(lay, starts, rows):
    me = lax.axis_index("seq")
    source = me ^ jnp.arange(lay.seq, dtype=jnp.int32)
    hops = source - me - 1
    low, high = (me + 1) * rows, source * rows
    hit = jnp.any((starts[None, :] >= low) & (starts[None, :] < high[:, None]), axis=1)
    return jnp.where((hops >= 0) & ~hit, (hops * rows).astype(F32), -1.0)[:, None]


def local(
    lay,
    tokens,
    ln_gain,
    ln_shift,
    w_gate,
    w_reduce,
    decay_rate,
    state_scale,
    skip_scale,
    w_expand,
    w_out,
    prev_state,
    item_lengths,
    cotangent,
):
    rows, width = tokens.shape
    chan = w_expand.shape[1]
    small_rows = w_reduce.shape[2]
    ff_rows = w_gate.shape[2]
    job_rows = ff_rows // JOBS
    me_seq = lax.axis_index("seq")
    starts = jnp.cumsum(item_lengths[0])[:-1].astype(jnp.int32)
    near = starts - me_seq * rows
    hops_fore, hops_back = hops_forward(lay, starts, rows), hops_backward(lay, starts, rows)

    def vectors(layer):
        return jnp.concatenate(
            [
                ln_gain[layer].reshape(small_rows, 2),
                ln_shift[layer].reshape(small_rows, 2),
                decay_rate[layer][:, None],
                state_scale[layer][:, None],
                skip_scale[layer][:, None],
                jnp.zeros((small_rows, PAD - SMALL), BF),
            ],
            axis=1,
        )

    head = cat(*[jnp.concatenate([w_reduce[i].T, vectors(i)], axis=1) for i in range(LAYERS)])
    bundles = [jnp.concatenate([w_gate[i].T, w_out[i], w_expand[i].T], axis=1) for i in range(LAYERS)]
    shard_a, shard_b, shard_c, shard_d = [
        bundle[job * job_rows : (job + 1) * job_rows] for bundle in bundles for job in range(JOBS)
    ]
    nature = lay.natural_rows(small_rows)
    lanes = bundles[0].shape[1]
    group = jnp.arange(LAYERS, dtype=jnp.int32)[None, :, None] * chan
    key = (nature.reshape(lay.count, 1, small_rows) + group).reshape(1, -1)

    steps = [list(range(1, lay.nq))[i::3] for i in range(3)]

    def pulls(shard, *which):
        return {k: permute(shard, lay.q[k]) for i in which for k in steps[i]}

    def line_of(shard, pulled):
        return cat(shard, *[pulled[k] for k in range(1, lay.nq)])

    def swap(*arrays):
        return [permute(array, lay.core) for array in arrays]

    line_h = stage(head, lay.q)
    line_h, shard_a = fence(line_h, shard_a)
    plane_h = stage(line_h, lay.p1)
    pulled = pulls(shard_a, 0)
    plane_h, shard_a, pulled = fence(plane_h, shard_a, pulled)
    head_own = stage(plane_h, lay.p2)
    pulled |= pulls(shard_a, 1)
    head_own, shard_a, pulled = fence(head_own, shard_a, pulled)
    head_other = permute(head_own, lay.core)
    pulled |= pulls(shard_a, 2)
    head_own, head_other, line_a, shard_b = fence(head_own, head_other, line_of(shard_a, pulled), shard_b)

    plane_a = stage(line_a, lay.p1)
    pulled = pulls(shard_b, 0)
    wr_all, rows_all = params_call(key, head_own, head_other, width, chan)
    entered = enter_call(0, near, tokens, rows_all, wr_all)
    lasts = seq_gather(lay, entered[3])
    plane_a, shard_b, pulled, entered, lasts = fence(plane_a, shard_b, pulled, entered, lasts)

    def enter(layer, stream, entered, lasts):
        normed, pre_reduce, local_states, _ = entered
        states, state_in, mixed = mix_call(
            layer, near, hops_fore, lasts, prev_state[layer], rows_all, pre_reduce, local_states
        )
        return dict(stream=stream, normed=normed, pre_reduce=pre_reduce, states=states, state_in=state_in, mixed=mixed)

    def turn_back(layer, sums):
        back_local, first_row = back_scan_call(layer, near, sums[1], rows_all)
        return back_local, seq_gather(lay, first_row)

    def leave(layer, kept, sums, reached, upstream):
        upstream, low, *head = leave_call(
            layer, near, hops_back, reached[1], nature, sums[1], reached[0], kept, rows_all, wr_all, sums[0], upstream
        )
        return upstream, low, head

    def both(own, other, base, sums, out_dtype=F32):
        out, d_normed, d_mixed, mine, peers = wide_call(
            "both",
            own,
            other,
            k1["normed"],
            k1["mixed"],
            base=base,
            low=cotangent,
            sums=sums,
            out_dtype=out_dtype,
        )
        return out, [d_normed, d_mixed], mine, peers

    def back(own, other, saved, sums):
        d_normed, d_mixed, mine, peers = wide_call(
            "back", own, other, k0["normed"], k0["mixed"], low=low, saved=saved, sums=sums
        )
        return [d_normed, d_mixed], mine, peers

    k0 = enter(0, tokens, entered, lasts)
    a_own = stage(plane_a, lay.p2)
    pulled |= pulls(shard_b, 1, 2)
    a_own, line_b, k0, shard_c = fence(a_own, line_of(shard_b, pulled), k0, shard_c)
    (a_other,) = swap(a_own)
    plane_b = stage(line_b, lay.p1)
    pulled = pulls(shard_c, 0)
    a_own, a_other, plane_b, shard_c, pulled = fence(a_own, a_other, plane_b, shard_c, pulled)
    b_own = stage(plane_b, lay.p2)
    pulled |= pulls(shard_c, 1, 2)
    *save_a, acc = wide_call("fore", a_own, a_other, k0["normed"], k0["mixed"], base=tokens)
    b_own, line_c, acc, shard_d = fence(b_own, line_of(shard_c, pulled), acc, shard_d)
    (b_other,) = swap(b_own)
    plane_c = stage(line_c, lay.p1)
    pulled = pulls(shard_d, 0)
    b_own, b_other, plane_c, shard_d, pulled = fence(b_own, b_other, plane_c, shard_d, pulled)
    c_own = stage(plane_c, lay.p2)
    pulled |= pulls(shard_d, 1, 2)
    *save_b, acc = wide_call("fore", b_own, b_other, k0["normed"], k0["mixed"], base=acc)
    entered = enter_call(1, near, acc, rows_all, wr_all)
    c_own, line_d, acc, entered = fence(c_own, line_of(shard_d, pulled), acc, entered)
    (c_other,) = swap(c_own)
    plane_d = stage(line_d, lay.p1)
    k1 = enter(1, acc, entered, seq_gather(lay, entered[3]))
    c_own, c_other, plane_d, k1 = fence(c_own, c_other, plane_d, k1)

    d_own = stage(plane_d, lay.p2)
    ins_1 = (k1["normed"], cotangent, k1["mixed"])
    peer_1 = swap(*ins_1)
    acc, sums, a1_own, a1_peer = both(c_own, c_other, acc, None)
    d_own, acc, sums, a1_own, a1_peer, peer_1 = fence(d_own, acc, sums, a1_own, a1_peer, peer_1)
    (a1_peer,) = swap(a1_peer)
    (d_other,) = swap(d_own)
    a1 = grads_call(a1_own, a1_peer, ins_1, peer_1)
    d_own, d_other, a1 = fence(d_own, d_other, a1)
    a1 = fold(a1, lay.p2)
    output, sums, b1_own, b1_peer = both(d_own, d_other, acc, sums, BF)
    a1, sums, b1_own, b1_peer = fence(a1, sums, b1_own, b1_peer)

    (b1_peer,) = swap(b1_peer)
    reached = turn_back(1, sums)
    b1 = grads_call(b1_own, b1_peer, ins_1, peer_1)
    a1, b1, sums, reached = fence(a1, b1, sums, reached)
    upstream, low, head_1 = leave(1, k1, sums, reached, cotangent)

    b1 = fold(b1, lay.p2)
    a1_done = fold(fold(a1, lay.p1), lay.q, F32)
    peer_0 = swap(k0["normed"], low, k0["mixed"])
    (head_peer,) = swap(head_1[1])
    sums, a0_own, a0_peer = back(a_own, a_other, save_a, None)
    sums, a0_sent = fence(sums, a0_peer)
    (a0_peer,) = swap(a0_sent)
    sums, b0_own, b0_peer = back(b_own, b_other, save_b, sums)
    a1_done, b1, peer_0, head_peer, a0_own, a0_peer, sums, b0_own, b0_peer = fence(
        a1_done, b1, peer_0, head_peer, a0_own, a0_peer, sums, b0_own, b0_peer
    )
    ins_0 = (k0["normed"], low, k0["mixed"])
    b1 = fold(b1, lay.p1)
    (b0_peer,) = swap(b0_peer)
    a0 = grads_call(a0_own, a0_peer, ins_0, peer_0, heads=(head_1[0], head_peer), head_rows=small_rows)
    b1, a0, sums, b0_own, b0_peer = fence(b1, a0, sums, b0_own, b0_peer)

    a0 = fold(a0, lay.p2)
    b1_done = fold(b1, lay.q, F32)
    b0 = grads_call(b0_own, b0_peer, ins_0, peer_0)
    sums[1] = after(sums[1], b0)
    reached = turn_back(0, sums)
    a0, b0, b1_done, sums, reached = fence(a0, b0, b1_done, sums, reached)
    a0 = fold(a0, lay.p1)
    _, input_grad, (head_own, head_other) = leave(0, k0, sums, reached, upstream)
    a0, head_own, head_other = fence(a0, head_own, head_other)
    a0_done = fold(a0, lay.q, F32)
    b0 = fold(b0, lay.p2)
    h0 = add_parts([head_own, *swap(head_other)], BF)
    a0_done, b0, h0 = fence(a0_done, b0, h0)
    b0, h0 = fold(b0, lay.p1), fold(h0, lay.p2)
    b0, h0 = fence(b0, h0)
    b0_done = fold(b0, lay.q, F32)
    h0_done = fold(fold(h0, lay.p1), lay.q, F32)

    h1_done = close_lanes(a0_done[:, lanes:], small_rows)
    grads = [cat(a0_done[:, :lanes], b0_done), cat(a1_done, b1_done)]
    heads_done = [h0_done, h1_done]
    vecs = [h[:, width : width + SMALL] for h in heads_done]
    return (
        output,
        input_grad,
        jnp.stack([v[:, 0:2].reshape(-1) for v in vecs]),
        jnp.stack([v[:, 2:4].reshape(-1) for v in vecs]),
        jnp.stack([g[:, :width].T for g in grads]),
        jnp.stack([h[:, :width].T for h in heads_done]),
        jnp.stack([v[:, 4] for v in vecs]),
        jnp.stack([v[:, 5] for v in vecs]),
        jnp.stack([v[:, 6] for v in vecs]),
        jnp.stack([g[:, 2 * width :].T for g in grads]),
        jnp.stack([g[:, width : 2 * width] for g in grads]),
    )


def solution(mesh):
    lay = Layout(mesh)
    both = ("dp", "seq")
    return jax.shard_map(
        functools.partial(local, lay),
        mesh=mesh,
        in_specs=(
            P(both, None),
            P(None, both),
            P(None, both),
            P(None, None, both),
            P(None, None, both),
            P(None, both),
            P(None, both),
            P(None, both),
            P(None, None, both),
            P(None, both, None),
            P(None, "dp", None),
            P("dp", None),
            P(both, None),
        ),
        out_specs=(
            P(both, None),
            P(both, None),
            P(None, both),
            P(None, both),
            P(None, None, both),
            P(None, None, both),
            P(None, both),
            P(None, both),
            P(None, both),
            P(None, None, both),
            P(None, both, None),
        ),
        check_vma=False,
    )
```

```python
import functools
import itertools
import math

import jax
import jax.numpy as jnp
from jax import lax
from jax.experimental import pallas as pl
from jax.experimental.pallas import tpu as pltpu
from jax.sharding import PartitionSpec as P

LAYERS = 2
JOBS = 2
AXES = ("dp", "seq")
BF = jnp.bfloat16
F32 = jnp.float32
VMEM_LIMIT = 24 << 20
C0 = math.sqrt(2.0 / math.pi)
C1 = 0.044715
SMALL = 7
PAD = 128


class Layout:
    def __init__(self, mesh):
        self.dp, self.seq = mesh.shape["dp"], mesh.shape["seq"]
        self.x, self.c = self.dp // 2, 2
        self.s1 = 4
        self.s0 = self.seq // 4
        self.count = self.dp * self.seq
        self.alt_minor = self.s0 == self.x
        self.swap = self.s0 == self.x or self.s1 == self.x
        if self.alt_minor or not self.swap:
            self.alt, self.nq = self.s0, self.s1
        else:
            self.alt, self.nq = self.s1, self.s0
        self.n1, self.n2 = self.alt, self.x
        self.q = [self.pairs(self.move_q, k) for k in range(self.nq)]
        self.p1 = [self.pairs(self.move_1, k) for k in range(self.n1)]
        self.p2 = [self.pairs(self.move_2, k) for k in range(self.n2)]
        self.core = self.pairs(lambda x, c, a, q, k: (x, c ^ 1, a, q), 0)

    def place(self, x, c, a, q):
        s1, s0 = (q, a) if (self.alt_minor or not self.swap) else (a, q)
        return ((x * 2 + c) * self.s1 + s1) * self.s0 + s0

    def pairs(self, move, k):
        spots = itertools.product(range(self.x), range(2), range(self.alt), range(self.nq))
        return [(self.place(*spot), self.place(*move(*spot, k))) for spot in spots]

    def move_q(self, x, c, a, q, k):
        return (x, c, a, q ^ k)

    def move_1(self, x, c, a, q, k):
        return (x ^ k, c, a, q) if (self.swap and c == 1) else (x, c, a ^ k, q)

    def move_2(self, x, c, a, q, k):
        return (x, c, a ^ k, q) if (self.swap and c == 1) else (x ^ k, c, a, q)

    def natural_rows(self, rows):
        me_dp, me_seq = lax.axis_index("dp"), lax.axis_index("seq")
        mx, mc = me_dp // 2, me_dp % 2
        m1, m0 = me_seq // self.s0, me_seq % self.s0
        minor = self.alt_minor or not self.swap
        ma, mq = (m0, m1) if minor else (m1, m0)
        at = jnp.arange(self.count * rows, dtype=jnp.int32)
        row, at = at % rows, at // rows
        kq, at = at % self.nq, at // self.nq
        k1, at = at % self.n1, at // self.n1
        k2, half = at % self.n2, at // self.n2
        core = mc ^ half
        turned = (core == 1) if self.swap else (core > 1)
        kx = jnp.where(turned, k1, k2)
        ka = jnp.where(turned, k2, k1)
        x, a, q = mx ^ kx, ma ^ ka, mq ^ kq
        s1, s0 = (q, a) if minor else (a, q)
        return (((x * 2 + core) * self.s1 + s1) * self.s0 + s0) * rows + row


def permute(array, pairs):
    return lax.ppermute(array, AXES, pairs)


def cat(*arrays):
    return jnp.concatenate(arrays, axis=0)


def after(array, *others):
    return lax.optimization_barrier((array,) + others)[0]


def fence(*arrays):
    return lax.optimization_barrier(arrays)


def close_lanes(block, rows):
    parts = block.reshape(-1, 3, rows, block.shape[1])
    return jnp.concatenate([parts[:, i] for i in range(3)], axis=-1).reshape(-1, 3 * block.shape[1])


def stage(array, pairs):
    return cat(array, *[permute(array, pairs[k]) for k in range(1, len(pairs))])


def add_parts(parts, dtype):
    total = parts[0].astype(F32)
    for part in parts[1:]:
        total = total + part.astype(F32)
    return total.astype(dtype)


def fold(array, pairs, dtype=None):
    count = len(pairs)
    rows = array.shape[0] // count
    parts = [array[:rows]]
    for k in range(1, count):
        parts.append(permute(array[k * rows : (k + 1) * rows], pairs[k]))
    return add_parts(parts, dtype or array.dtype)


def dot_nn(a, b):
    return jnp.dot(a, b, preferred_element_type=F32)


def dot_nt(a, b):
    return lax.dot_general(a, b, (((1,), (1,)), ((), ())), preferred_element_type=F32)


def dot_tn(a, b):
    return lax.dot_general(a, b, (((0,), (0,)), ((), ())), preferred_element_type=F32)


def gelu(v):
    return 0.5 * v * (1.0 + jnp.tanh(C0 * (v + C1 * v * v * v)))


def gelu_both(v):
    square = v * v
    t = jnp.tanh(C0 * (v + C1 * v * square))
    half = 0.5 * (1.0 + t)
    slope = half + 0.5 * v * (1.0 - t * t) * (C0 * (1.0 + 3.0 * C1 * square))
    return v * half, slope


def full_spec(shape):
    return pl.BlockSpec(memory_space=pltpu.VMEM)


COST = pl.CostEstimate(flops=1000, bytes_accessed=1000, transcendentals=0)
SCALARS = pl.BlockSpec(memory_space=pltpu.SMEM)
VMEM = pl.BlockSpec(memory_space=pltpu.VMEM)


def one_hot(left, right):
    return jnp.where(left == right, 1.0, 0.0).astype(BF)


def column(count):
    return lax.broadcasted_iota(jnp.int32, (count, 1), 0)


def lane(count):
    return lax.broadcasted_iota(jnp.int32, (1, count), 1)


GAIN, SHIFT, RATE, SCALE, SKIP = range(5)


def params_kernel(key_ref, own_ref, other_ref, wr_ref, rows_ref):
    chan, width = wr_ref.shape[1:]
    half = own_ref.shape[0]
    rows_ref[...] = jnp.zeros_like(rows_ref)
    even = one_hot(2 * column(chan), lane(width))
    odd = one_hot(2 * column(chan) + 1, lane(width))
    same = one_hot(column(chan), lane(chan))
    for layer in range(LAYERS):
        key = key_ref[...] - layer * chan
        whole = dot_nn(one_hot(key[:, :half], column(chan)), own_ref[...])
        whole += dot_nn(one_hot(key[:, half:], column(chan)), other_ref[...])
        whole = whole.astype(BF)
        wr_ref[layer] = whole[:, :width]
        vec = whole[:, width:]
        evens, odds = dot_tn(vec, even), dot_tn(vec, odd)
        turned = dot_tn(vec, same)
        rows_ref[layer, GAIN : GAIN + 1, :] = evens[0:1] + odds[1:2]
        rows_ref[layer, SHIFT : SHIFT + 1, :] = evens[2:3] + odds[3:4]
        for name, k in ((RATE, 4), (SCALE, 5), (SKIP, 6)):
            rows_ref[layer, name : name + 1, :chan] = turned[k : k + 1]


def params_call(key, own, other, width, chan):
    return pl.pallas_call(
        params_kernel,
        out_shape=(
            jax.ShapeDtypeStruct((LAYERS, chan, width), BF),
            jax.ShapeDtypeStruct((LAYERS, 8, width), F32),
        ),
        in_specs=[VMEM] * 3,
        out_specs=(VMEM,) * 2,
        compiler_params=pltpu.CompilerParams(vmem_limit_bytes=VMEM_LIMIT),
        cost_estimate=COST,
        name="params",
    )(key, own, other)


def enter_kernel(starts_n, layer, scal, x_ref, rows_ref, wr_ref, normed_ref, pre_ref, local_ref, last_ref):
    x = x_ref[...].astype(F32)
    centred = x - jnp.mean(x, axis=-1, keepdims=True)
    spread = jnp.mean(centred * centred, axis=-1, keepdims=True)
    gain, shift = rows_ref[layer, GAIN : GAIN + 1, :], rows_ref[layer, SHIFT : SHIFT + 1, :]
    normed = (centred * lax.rsqrt(spread + 1e-05) * gain + shift).astype(BF)
    normed_ref[...] = normed
    pre = dot_nt(normed, wr_ref[layer])
    pre_ref[...] = pre
    rows, chan = pre.shape
    rate = rows_ref[layer, RATE : RATE + 1, :chan]
    state = (1.0 - jnp.exp(-rate)) * gelu(pre)
    row = column(rows)
    k = 1
    while k < rows:
        open_rows = row >= k
        for s in range(starts_n):
            open_rows = open_rows & ~((row >= scal[s]) & (row < scal[s] + k))
        factor = jnp.where(open_rows, jnp.exp(-float(k) * rate), 0.0)
        state = state + factor * pltpu.roll(state, k, 0)
        k *= 2
    local_ref[...] = state
    last_ref[...] = state[rows - 1 :]


def enter_call(layer, starts, x, rows_all, wr_all):
    rows, width = x.shape
    chan = wr_all.shape[1]
    return pl.pallas_call(
        functools.partial(enter_kernel, starts.shape[0], layer),
        out_shape=(
            jax.ShapeDtypeStruct((rows, width), BF),
            jax.ShapeDtypeStruct((rows, chan), F32),
            jax.ShapeDtypeStruct((rows, chan), F32),
            jax.ShapeDtypeStruct((1, chan), F32),
        ),
        in_specs=[SCALARS] + [VMEM] * 3,
        out_specs=(VMEM,) * 4,
        compiler_params=pltpu.CompilerParams(vmem_limit_bytes=VMEM_LIMIT),
        cost_estimate=COST,
        name="enter",
    )(starts, x, rows_all, wr_all)


def mix_kernel(starts_n, layer, scal, hops_ref, lasts_ref, start_ref, rows_ref, pre_ref, local_ref, states_ref, in_ref, mixed_ref):
    rows, chan = pre_ref.shape
    rate = rows_ref[layer, RATE : RATE + 1, :chan]
    hops = hops_ref[...]
    weight = jnp.where(hops >= 0.0, jnp.exp(-jnp.maximum(hops, 0.0) * rate), 0.0)
    many = lasts_ref.shape[0]
    entered = jnp.sum(weight[:many] * lasts_ref[...], axis=0, keepdims=True) + weight[many:] * start_ref[...]
    in_ref[...] = entered
    row = column(rows)
    open_rows = row >= 0
    for s in range(starts_n):
        open_rows = open_rows & ~((row >= scal[s]) & (scal[s] >= 0))
    running = jnp.where(open_rows, jnp.exp(-(row + 1).astype(F32) * rate), 0.0)
    states = local_ref[...] + running * entered
    states_ref[...] = states
    scale, skip = rows_ref[layer, SCALE : SCALE + 1, :chan], rows_ref[layer, SKIP : SKIP + 1, :chan]
    mixed_ref[...] = (scale * states + skip * gelu(pre_ref[...])).astype(BF)


def mix_call(layer, starts, hops, lasts, start_state, rows_all, pre, local_states):
    rows, chan = pre.shape
    return pl.pallas_call(
        functools.partial(mix_kernel, starts.shape[0], layer),
        out_shape=(
            jax.ShapeDtypeStruct((rows, chan), F32),
            jax.ShapeDtypeStruct((1, chan), F32),
            jax.ShapeDtypeStruct((rows, chan), BF),
        ),
        in_specs=[SCALARS] + [VMEM] * 6,
        out_specs=(VMEM,) * 3,
        compiler_params=pltpu.CompilerParams(vmem_limit_bytes=VMEM_LIMIT),
        cost_estimate=COST,
        name="mix",
    )(starts, hops, lasts, start_state, rows_all, pre, local_states)


def back_scan_kernel(starts_n, layer, scal, dmix_ref, rows_ref, local_ref, first_ref):
    rows, chan = dmix_ref.shape
    rate = rows_ref[layer, RATE : RATE + 1, :chan]
    grad = rows_ref[layer, SCALE : SCALE + 1, :chan] * dmix_ref[...]
    row = column(rows)
    k = 1
    while k < rows:
        open_rows = row < rows - k
        for s in range(starts_n):
            open_rows = open_rows & ~((row < scal[s]) & (row >= scal[s] - k))
        factor = jnp.where(open_rows, jnp.exp(-float(k) * rate), 0.0)
        grad = grad + factor * pltpu.roll(grad, rows - k, 0)
        k *= 2
    local_ref[...] = grad
    keep = 1.0
    for s in range(starts_n):
        keep = jnp.where(scal[s] == 0, 0.0, keep)
    first_ref[...] = keep * jnp.exp(-rate) * grad[:1]


def back_scan_call(layer, starts, dmix, rows_all):
    rows, chan = dmix.shape
    return pl.pallas_call(
        functools.partial(back_scan_kernel, starts.shape[0], layer),
        out_shape=(jax.ShapeDtypeStruct((rows, chan), F32), jax.ShapeDtypeStruct((1, chan), F32)),
        in_specs=[SCALARS] + [VMEM] * 2,
        out_specs=(VMEM,) * 2,
        compiler_params=pltpu.CompilerParams(vmem_limit_bytes=VMEM_LIMIT),
        cost_estimate=COST,
        name="back_scan",
    )(starts, dmix, rows_all)


def leave_kernel(
    starts_n,
    layer,
    scal,
    hops_ref,
    firsts_ref,
    key_ref,
    key_col_ref,
    dmix_ref,
    local_ref,
    states_ref,
    in_ref,
    pre_ref,
    normed_ref,
    x_ref,
    rows_ref,
    wr_ref,
    dnorm_ref,
    up_ref,
    up_out_ref,
    low_ref,
    own_ref,
    other_ref,
    small,
):
    rows, chan = dmix_ref.shape
    width = x_ref.shape[1]
    rate = rows_ref[layer, RATE : RATE + 1, :chan]
    decay = jnp.exp(-rate)
    hops = hops_ref[...]
    weight = jnp.where(hops >= 0.0, jnp.exp(-jnp.maximum(hops, 0.0) * rate), 0.0)
    arriving = jnp.sum(weight * firsts_ref[...], axis=0, keepdims=True)
    dmix = dmix_ref[...]
    row = column(rows)
    later = row >= 0
    first = row < 0
    for s in range(starts_n):
        later = later & ~((row < scal[s]) & (scal[s] < rows))
        first = first | (row == scal[s])
    running = jnp.where(later, jnp.exp(-(rows - 1 - row).astype(F32) * rate), 0.0)
    grad = local_ref[...] + running * arriving
    reduced, slope = gelu_both(pre_ref[...])
    states = states_ref[...]
    before = jnp.where(row == 0, in_ref[...], pltpu.roll(states, 1, 0))
    before = jnp.where(first, 0.0, before)
    small[...] = jnp.zeros_like(small)
    small[4:5, :chan] = -decay * jnp.sum(grad * (before - reduced), axis=0, keepdims=True)
    small[5:6, :chan] = jnp.sum(dmix * states, axis=0, keepdims=True)
    small[6:7, :chan] = jnp.sum(dmix * reduced, axis=0, keepdims=True)
    d_reduced = (1.0 - decay) * grad + rows_ref[layer, SKIP : SKIP + 1, :chan] * dmix
    d_pre = (d_reduced * slope).astype(BF)
    d_normed = dnorm_ref[...] + dot_nn(d_pre, wr_ref[layer])
    x = x_ref[...].astype(F32)
    centred = x - jnp.mean(x, axis=-1, keepdims=True)
    spread = jnp.mean(centred * centred, axis=-1, keepdims=True)
    rs = lax.rsqrt(spread + 1e-05)
    xhat = centred * rs
    small[0:1, :] = jnp.sum(d_normed * xhat, axis=0, keepdims=True)
    small[2:3, :] = jnp.sum(d_normed, axis=0, keepdims=True)
    e = d_normed * rows_ref[layer, GAIN : GAIN + 1, :]
    mean_e = jnp.mean(e, axis=-1, keepdims=True)
    mean_ex = jnp.mean(e * xhat, axis=-1, keepdims=True)
    up = up_ref[...].astype(F32) + rs * (e - mean_e - xhat * mean_ex)
    up_out_ref[...] = up
    low_ref[...] = up.astype(BF)
    key = key_ref[...]
    turned = dot_nn(d_pre, one_hot(column(chan), key)).astype(BF)
    grads = dot_tn(turned, normed_ref[...]).astype(BF)
    vecs = small[...].astype(BF)
    key_col = key_col_ref[...]
    pick = column(small.shape[0])
    tail = jnp.zeros((chan, PAD), F32)
    for source, at, spot in ((vecs, 2 * key_col, (0, 2)), (vecs, 2 * key_col + 1, (1, 3))):
        wide = dot_nt(one_hot(at, lane(width)), source)
        tail += dot_nn(wide.astype(BF), one_hot(jnp.where(pick == 0, spot[0], jnp.where(pick == 2, spot[1], -1)), lane(PAD)))
    thin = dot_nt(one_hot(key_col, lane(chan)), vecs[:, :chan])
    tail += dot_nn(thin.astype(BF), one_hot(jnp.where((pick >= 4) & (pick < 7), pick, -1), lane(PAD)))
    half = chan // 2
    own_ref[:, :width] = grads[:half]
    other_ref[:, :width] = grads[half:]
    own_ref[:, width:] = tail[:half].astype(BF)
    other_ref[:, width:] = tail[half:].astype(BF)


def leave_call(layer, starts, hops, firsts, key, dmix, local_grad, kept, rows_all, wr_all, dnorm, up):
    rows, width = kept["stream"].shape
    chan = dmix.shape[1]
    head = jax.ShapeDtypeStruct((chan // 2, width + PAD), BF)
    return pl.pallas_call(
        functools.partial(leave_kernel, starts.shape[0], layer),
        out_shape=(
            jax.ShapeDtypeStruct((rows, width), F32),
            jax.ShapeDtypeStruct((rows, width), BF),
            head,
            head,
        ),
        in_specs=[SCALARS] + [VMEM] * 15,
        out_specs=(VMEM,) * 4,
        scratch_shapes=[pltpu.VMEM((16, width), F32)],
        compiler_params=pltpu.CompilerParams(vmem_limit_bytes=VMEM_LIMIT),
        cost_estimate=COST,
        name="leave",
    )(
        starts,
        hops,
        firsts,
        key.reshape(1, chan),
        key.reshape(chan, 1),
        dmix,
        local_grad,
        kept["states"],
        kept["state_in"],
        kept["pre_reduce"],
        kept["normed"],
        kept["stream"],
        rows_all,
        wr_all,
        dnorm,
        up,
    )


def spread_block(head, count, rows, block):
    at = block * count + column(count)
    slot, group, row = at // (3 * rows), (at // rows) % 3, at % rows
    span = head.shape[1] // 3
    total = None
    for g in range(3):
        source = jnp.where(group == g, slot * rows + row, -1)
        part = dot_nn(one_hot(source, lane(head.shape[0])), head[:, g * span : (g + 1) * span])
        total = part if total is None else total + part
    return total.astype(BF)


def wide_kernel(names, mode, blocks, dims, groups, *refs):
    r = dict(zip(names, (groups,) + refs))
    width, chan = dims
    step = pl.program_id(0)
    forward, backward = mode != "back", mode != "fore"
    pair = "other" in r
    weights = r["weights"] if pair else r["own"]

    def part(low, high):
        if len(weights.shape) == 4:
            return weights[:, 0, :, low:high].reshape(-1, high - low)
        return weights[:, low:high]

    w_gate, w_out, w_expand = [functools.partial(part, *at) for at in ((0, width), (width, 2 * width), (2 * width, 2 * width + chan))]

    @pl.when(step == 0)
    def _():
        if forward:
            r["acc"][...] = r["base"][...].astype(F32)
        if backward:
            r["d_normed"][...] = r["d_normed_in"][...] if "d_normed_in" in r else jnp.zeros_like(r["d_normed"])
            r["d_mixed"][...] = r["d_mixed_in"][...] if "d_mixed_in" in r else jnp.zeros_like(r["d_mixed"])

    if pair:

        @pl.when(step < blocks)
        def _():
            weights[...] = r["own"][...]

        @pl.when(step >= blocks)
        def _():
            weights[...] = r["other"][...]

    normed, mixed = r["normed"][...], r["mixed"][...]
    if forward:
        pre = dot_nt(normed, w_gate())
        expanded = dot_nt(mixed, w_expand())
        if mode == "fore":
            r["pre"][...] = pre
            r["expanded"][...] = expanded
    else:
        pre, expanded = r["pre"][...], r["expanded"][...]
    if backward:
        gate, slope = gelu_both(pre)
    else:
        gate = gelu(pre)
    joined = (expanded * gate).astype(BF)
    if forward:
        r["acc"][...] += dot_nn(joined, w_out())
    if backward:
        low = r["low"][...]
        d_joined = dot_nt(low, w_out())
        d_expanded = (d_joined * gate).astype(BF)
        d_pre = (d_joined * expanded * slope).astype(BF)
        r["d_mixed"][...] += dot_nn(d_expanded, w_expand())
        r["d_normed"][...] += dot_nn(d_pre, w_gate())

        def keep(out):
            out[0], out[1], out[2] = d_pre, joined, d_expanded

        @pl.when(step < blocks)
        def _():
            keep(r["acts_first"])

        @pl.when(step >= blocks)
        def _():
            keep(r["acts_last"])

    if "out" in r:

        @pl.when(step == pl.num_programs(0) - 1)
        def _():
            r["out"][...] = r["acc"][...].astype(r["out"].dtype)


def wide_call(mode, own, other, normed, mixed, base=None, low=None, saved=None, sums=None, out_dtype=F32, job=0, groups=None):
    rows, width = normed.shape
    chan = mixed.shape[1]
    pair = groups is None
    if pair:
        groups = jnp.zeros((1,), jnp.int32)
        blocks, block = 2, own.shape[0] // 2
    else:
        blocks = groups.shape[0] // 2
        block = own.shape[0] * own.shape[2] // groups.shape[0]
    lanes = 2 * width + chan
    forward, backward = mode != "back", mode != "fore"
    ins, outs, scratch = [], [], []
    early = lambda i, _: (jnp.minimum(i, blocks - 1), 0)
    late = lambda i, _: (jnp.maximum(i - blocks, 0), 0)
    if pair:
        ins.append(("own", own, pl.BlockSpec((block, lanes), early)))
        ins.append(("other", other, pl.BlockSpec((block, lanes), late)))
    else:
        deep = (block // own.shape[2], 1, own.shape[2], lanes)
        ins.append(("own", own, pl.BlockSpec(deep, lambda i, at: (at[i], job, 0, 0))))
    ins.append(("normed", normed, full_spec(normed.shape)))
    ins.append(("mixed", mixed, full_spec(mixed.shape)))
    side = pl.BlockSpec((rows, block), lambda i, _: (0, i))
    if forward:
        ins.append(("base", base, full_spec(base.shape)))
    if backward:
        ins.append(("low", low, full_spec(low.shape)))
        if sums is not None:
            ins.append(("d_normed_in", sums[0], full_spec(sums[0].shape)))
            ins.append(("d_mixed_in", sums[1], full_spec(sums[1].shape)))
    if mode == "back":
        ins.append(("pre", saved[0], side))
        ins.append(("expanded", saved[1], side))
    if mode == "fore":
        for name in ("pre", "expanded"):
            outs.append((name, jax.ShapeDtypeStruct((rows, 2 * blocks * block), F32), side))
    if forward:
        if out_dtype == F32:
            outs.append(("acc", jax.ShapeDtypeStruct((rows, width), F32), full_spec((rows, width))))
        else:
            outs.append(("out", jax.ShapeDtypeStruct((rows, width), out_dtype), full_spec((rows, width))))
            scratch.append(("acc", pltpu.VMEM((rows, width), F32)))
    if backward:
        outs.append(("d_normed", jax.ShapeDtypeStruct((rows, width), F32), full_spec((rows, width))))
        outs.append(("d_mixed", jax.ShapeDtypeStruct((rows, chan), F32), full_spec((rows, chan))))
        acts = jax.ShapeDtypeStruct((3, rows, blocks * block), BF)
        for name, at in (("acts_first", early), ("acts_last", late)):
            outs.append((name, acts, pl.BlockSpec((3, rows, block), lambda i, _, at=at: (0, 0, at(i, _)[0]))))
    if pair:
        scratch.append(("weights", pltpu.VMEM((block, lanes), BF)))
    names = ["groups"] + [name for name, _, _ in ins + outs] + [name for name, _ in scratch]
    return pl.pallas_call(
        functools.partial(wide_kernel, names, mode, blocks, (width, chan)),
        grid_spec=pltpu.PrefetchScalarGridSpec(
            num_scalar_prefetch=1,
            grid=(2 * blocks,),
            in_specs=[spec for _, _, spec in ins],
            out_specs=tuple(spec for _, _, spec in outs),
            scratch_shapes=[shape for _, shape in scratch],
        ),
        out_shape=tuple(shape for _, shape, _ in outs),
        compiler_params=pltpu.CompilerParams(vmem_limit_bytes=VMEM_LIMIT),
        cost_estimate=COST,
        name="wide_" + mode,
    )(groups, *[array for _, array, _ in ins])


def grads_kernel(names, head_rows, sub, places, *refs):
    r = dict(zip(names, refs))
    step = pl.program_id(0)
    out = r["grads"] if sub else r["out"]
    at = 0
    for k, name in enumerate(("normed", "low", "mixed")):
        span = r[name].shape[1]
        total = dot_tn(r["acts"][k], r[name][...]) + dot_tn(r["peer_acts"][k], r["peer_" + name][...])
        out[:, at : at + span] = total.astype(BF)
        at += span
    if "head" in r:
        head = (r["head"][...].astype(F32) + r["peer_head"][...].astype(F32)).astype(BF)
        out[:, at:] = spread_block(head, out.shape[0], head_rows, step)
    if sub:
        count = out.shape[0] // sub
        for j in range(count):
            to = pl.multiple_of(places[step * count + j] * sub, 16)
            r["out"][pl.ds(to, sub), :] = out[j * sub : (j + 1) * sub, :]


def grads_call(acts, peer_acts, inputs, peer_inputs, places=None, sub=0, heads=None, head_rows=0):
    rows, span = acts.shape[1:]
    steps = 2
    block = span // steps
    ins = []
    for prefix, array, sides in (("", acts, inputs), ("peer_", peer_acts, peer_inputs)):
        ins.append((prefix + "acts", array, pl.BlockSpec((3, rows, block), lambda i, _: (0, 0, i))))
        for name, side in zip(("normed", "low", "mixed"), sides):
            ins.append((prefix + name, side, full_spec(side.shape)))
    lanes = sum(side.shape[1] for side in inputs)
    if heads is not None:
        ins.append(("head", heads[0], full_spec(heads[0].shape)))
        ins.append(("peer_head", heads[1], full_spec(heads[1].shape)))
        lanes += heads[0].shape[1] // 3
    out_spec = full_spec((span, lanes)) if sub else pl.BlockSpec((block, lanes), lambda i, _: (i, 0))
    names = [name for name, _, _ in ins] + ["out"] + (["grads"] if sub else [])
    return pl.pallas_call(
        functools.partial(grads_kernel, names, head_rows, sub),
        grid_spec=pltpu.PrefetchScalarGridSpec(
            num_scalar_prefetch=1,
            grid=(steps,),
            in_specs=[spec for _, _, spec in ins],
            out_specs=out_spec,
            scratch_shapes=[pltpu.VMEM((block, lanes), BF)] if sub else [],
        ),
        out_shape=jax.ShapeDtypeStruct((span, lanes), BF),
        compiler_params=pltpu.CompilerParams(vmem_limit_bytes=VMEM_LIMIT),
        cost_estimate=COST,
        name="grads",
    )(jnp.zeros((1,), jnp.int32) if places is None else places, *[array for _, array, _ in ins])


def seq_step(lay, held, k):
    pairs = [(d * lay.seq + s, d * lay.seq + (s ^ k)) for d in range(lay.dp) for s in range(lay.seq)]
    return cat(held, permute(held, pairs))


def seq_rest(lay, held):
    k = 2
    while k < lay.seq:
        held = seq_step(lay, held, k)
        k *= 2
    return held


def hops_forward(lay, starts, rows):
    me = lax.axis_index("seq")
    source = jnp.concatenate([me ^ jnp.arange(lay.seq, dtype=jnp.int32), jnp.full((1,), -1, jnp.int32)])
    hops = me - 1 - source
    low, high = (source + 1) * rows, me * rows
    hit = jnp.any((starts[None, :] >= low[:, None]) & (starts[None, :] < high), axis=1)
    return jnp.where((hops >= 0) & ~hit, (hops * rows).astype(F32), -1.0)[:, None]


def hops_backward(lay, starts, rows):
    me = lax.axis_index("seq")
    source = me ^ jnp.arange(lay.seq, dtype=jnp.int32)
    hops = source - me - 1
    low, high = (me + 1) * rows, source * rows
    hit = jnp.any((starts[None, :] >= low) & (starts[None, :] < high[:, None]), axis=1)
    return jnp.where((hops >= 0) & ~hit, (hops * rows).astype(F32), -1.0)[:, None]


def local(
    lay,
    tokens,
    ln_gain,
    ln_shift,
    w_gate,
    w_reduce,
    decay_rate,
    state_scale,
    skip_scale,
    w_expand,
    w_out,
    prev_state,
    item_lengths,
    cotangent,
):
    rows, width = tokens.shape
    chan = w_expand.shape[1]
    small_rows = w_reduce.shape[2]
    ff_rows = w_gate.shape[2]
    job_rows = ff_rows // JOBS
    me_seq = lax.axis_index("seq")
    starts = jnp.cumsum(item_lengths[0])[:-1].astype(jnp.int32)
    near = starts - me_seq * rows
    hops_fore, hops_back = hops_forward(lay, starts, rows), hops_backward(lay, starts, rows)

    def vectors(layer):
        return jnp.concatenate(
            [
                ln_gain[layer].reshape(small_rows, 2),
                ln_shift[layer].reshape(small_rows, 2),
                decay_rate[layer][:, None],
                state_scale[layer][:, None],
                skip_scale[layer][:, None],
                jnp.zeros((small_rows, PAD - SMALL), BF),
            ],
            axis=1,
        )

    head = cat(*[jnp.concatenate([w_reduce[i].T, vectors(i)], axis=1) for i in range(LAYERS)])
    bundles = [jnp.concatenate([w_gate[i].T, w_out[i], w_expand[i].T], axis=1) for i in range(LAYERS)]
    shard_a, shard_b, shard_c, shard_d = [
        bundle[job * job_rows : (job + 1) * job_rows] for bundle in bundles for job in range(JOBS)
    ]
    nature = lay.natural_rows(small_rows)
    lanes = bundles[0].shape[1]
    group = jnp.arange(LAYERS, dtype=jnp.int32)[None, :, None] * chan
    key = (nature.reshape(lay.count, 1, small_rows) + group).reshape(1, -1)

    steps = [list(range(1, lay.nq))[i::3] for i in range(3)]

    def pulls(shard, *which):
        return {k: permute(shard, lay.q[k]) for i in which for k in steps[i]}

    def line_of(shard, pulled):
        return cat(shard, *[pulled[k] for k in range(1, lay.nq)])

    def swap(*arrays):
        return [permute(array, lay.core) for array in arrays]

    line_h = stage(head, lay.q)
    line_h, shard_a = fence(line_h, shard_a)
    plane_h = stage(line_h, lay.p1)
    pulled = pulls(shard_a, 0)
    plane_h, shard_a, pulled = fence(plane_h, shard_a, pulled)
    head_own = stage(plane_h, lay.p2)
    pulled |= pulls(shard_a, 1)
    head_own, shard_a, pulled = fence(head_own, shard_a, pulled)
    head_other = permute(head_own, lay.core)
    pulled |= pulls(shard_a, 2)
    head_own, head_other, line_a, shard_b = fence(head_own, head_other, line_of(shard_a, pulled), shard_b)

    plane_a = stage(line_a, lay.p1)
    pulled = pulls(shard_b, 0)
    wr_all, rows_all = params_call(key, head_own, head_other, width, chan)
    entered = enter_call(0, near, tokens, rows_all, wr_all)
    held = seq_step(lay, entered[3], 1)
    plane_a, shard_b, pulled, entered, held = fence(plane_a, shard_b, pulled, entered, held)

    def enter(layer, stream, entered, lasts):
        normed, pre_reduce, local_states, _ = entered
        states, state_in, mixed = mix_call(
            layer, near, hops_fore, lasts, prev_state[layer], rows_all, pre_reduce, local_states
        )
        return dict(stream=stream, normed=normed, pre_reduce=pre_reduce, states=states, state_in=state_in, mixed=mixed)

    def leave(layer, kept, sums, reached, upstream):
        upstream, low, *head = leave_call(
            layer, near, hops_back, reached[1], nature, sums[1], reached[0], kept, rows_all, wr_all, sums[0], upstream
        )
        return upstream, low, head

    def both(own, other, base, sums, out_dtype=F32):
        out, d_normed, d_mixed, mine, peers = wide_call(
            "both",
            own,
            other,
            k1["normed"],
            k1["mixed"],
            base=base,
            low=cotangent,
            sums=sums,
            out_dtype=out_dtype,
        )
        return out, [d_normed, d_mixed], mine, peers

    def back(own, other, saved, sums):
        d_normed, d_mixed, mine, peers = wide_call(
            "back", own, other, k0["normed"], k0["mixed"], low=low, saved=saved, sums=sums
        )
        return [d_normed, d_mixed], mine, peers

    k0 = enter(0, tokens, entered, seq_rest(lay, held))
    a_own = stage(plane_a, lay.p2)
    pulled |= pulls(shard_b, 1, 2)
    a_own, line_b, k0, shard_c = fence(a_own, line_of(shard_b, pulled), k0, shard_c)
    (a_other,) = swap(a_own)
    plane_b = stage(line_b, lay.p1)
    pulled = pulls(shard_c, 0)
    a_own, a_other, plane_b, shard_c, pulled = fence(a_own, a_other, plane_b, shard_c, pulled)
    b_own = stage(plane_b, lay.p2)
    pulled |= pulls(shard_c, 1, 2)
    *save_a, acc = wide_call("fore", a_own, a_other, k0["normed"], k0["mixed"], base=tokens)
    b_own, line_c, acc, shard_d = fence(b_own, line_of(shard_c, pulled), acc, shard_d)
    (b_other,) = swap(b_own)
    plane_c = stage(line_c, lay.p1)
    pulled = pulls(shard_d, 0)
    b_own, b_other, plane_c, shard_d, pulled = fence(b_own, b_other, plane_c, shard_d, pulled)
    c_own = stage(plane_c, lay.p2)
    pulled |= pulls(shard_d, 1, 2)
    *save_b, acc = wide_call("fore", b_own, b_other, k0["normed"], k0["mixed"], base=acc)
    entered = enter_call(1, near, acc, rows_all, wr_all)
    c_own, line_d, acc, entered = fence(c_own, line_of(shard_d, pulled), acc, entered)
    (c_other,) = swap(c_own)
    held = seq_step(lay, entered[3], 1)
    plane_d = stage(after(line_d, held), lay.p1)
    k1 = enter(1, acc, entered, seq_rest(lay, held))
    c_own, c_other, plane_d, k1 = fence(c_own, c_other, plane_d, k1)

    d_own = stage(plane_d, lay.p2)
    ins_1 = (k1["normed"], cotangent, k1["mixed"])
    peer_1 = swap(*ins_1)
    acc, sums, a1_own, a1_peer = both(c_own, c_other, acc, None)
    d_own, acc, sums, a1_own, a1_peer, peer_1 = fence(d_own, acc, sums, a1_own, a1_peer, peer_1)
    (a1_peer,) = swap(a1_peer)
    (d_other,) = swap(d_own)
    a1 = grads_call(a1_own, a1_peer, ins_1, peer_1)
    d_own, d_other, a1 = fence(d_own, d_other, a1)
    a1 = fold(a1, lay.p2)
    output, sums, b1_own, b1_peer = both(d_own, d_other, acc, sums, BF)
    a1, sums, b1_own, b1_peer = fence(a1, sums, b1_own, b1_peer)

    (b1_peer,) = swap(b1_peer)
    back_local, first_row = back_scan_call(1, near, sums[1], rows_all)
    held = seq_step(lay, first_row, 1)
    a1 = fold(after(a1, held), lay.p1)
    b1 = grads_call(b1_own, b1_peer, ins_1, peer_1)
    reached = back_local, seq_rest(lay, after(held, b1))
    upstream, low, head_1 = leave(1, k1, sums, reached, cotangent)
    a1, b1, upstream, low, head_1 = fence(a1, b1, upstream, low, head_1)

    b1 = fold(b1, lay.p2)
    a1_done = fold(a1, lay.q, F32)
    peer_0 = swap(k0["normed"], low, k0["mixed"])
    (head_peer,) = swap(head_1[1])
    sums, a0_own, a0_peer = back(a_own, a_other, save_a, None)
    sums, a0_sent = fence(sums, a0_peer)
    (a0_peer,) = swap(a0_sent)
    sums, b0_own, b0_peer = back(b_own, b_other, save_b, sums)
    a1_done, b1, peer_0, head_peer, a0_own, a0_peer, sums, b0_own, b0_peer = fence(
        a1_done, b1, peer_0, head_peer, a0_own, a0_peer, sums, b0_own, b0_peer
    )
    ins_0 = (k0["normed"], low, k0["mixed"])
    b1 = fold(b1, lay.p1)
    (b0_peer,) = swap(b0_peer)
    a0 = grads_call(a0_own, a0_peer, ins_0, peer_0, heads=(head_1[0], head_peer), head_rows=small_rows)
    back_local, first_row = back_scan_call(0, near, sums[1], rows_all)
    b1, a0, sums, b0_own, b0_peer, back_local, first_row = fence(
        b1, a0, sums, b0_own, b0_peer, back_local, first_row
    )

    held = seq_step(lay, first_row, 1)
    a0 = fold(after(a0, held), lay.p2)
    b0 = grads_call(b0_own, b0_peer, ins_0, peer_0)
    _, input_grad, (head_own, head_other) = leave(0, k0, sums, (back_local, seq_rest(lay, held)), upstream)
    a0, b0, b1, head_own, head_other = fence(a0, b0, b1, head_own, head_other)

    a0 = fold(a0, lay.p1)
    size = b1.shape[0] // lay.nq
    cut = (2 * lay.nq + 2) // 3
    b1_parts = [b1[k * size : (k + 1) * size] for k in range(lay.nq)]
    b1_parts[1:cut] = [permute(b1_parts[k], lay.q[k]) for k in range(1, cut)]
    h0 = add_parts([head_own, *swap(head_other)], BF)
    a0, b0, b1_parts, h0 = fence(a0, b0, b1_parts, h0)

    a0_done = fold(a0, lay.q, F32)
    b0, h0 = fold(b0, lay.p2), fold(h0, lay.p2)
    a0_done, b0, b1_parts, h0 = fence(a0_done, b0, b1_parts, h0)

    b1_parts[cut:] = [permute(b1_parts[k], lay.q[k]) for k in range(cut, lay.nq)]
    b1_done = add_parts(b1_parts, F32)
    b0, h0 = fold(b0, lay.p1), fold(h0, lay.p1)
    b1_done, b0, h0 = fence(b1_done, b0, h0)
    b0_done, h0_done = fold(b0, lay.q, F32), fold(h0, lay.q, F32)

    h1_done = close_lanes(a0_done[:, lanes:], small_rows)
    grads = [cat(a0_done[:, :lanes], b0_done), cat(a1_done, b1_done)]
    heads_done = [h0_done, h1_done]
    vecs = [h[:, width : width + SMALL] for h in heads_done]
    return (
        output,
        input_grad,
        jnp.stack([v[:, 0:2].reshape(-1) for v in vecs]),
        jnp.stack([v[:, 2:4].reshape(-1) for v in vecs]),
        jnp.stack([g[:, :width].T for g in grads]),
        jnp.stack([h[:, :width].T for h in heads_done]),
        jnp.stack([v[:, 4] for v in vecs]),
        jnp.stack([v[:, 5] for v in vecs]),
        jnp.stack([v[:, 6] for v in vecs]),
        jnp.stack([g[:, 2 * width :].T for g in grads]),
        jnp.stack([g[:, width : 2 * width] for g in grads]),
    )


def solution(mesh):
    lay = Layout(mesh)
    both = ("dp", "seq")
    return jax.shard_map(
        functools.partial(local, lay),
        mesh=mesh,
        in_specs=(
            P(both, None),
            P(None, both),
            P(None, both),
            P(None, None, both),
            P(None, None, both),
            P(None, both),
            P(None, both),
            P(None, both),
            P(None, None, both),
            P(None, both, None),
            P(None, "dp", None),
            P("dp", None),
            P(both, None),
        ),
        out_specs=(
            P(both, None),
            P(both, None),
            P(None, both),
            P(None, both),
            P(None, None, both),
            P(None, None, both),
            P(None, both),
            P(None, both),
            P(None, both),
            P(None, None, both),
            P(None, both, None),
        ),
        check_vma=False,
    )
```

```python
import functools
import itertools
import math

import jax
import jax.numpy as jnp
from jax import lax
from jax.experimental import pallas as pl
from jax.experimental.pallas import tpu as pltpu
from jax.sharding import PartitionSpec as P

LAYERS = 2
JOBS = 2
AXES = ("dp", "seq")
BF = jnp.bfloat16
F32 = jnp.float32
VMEM_LIMIT = 24 << 20
C0 = math.sqrt(2.0 / math.pi)
C1 = 0.044715
SMALL = 7
PAD = 128


class Layout:
    def __init__(self, mesh):
        self.dp, self.seq = mesh.shape["dp"], mesh.shape["seq"]
        self.x, self.c = self.dp // 2, 2
        self.s1 = 4
        self.s0 = self.seq // 4
        self.count = self.dp * self.seq
        self.alt_minor = self.s0 == self.x
        self.swap = self.s0 == self.x or self.s1 == self.x
        if self.alt_minor or not self.swap:
            self.alt, self.nq = self.s0, self.s1
        else:
            self.alt, self.nq = self.s1, self.s0
        self.n1, self.n2 = self.alt, self.x
        self.q = [self.pairs(self.move_q, k) for k in range(self.nq)]
        self.p1 = [self.pairs(self.move_1, k) for k in range(self.n1)]
        self.p2 = [self.pairs(self.move_2, k) for k in range(self.n2)]
        self.core = self.pairs(lambda x, c, a, q, k: (x, c ^ 1, a, q), 0)

    def place(self, x, c, a, q):
        s1, s0 = (q, a) if (self.alt_minor or not self.swap) else (a, q)
        return ((x * 2 + c) * self.s1 + s1) * self.s0 + s0

    def pairs(self, move, k):
        spots = itertools.product(range(self.x), range(2), range(self.alt), range(self.nq))
        return [(self.place(*spot), self.place(*move(*spot, k))) for spot in spots]

    def move_q(self, x, c, a, q, k):
        return (x, c, a, q ^ k)

    def move_1(self, x, c, a, q, k):
        return (x ^ k, c, a, q) if (self.swap and c == 1) else (x, c, a ^ k, q)

    def move_2(self, x, c, a, q, k):
        return (x, c, a ^ k, q) if (self.swap and c == 1) else (x ^ k, c, a, q)

    def natural_rows(self, rows):
        me_dp, me_seq = lax.axis_index("dp"), lax.axis_index("seq")
        mx, mc = me_dp // 2, me_dp % 2
        m1, m0 = me_seq // self.s0, me_seq % self.s0
        minor = self.alt_minor or not self.swap
        ma, mq = (m0, m1) if minor else (m1, m0)
        at = jnp.arange(self.count * rows, dtype=jnp.int32)
        row, at = at % rows, at // rows
        kq, at = at % self.nq, at // self.nq
        k1, at = at % self.n1, at // self.n1
        k2, half = at % self.n2, at // self.n2
        core = mc ^ half
        turned = (core == 1) if self.swap else (core > 1)
        kx = jnp.where(turned, k1, k2)
        ka = jnp.where(turned, k2, k1)
        x, a, q = mx ^ kx, ma ^ ka, mq ^ kq
        s1, s0 = (q, a) if minor else (a, q)
        return (((x * 2 + core) * self.s1 + s1) * self.s0 + s0) * rows + row


def permute(array, pairs):
    return lax.ppermute(array, AXES, pairs)


def cat(*arrays):
    return jnp.concatenate(arrays, axis=0)


def after(array, *others):
    return lax.optimization_barrier((array,) + others)[0]


def fence(*arrays):
    return lax.optimization_barrier(arrays)


def close_lanes(block, rows):
    parts = block.reshape(-1, 3, rows, block.shape[1])
    return jnp.concatenate([parts[:, i] for i in range(3)], axis=-1).reshape(-1, 3 * block.shape[1])


def stage(array, pairs):
    return cat(array, *[permute(array, pairs[k]) for k in range(1, len(pairs))])


def add_parts(parts, dtype):
    total = parts[0].astype(F32)
    for part in parts[1:]:
        total = total + part.astype(F32)
    return total.astype(dtype)


def fold(array, pairs, dtype=None):
    count = len(pairs)
    rows = array.shape[0] // count
    parts = [array[:rows]]
    for k in range(1, count):
        parts.append(permute(array[k * rows : (k + 1) * rows], pairs[k]))
    return add_parts(parts, dtype or array.dtype)


def fold_parts(array, pairs, parts, which):
    rows = array.shape[0] // len(pairs)
    cut = {k: array[k * rows : (k + 1) * rows] for k in which}
    return parts + [permute(cut[k], pairs[k]) if k else cut[k] for k in which]


def dot_nn(a, b):
    return jnp.dot(a, b, preferred_element_type=F32)


def dot_nt(a, b):
    return lax.dot_general(a, b, (((1,), (1,)), ((), ())), preferred_element_type=F32)


def dot_tn(a, b):
    return lax.dot_general(a, b, (((0,), (0,)), ((), ())), preferred_element_type=F32)


def gelu(v):
    return 0.5 * v * (1.0 + jnp.tanh(C0 * (v + C1 * v * v * v)))


def gelu_both(v):
    square = v * v
    t = jnp.tanh(C0 * (v + C1 * v * square))
    half = 0.5 * (1.0 + t)
    slope = half + 0.5 * v * (1.0 - t * t) * (C0 * (1.0 + 3.0 * C1 * square))
    return v * half, slope


def full_spec(shape):
    return pl.BlockSpec(memory_space=pltpu.VMEM)


COST = pl.CostEstimate(flops=1000, bytes_accessed=1000, transcendentals=0)
SCALARS = pl.BlockSpec(memory_space=pltpu.SMEM)
VMEM = pl.BlockSpec(memory_space=pltpu.VMEM)


def one_hot(left, right):
    return jnp.where(left == right, 1.0, 0.0).astype(BF)


def column(count):
    return lax.broadcasted_iota(jnp.int32, (count, 1), 0)


def lane(count):
    return lax.broadcasted_iota(jnp.int32, (1, count), 1)


GAIN, SHIFT, RATE, SCALE, SKIP = range(5)


def params_kernel(key_ref, own_ref, other_ref, wr_ref, rows_ref):
    chan, width = wr_ref.shape[1:]
    half = own_ref.shape[0]
    rows_ref[...] = jnp.zeros_like(rows_ref)
    even = one_hot(2 * column(chan), lane(width))
    odd = one_hot(2 * column(chan) + 1, lane(width))
    same = one_hot(column(chan), lane(chan))
    for layer in range(LAYERS):
        key = key_ref[...] - layer * chan
        whole = dot_nn(one_hot(key[:, :half], column(chan)), own_ref[...])
        whole += dot_nn(one_hot(key[:, half:], column(chan)), other_ref[...])
        whole = whole.astype(BF)
        wr_ref[layer] = whole[:, :width]
        vec = whole[:, width:]
        evens, odds = dot_tn(vec, even), dot_tn(vec, odd)
        turned = dot_tn(vec, same)
        rows_ref[layer, GAIN : GAIN + 1, :] = evens[0:1] + odds[1:2]
        rows_ref[layer, SHIFT : SHIFT + 1, :] = evens[2:3] + odds[3:4]
        for name, k in ((RATE, 4), (SCALE, 5), (SKIP, 6)):
            rows_ref[layer, name : name + 1, :chan] = turned[k : k + 1]


def params_call(key, own, other, width, chan):
    return pl.pallas_call(
        params_kernel,
        out_shape=(
            jax.ShapeDtypeStruct((LAYERS, chan, width), BF),
            jax.ShapeDtypeStruct((LAYERS, 8, width), F32),
        ),
        in_specs=[VMEM] * 3,
        out_specs=(VMEM,) * 2,
        compiler_params=pltpu.CompilerParams(vmem_limit_bytes=VMEM_LIMIT),
        cost_estimate=COST,
        name="params",
    )(key, own, other)


def enter_kernel(starts_n, layer, scal, x_ref, rows_ref, wr_ref, normed_ref, pre_ref, local_ref, last_ref):
    x = x_ref[...].astype(F32)
    centred = x - jnp.mean(x, axis=-1, keepdims=True)
    spread = jnp.mean(centred * centred, axis=-1, keepdims=True)
    gain, shift = rows_ref[layer, GAIN : GAIN + 1, :], rows_ref[layer, SHIFT : SHIFT + 1, :]
    normed = (centred * lax.rsqrt(spread + 1e-05) * gain + shift).astype(BF)
    normed_ref[...] = normed
    pre = dot_nt(normed, wr_ref[layer])
    pre_ref[...] = pre
    rows, chan = pre.shape
    rate = rows_ref[layer, RATE : RATE + 1, :chan]
    state = (1.0 - jnp.exp(-rate)) * gelu(pre)
    row = column(rows)
    k = 1
    while k < rows:
        open_rows = row >= k
        for s in range(starts_n):
            open_rows = open_rows & ~((row >= scal[s]) & (row < scal[s] + k))
        factor = jnp.where(open_rows, jnp.exp(-float(k) * rate), 0.0)
        state = state + factor * pltpu.roll(state, k, 0)
        k *= 2
    local_ref[...] = state
    last_ref[...] = state[rows - 1 :]


def enter_call(layer, starts, x, rows_all, wr_all):
    rows, width = x.shape
    chan = wr_all.shape[1]
    return pl.pallas_call(
        functools.partial(enter_kernel, starts.shape[0], layer),
        out_shape=(
            jax.ShapeDtypeStruct((rows, width), BF),
            jax.ShapeDtypeStruct((rows, chan), F32),
            jax.ShapeDtypeStruct((rows, chan), F32),
            jax.ShapeDtypeStruct((1, chan), F32),
        ),
        in_specs=[SCALARS] + [VMEM] * 3,
        out_specs=(VMEM,) * 4,
        compiler_params=pltpu.CompilerParams(vmem_limit_bytes=VMEM_LIMIT),
        cost_estimate=COST,
        name="enter",
    )(starts, x, rows_all, wr_all)


def mix_kernel(starts_n, layer, scal, hops_ref, lasts_ref, start_ref, rows_ref, pre_ref, local_ref, states_ref, in_ref, mixed_ref):
    rows, chan = pre_ref.shape
    rate = rows_ref[layer, RATE : RATE + 1, :chan]
    hops = hops_ref[...]
    weight = jnp.where(hops >= 0.0, jnp.exp(-jnp.maximum(hops, 0.0) * rate), 0.0)
    many = lasts_ref.shape[0]
    entered = jnp.sum(weight[:many] * lasts_ref[...], axis=0, keepdims=True) + weight[many:] * start_ref[...]
    in_ref[...] = entered
    row = column(rows)
    open_rows = row >= 0
    for s in range(starts_n):
        open_rows = open_rows & ~((row >= scal[s]) & (scal[s] >= 0))
    running = jnp.where(open_rows, jnp.exp(-(row + 1).astype(F32) * rate), 0.0)
    states = local_ref[...] + running * entered
    states_ref[...] = states
    scale, skip = rows_ref[layer, SCALE : SCALE + 1, :chan], rows_ref[layer, SKIP : SKIP + 1, :chan]
    mixed_ref[...] = (scale * states + skip * gelu(pre_ref[...])).astype(BF)


def mix_call(layer, starts, hops, lasts, start_state, rows_all, pre, local_states):
    rows, chan = pre.shape
    return pl.pallas_call(
        functools.partial(mix_kernel, starts.shape[0], layer),
        out_shape=(
            jax.ShapeDtypeStruct((rows, chan), F32),
            jax.ShapeDtypeStruct((1, chan), F32),
            jax.ShapeDtypeStruct((rows, chan), BF),
        ),
        in_specs=[SCALARS] + [VMEM] * 6,
        out_specs=(VMEM,) * 3,
        compiler_params=pltpu.CompilerParams(vmem_limit_bytes=VMEM_LIMIT),
        cost_estimate=COST,
        name="mix",
    )(starts, hops, lasts, start_state, rows_all, pre, local_states)


def back_scan_kernel(starts_n, layer, scal, dmix_ref, rows_ref, local_ref, first_ref):
    rows, chan = dmix_ref.shape
    rate = rows_ref[layer, RATE : RATE + 1, :chan]
    grad = rows_ref[layer, SCALE : SCALE + 1, :chan] * dmix_ref[...]
    row = column(rows)
    k = 1
    while k < rows:
        open_rows = row < rows - k
        for s in range(starts_n):
            open_rows = open_rows & ~((row < scal[s]) & (row >= scal[s] - k))
        factor = jnp.where(open_rows, jnp.exp(-float(k) * rate), 0.0)
        grad = grad + factor * pltpu.roll(grad, rows - k, 0)
        k *= 2
    local_ref[...] = grad
    keep = 1.0
    for s in range(starts_n):
        keep = jnp.where(scal[s] == 0, 0.0, keep)
    first_ref[...] = keep * jnp.exp(-rate) * grad[:1]


def back_scan_call(layer, starts, dmix, rows_all):
    rows, chan = dmix.shape
    return pl.pallas_call(
        functools.partial(back_scan_kernel, starts.shape[0], layer),
        out_shape=(jax.ShapeDtypeStruct((rows, chan), F32), jax.ShapeDtypeStruct((1, chan), F32)),
        in_specs=[SCALARS] + [VMEM] * 2,
        out_specs=(VMEM,) * 2,
        compiler_params=pltpu.CompilerParams(vmem_limit_bytes=VMEM_LIMIT),
        cost_estimate=COST,
        name="back_scan",
    )(starts, dmix, rows_all)


def leave_kernel(
    starts_n,
    layer,
    scal,
    hops_ref,
    firsts_ref,
    key_ref,
    key_col_ref,
    dmix_ref,
    local_ref,
    states_ref,
    in_ref,
    pre_ref,
    normed_ref,
    x_ref,
    rows_ref,
    wr_ref,
    dnorm_ref,
    up_ref,
    up_out_ref,
    low_ref,
    own_ref,
    other_ref,
    small,
):
    rows, chan = dmix_ref.shape
    width = x_ref.shape[1]
    rate = rows_ref[layer, RATE : RATE + 1, :chan]
    decay = jnp.exp(-rate)
    hops = hops_ref[...]
    weight = jnp.where(hops >= 0.0, jnp.exp(-jnp.maximum(hops, 0.0) * rate), 0.0)
    arriving = jnp.sum(weight * firsts_ref[...], axis=0, keepdims=True)
    dmix = dmix_ref[...]
    row = column(rows)
    later = row >= 0
    first = row < 0
    for s in range(starts_n):
        later = later & ~((row < scal[s]) & (scal[s] < rows))
        first = first | (row == scal[s])
    running = jnp.where(later, jnp.exp(-(rows - 1 - row).astype(F32) * rate), 0.0)
    grad = local_ref[...] + running * arriving
    reduced, slope = gelu_both(pre_ref[...])
    states = states_ref[...]
    before = jnp.where(row == 0, in_ref[...], pltpu.roll(states, 1, 0))
    before = jnp.where(first, 0.0, before)
    small[...] = jnp.zeros_like(small)
    small[4:5, :chan] = -decay * jnp.sum(grad * (before - reduced), axis=0, keepdims=True)
    small[5:6, :chan] = jnp.sum(dmix * states, axis=0, keepdims=True)
    small[6:7, :chan] = jnp.sum(dmix * reduced, axis=0, keepdims=True)
    d_reduced = (1.0 - decay) * grad + rows_ref[layer, SKIP : SKIP + 1, :chan] * dmix
    d_pre = (d_reduced * slope).astype(BF)
    d_normed = dnorm_ref[...] + dot_nn(d_pre, wr_ref[layer])
    x = x_ref[...].astype(F32)
    centred = x - jnp.mean(x, axis=-1, keepdims=True)
    spread = jnp.mean(centred * centred, axis=-1, keepdims=True)
    rs = lax.rsqrt(spread + 1e-05)
    xhat = centred * rs
    small[0:1, :] = jnp.sum(d_normed * xhat, axis=0, keepdims=True)
    small[2:3, :] = jnp.sum(d_normed, axis=0, keepdims=True)
    e = d_normed * rows_ref[layer, GAIN : GAIN + 1, :]
    mean_e = jnp.mean(e, axis=-1, keepdims=True)
    mean_ex = jnp.mean(e * xhat, axis=-1, keepdims=True)
    up = up_ref[...].astype(F32) + rs * (e - mean_e - xhat * mean_ex)
    up_out_ref[...] = up
    low_ref[...] = up.astype(BF)
    key = key_ref[...]
    turned = dot_nn(d_pre, one_hot(column(chan), key)).astype(BF)
    grads = dot_tn(turned, normed_ref[...]).astype(BF)
    vecs = small[...].astype(BF)
    key_col = key_col_ref[...]
    pick = column(small.shape[0])
    tail = jnp.zeros((chan, PAD), F32)
    for source, at, spot in ((vecs, 2 * key_col, (0, 2)), (vecs, 2 * key_col + 1, (1, 3))):
        wide = dot_nt(one_hot(at, lane(width)), source)
        tail += dot_nn(wide.astype(BF), one_hot(jnp.where(pick == 0, spot[0], jnp.where(pick == 2, spot[1], -1)), lane(PAD)))
    thin = dot_nt(one_hot(key_col, lane(chan)), vecs[:, :chan])
    tail += dot_nn(thin.astype(BF), one_hot(jnp.where((pick >= 4) & (pick < 7), pick, -1), lane(PAD)))
    half = chan // 2
    own_ref[:, :width] = grads[:half]
    other_ref[:, :width] = grads[half:]
    own_ref[:, width:] = tail[:half].astype(BF)
    other_ref[:, width:] = tail[half:].astype(BF)


def leave_call(layer, starts, hops, firsts, key, dmix, local_grad, kept, rows_all, wr_all, dnorm, up):
    rows, width = kept["stream"].shape
    chan = dmix.shape[1]
    head = jax.ShapeDtypeStruct((chan // 2, width + PAD), BF)
    return pl.pallas_call(
        functools.partial(leave_kernel, starts.shape[0], layer),
        out_shape=(
            jax.ShapeDtypeStruct((rows, width), F32),
            jax.ShapeDtypeStruct((rows, width), BF),
            head,
            head,
        ),
        in_specs=[SCALARS] + [VMEM] * 15,
        out_specs=(VMEM,) * 4,
        scratch_shapes=[pltpu.VMEM((16, width), F32)],
        compiler_params=pltpu.CompilerParams(vmem_limit_bytes=VMEM_LIMIT),
        cost_estimate=COST,
        name="leave",
    )(
        starts,
        hops,
        firsts,
        key.reshape(1, chan),
        key.reshape(chan, 1),
        dmix,
        local_grad,
        kept["states"],
        kept["state_in"],
        kept["pre_reduce"],
        kept["normed"],
        kept["stream"],
        rows_all,
        wr_all,
        dnorm,
        up,
    )


def spread_block(head, count, rows, block):
    at = block * count + column(count)
    slot, group, row = at // (3 * rows), (at // rows) % 3, at % rows
    span = head.shape[1] // 3
    total = None
    for g in range(3):
        source = jnp.where(group == g, slot * rows + row, -1)
        part = dot_nn(one_hot(source, lane(head.shape[0])), head[:, g * span : (g + 1) * span])
        total = part if total is None else total + part
    return total.astype(BF)


def wide_kernel(names, mode, blocks, dims, groups, *refs):
    r = dict(zip(names, (groups,) + refs))
    width, chan = dims
    step = pl.program_id(0)
    forward, backward = mode != "back", mode != "fore"
    pair = "other" in r
    weights = r["weights"] if pair else r["own"]

    def part(low, high):
        if len(weights.shape) == 4:
            return weights[:, 0, :, low:high].reshape(-1, high - low)
        return weights[:, low:high]

    w_gate, w_out, w_expand = [functools.partial(part, *at) for at in ((0, width), (width, 2 * width), (2 * width, 2 * width + chan))]

    @pl.when(step == 0)
    def _():
        if forward:
            r["acc"][...] = r["base"][...].astype(F32)
        if backward:
            r["d_normed"][...] = r["d_normed_in"][...] if "d_normed_in" in r else jnp.zeros_like(r["d_normed"])
            r["d_mixed"][...] = r["d_mixed_in"][...] if "d_mixed_in" in r else jnp.zeros_like(r["d_mixed"])

    if pair:

        @pl.when(step < blocks)
        def _():
            weights[...] = r["own"][...]

        @pl.when(step >= blocks)
        def _():
            weights[...] = r["other"][...]

    normed, mixed = r["normed"][...], r["mixed"][...]
    if forward:
        pre = dot_nt(normed, w_gate())
        expanded = dot_nt(mixed, w_expand())
        if mode == "fore":
            r["pre"][...] = pre
            r["expanded"][...] = expanded
    else:
        pre, expanded = r["pre"][...], r["expanded"][...]
    if backward:
        gate, slope = gelu_both(pre)
    else:
        gate = gelu(pre)
    joined = (expanded * gate).astype(BF)
    if forward:
        r["acc"][...] += dot_nn(joined, w_out())
    if backward:
        low = r["low"][...]
        d_joined = dot_nt(low, w_out())
        d_expanded = (d_joined * gate).astype(BF)
        d_pre = (d_joined * expanded * slope).astype(BF)
        r["d_mixed"][...] += dot_nn(d_expanded, w_expand())
        r["d_normed"][...] += dot_nn(d_pre, w_gate())

        def keep(out):
            out[0], out[1], out[2] = d_pre, joined, d_expanded

        @pl.when(step < blocks)
        def _():
            keep(r["acts_first"])

        @pl.when(step >= blocks)
        def _():
            keep(r["acts_last"])

    if "out" in r:

        @pl.when(step == pl.num_programs(0) - 1)
        def _():
            r["out"][...] = r["acc"][...].astype(r["out"].dtype)


def wide_call(mode, own, other, normed, mixed, base=None, low=None, saved=None, sums=None, out_dtype=F32, job=0, groups=None):
    rows, width = normed.shape
    chan = mixed.shape[1]
    pair = groups is None
    if pair:
        groups = jnp.zeros((1,), jnp.int32)
        blocks, block = 2, own.shape[0] // 2
    else:
        blocks = groups.shape[0] // 2
        block = own.shape[0] * own.shape[2] // groups.shape[0]
    lanes = 2 * width + chan
    forward, backward = mode != "back", mode != "fore"
    ins, outs, scratch = [], [], []
    early = lambda i, _: (jnp.minimum(i, blocks - 1), 0)
    late = lambda i, _: (jnp.maximum(i - blocks, 0), 0)
    if pair:
        ins.append(("own", own, pl.BlockSpec((block, lanes), early)))
        ins.append(("other", other, pl.BlockSpec((block, lanes), late)))
    else:
        deep = (block // own.shape[2], 1, own.shape[2], lanes)
        ins.append(("own", own, pl.BlockSpec(deep, lambda i, at: (at[i], job, 0, 0))))
    ins.append(("normed", normed, full_spec(normed.shape)))
    ins.append(("mixed", mixed, full_spec(mixed.shape)))
    side = pl.BlockSpec((rows, block), lambda i, _: (0, i))
    if forward:
        ins.append(("base", base, full_spec(base.shape)))
    if backward:
        ins.append(("low", low, full_spec(low.shape)))
        if sums is not None:
            ins.append(("d_normed_in", sums[0], full_spec(sums[0].shape)))
            ins.append(("d_mixed_in", sums[1], full_spec(sums[1].shape)))
    if mode == "back":
        ins.append(("pre", saved[0], side))
        ins.append(("expanded", saved[1], side))
    if mode == "fore":
        for name in ("pre", "expanded"):
            outs.append((name, jax.ShapeDtypeStruct((rows, 2 * blocks * block), F32), side))
    if forward:
        if out_dtype == F32:
            outs.append(("acc", jax.ShapeDtypeStruct((rows, width), F32), full_spec((rows, width))))
        else:
            outs.append(("out", jax.ShapeDtypeStruct((rows, width), out_dtype), full_spec((rows, width))))
            scratch.append(("acc", pltpu.VMEM((rows, width), F32)))
    if backward:
        outs.append(("d_normed", jax.ShapeDtypeStruct((rows, width), F32), full_spec((rows, width))))
        outs.append(("d_mixed", jax.ShapeDtypeStruct((rows, chan), F32), full_spec((rows, chan))))
        acts = jax.ShapeDtypeStruct((3, rows, blocks * block), BF)
        for name, at in (("acts_first", early), ("acts_last", late)):
            outs.append((name, acts, pl.BlockSpec((3, rows, block), lambda i, _, at=at: (0, 0, at(i, _)[0]))))
    if pair:
        scratch.append(("weights", pltpu.VMEM((block, lanes), BF)))
    names = ["groups"] + [name for name, _, _ in ins + outs] + [name for name, _ in scratch]
    return pl.pallas_call(
        functools.partial(wide_kernel, names, mode, blocks, (width, chan)),
        grid_spec=pltpu.PrefetchScalarGridSpec(
            num_scalar_prefetch=1,
            grid=(2 * blocks,),
            in_specs=[spec for _, _, spec in ins],
            out_specs=tuple(spec for _, _, spec in outs),
            scratch_shapes=[shape for _, shape in scratch],
        ),
        out_shape=tuple(shape for _, shape, _ in outs),
        compiler_params=pltpu.CompilerParams(vmem_limit_bytes=VMEM_LIMIT),
        cost_estimate=COST,
        name="wide_" + mode,
    )(groups, *[array for _, array, _ in ins])


def grads_kernel(names, head_rows, sub, places, *refs):
    r = dict(zip(names, refs))
    step = pl.program_id(0)
    out = r["grads"] if sub else r["out"]
    at = 0
    for k, name in enumerate(("normed", "low", "mixed")):
        span = r[name].shape[1]
        total = dot_tn(r["acts"][k], r[name][...]) + dot_tn(r["peer_acts"][k], r["peer_" + name][...])
        out[:, at : at + span] = total.astype(BF)
        at += span
    if "head" in r:
        head = (r["head"][...].astype(F32) + r["peer_head"][...].astype(F32)).astype(BF)
        out[:, at:] = spread_block(head, out.shape[0], head_rows, step)
    if sub:
        count = out.shape[0] // sub
        for j in range(count):
            to = pl.multiple_of(places[step * count + j] * sub, 16)
            r["out"][pl.ds(to, sub), :] = out[j * sub : (j + 1) * sub, :]


def grads_call(acts, peer_acts, inputs, peer_inputs, places=None, sub=0, heads=None, head_rows=0):
    rows, span = acts.shape[1:]
    steps = 2
    block = span // steps
    ins = []
    for prefix, array, sides in (("", acts, inputs), ("peer_", peer_acts, peer_inputs)):
        ins.append((prefix + "acts", array, pl.BlockSpec((3, rows, block), lambda i, _: (0, 0, i))))
        for name, side in zip(("normed", "low", "mixed"), sides):
            ins.append((prefix + name, side, full_spec(side.shape)))
    lanes = sum(side.shape[1] for side in inputs)
    if heads is not None:
        ins.append(("head", heads[0], full_spec(heads[0].shape)))
        ins.append(("peer_head", heads[1], full_spec(heads[1].shape)))
        lanes += heads[0].shape[1] // 3
    out_spec = full_spec((span, lanes)) if sub else pl.BlockSpec((block, lanes), lambda i, _: (i, 0))
    names = [name for name, _, _ in ins] + ["out"] + (["grads"] if sub else [])
    return pl.pallas_call(
        functools.partial(grads_kernel, names, head_rows, sub),
        grid_spec=pltpu.PrefetchScalarGridSpec(
            num_scalar_prefetch=1,
            grid=(steps,),
            in_specs=[spec for _, _, spec in ins],
            out_specs=out_spec,
            scratch_shapes=[pltpu.VMEM((block, lanes), BF)] if sub else [],
        ),
        out_shape=jax.ShapeDtypeStruct((span, lanes), BF),
        compiler_params=pltpu.CompilerParams(vmem_limit_bytes=VMEM_LIMIT),
        cost_estimate=COST,
        name="grads",
    )(jnp.zeros((1,), jnp.int32) if places is None else places, *[array for _, array, _ in ins])


def seq_step(lay, held, k):
    pairs = [(d * lay.seq + s, d * lay.seq + (s ^ k)) for d in range(lay.dp) for s in range(lay.seq)]
    return cat(held, permute(held, pairs))


def seq_rest(lay, held):
    k = 2
    while k < lay.seq:
        held = seq_step(lay, held, k)
        k *= 2
    return held


def hops_forward(lay, starts, rows):
    me = lax.axis_index("seq")
    source = jnp.concatenate([me ^ jnp.arange(lay.seq, dtype=jnp.int32), jnp.full((1,), -1, jnp.int32)])
    hops = me - 1 - source
    low, high = (source + 1) * rows, me * rows
    hit = jnp.any((starts[None, :] >= low[:, None]) & (starts[None, :] < high), axis=1)
    return jnp.where((hops >= 0) & ~hit, (hops * rows).astype(F32), -1.0)[:, None]


def hops_backward(lay, starts, rows):
    me = lax.axis_index("seq")
    source = me ^ jnp.arange(lay.seq, dtype=jnp.int32)
    hops = source - me - 1
    low, high = (me + 1) * rows, source * rows
    hit = jnp.any((starts[None, :] >= low) & (starts[None, :] < high[:, None]), axis=1)
    return jnp.where((hops >= 0) & ~hit, (hops * rows).astype(F32), -1.0)[:, None]


def local(
    lay,
    tokens,
    ln_gain,
    ln_shift,
    w_gate,
    w_reduce,
    decay_rate,
    state_scale,
    skip_scale,
    w_expand,
    w_out,
    prev_state,
    item_lengths,
    cotangent,
):
    rows, width = tokens.shape
    chan = w_expand.shape[1]
    small_rows = w_reduce.shape[2]
    ff_rows = w_gate.shape[2]
    job_rows = ff_rows // JOBS
    me_seq = lax.axis_index("seq")
    starts = jnp.cumsum(item_lengths[0])[:-1].astype(jnp.int32)
    near = starts - me_seq * rows
    hops_fore, hops_back = hops_forward(lay, starts, rows), hops_backward(lay, starts, rows)

    def vectors(layer):
        return jnp.concatenate(
            [
                ln_gain[layer].reshape(small_rows, 2),
                ln_shift[layer].reshape(small_rows, 2),
                decay_rate[layer][:, None],
                state_scale[layer][:, None],
                skip_scale[layer][:, None],
                jnp.zeros((small_rows, PAD - SMALL), BF),
            ],
            axis=1,
        )

    head = cat(*[jnp.concatenate([w_reduce[i].T, vectors(i)], axis=1) for i in range(LAYERS)])
    bundles = [jnp.concatenate([w_gate[i].T, w_out[i], w_expand[i].T], axis=1) for i in range(LAYERS)]
    shard_a, shard_b, shard_c, shard_d = [
        bundle[job * job_rows : (job + 1) * job_rows] for bundle in bundles for job in range(JOBS)
    ]
    nature = lay.natural_rows(small_rows)
    lanes = bundles[0].shape[1]
    group = jnp.arange(LAYERS, dtype=jnp.int32)[None, :, None] * chan
    key = (nature.reshape(lay.count, 1, small_rows) + group).reshape(1, -1)

    steps = [list(range(1, lay.nq))[i::3] for i in range(3)]

    def pulls(shard, *which):
        return {k: permute(shard, lay.q[k]) for i in which for k in steps[i]}

    def line_of(shard, pulled):
        return cat(shard, *[pulled[k] for k in range(1, lay.nq)])

    def swap(*arrays):
        return [permute(array, lay.core) for array in arrays]

    line_h = stage(head, lay.q)
    pulled = pulls(shard_a, 0)
    line_h, shard_a, pulled = fence(line_h, shard_a, pulled)
    plane_h = stage(line_h, lay.p1)
    pulled |= pulls(shard_a, 1)
    plane_h, shard_a, pulled = fence(plane_h, shard_a, pulled)
    head_own = stage(plane_h, lay.p2)
    pulled |= pulls(shard_a, 2)
    head_own, line_a, shard_b = fence(head_own, line_of(shard_a, pulled), shard_b)
    (head_other,) = swap(head_own)
    plane_a = stage(line_a, lay.p1)
    pulled = pulls(shard_b, 0)
    head_own, head_other, plane_a, shard_b, pulled = fence(head_own, head_other, plane_a, shard_b, pulled)
    wr_all, rows_all = params_call(key, head_own, head_other, width, chan)
    entered = enter_call(0, near, tokens, rows_all, wr_all)

    def enter(layer, stream, entered, lasts):
        normed, pre_reduce, local_states, _ = entered
        states, state_in, mixed = mix_call(
            layer, near, hops_fore, lasts, prev_state[layer], rows_all, pre_reduce, local_states
        )
        return dict(stream=stream, normed=normed, pre_reduce=pre_reduce, states=states, state_in=state_in, mixed=mixed)

    def leave(layer, kept, sums, reached, upstream):
        upstream, low, *head = leave_call(
            layer, near, hops_back, reached[1], nature, sums[1], reached[0], kept, rows_all, wr_all, sums[0], upstream
        )
        return upstream, low, head

    def both(own, other, base, sums, out_dtype=F32):
        out, d_normed, d_mixed, mine, peers = wide_call(
            "both",
            own,
            other,
            k1["normed"],
            k1["mixed"],
            base=base,
            low=cotangent,
            sums=sums,
            out_dtype=out_dtype,
        )
        return out, [d_normed, d_mixed], mine, peers

    def back(own, other, saved, sums):
        d_normed, d_mixed, mine, peers = wide_call(
            "back", own, other, k0["normed"], k0["mixed"], low=low, saved=saved, sums=sums
        )
        return [d_normed, d_mixed], mine, peers

    a_own = stage(plane_a, lay.p2)
    pulled |= pulls(shard_b, 1, 2)
    a_own, line_b, entered, shard_c = fence(a_own, line_of(shard_b, pulled), entered, shard_c)
    held = seq_step(lay, entered[3], 1)
    (a_other,) = swap(a_own)
    plane_b = stage(after(line_b, held), lay.p1)
    lasts = seq_rest(lay, held)
    pulled = pulls(shard_c, 0)
    a_own, a_other, plane_b, shard_c, pulled, entered, lasts = fence(
        a_own, a_other, plane_b, shard_c, pulled, entered, lasts
    )
    k0 = enter(0, tokens, entered, lasts)
    b_own = stage(plane_b, lay.p2)
    pulled |= pulls(shard_c, 1, 2)
    *save_a, acc = wide_call("fore", a_own, a_other, k0["normed"], k0["mixed"], base=tokens)
    b_own, line_c, acc, shard_d = fence(b_own, line_of(shard_c, pulled), acc, shard_d)
    (b_other,) = swap(b_own)
    plane_c = stage(line_c, lay.p1)
    pulled = pulls(shard_d, 0)
    b_own, b_other, plane_c, shard_d, pulled = fence(b_own, b_other, plane_c, shard_d, pulled)
    c_own = stage(plane_c, lay.p2)
    pulled |= pulls(shard_d, 1, 2)
    *save_b, acc = wide_call("fore", b_own, b_other, k0["normed"], k0["mixed"], base=acc)
    entered = enter_call(1, near, acc, rows_all, wr_all)
    held = seq_step(lay, entered[3], 1)
    c_own, line_d, acc, entered, held = fence(c_own, line_of(shard_d, pulled), acc, entered, held)
    (c_other,) = swap(c_own)
    plane_d = stage(line_d, lay.p1)
    k1 = enter(1, acc, entered, seq_rest(lay, held))
    c_own, c_other, plane_d, k1 = fence(c_own, c_other, plane_d, k1)

    d_own = stage(plane_d, lay.p2)
    ins_1 = (k1["normed"], cotangent, k1["mixed"])
    peer_1 = swap(*ins_1)
    acc, sums, a1_own, a1_peer = both(c_own, c_other, acc, None)
    d_own, acc, sums, a1_own, a1_peer, peer_1 = fence(d_own, acc, sums, a1_own, a1_peer, peer_1)
    (a1_peer,) = swap(a1_peer)
    (d_other,) = swap(d_own)
    a1 = grads_call(a1_own, a1_peer, ins_1, peer_1)
    d_own, d_other, a1 = fence(d_own, d_other, a1)
    a1 = fold(a1, lay.p2)
    output, sums, b1_own, b1_peer = both(d_own, d_other, acc, sums, BF)
    a1, sums, b1_own, b1_peer = fence(a1, sums, b1_own, b1_peer)

    back_local, first_row = back_scan_call(1, near, sums[1], rows_all)
    (b1_peer,) = swap(after(b1_peer, first_row))
    held = seq_step(lay, first_row, 1)
    a1 = fold(after(a1, held), lay.p1)
    b1 = grads_call(b1_own, b1_peer, ins_1, peer_1)
    reached = back_local, seq_rest(lay, after(held, b1))
    upstream, low, head_1 = leave(1, k1, sums, reached, cotangent)
    a1, b1, upstream, low, head_1 = fence(a1, b1, upstream, low, head_1)

    b1 = fold(b1, lay.p2)
    cut = (2 * lay.nq + 2) // 3
    a1_parts = fold_parts(a1, lay.q, [], range(cut))
    peer_0 = swap(k0["normed"], low, k0["mixed"])
    (head_peer,) = swap(head_1[1])
    sums, a0_own, a0_peer = back(a_own, a_other, save_a, None)
    sums, a0_sent, a1, a1_parts = fence(sums, a0_peer, a1, a1_parts)
    a1_done = add_parts(fold_parts(a1, lay.q, a1_parts, range(cut, lay.nq)), F32)
    (a0_peer,) = swap(a0_sent)
    sums, b0_own, b0_peer = back(b_own, b_other, save_b, sums)
    a1_done, b1, peer_0, head_peer, a0_own, a0_peer, sums, b0_own, b0_peer = fence(
        a1_done, b1, peer_0, head_peer, a0_own, a0_peer, sums, b0_own, b0_peer
    )
    ins_0 = (k0["normed"], low, k0["mixed"])
    b1 = fold(b1, lay.p1)
    (b0_peer,) = swap(b0_peer)
    a0 = grads_call(a0_own, a0_peer, ins_0, peer_0, heads=(head_1[0], head_peer), head_rows=small_rows)
    back_local, first_row = back_scan_call(0, near, sums[1], rows_all)
    b1, a0, sums, b0_own, b0_peer, back_local, first_row = fence(
        b1, a0, sums, b0_own, b0_peer, back_local, first_row
    )

    held = seq_step(lay, first_row, 1)
    a0 = fold(after(a0, held), lay.p2)
    _, input_grad, (head_own, head_other) = leave(0, k0, sums, (back_local, seq_rest(lay, held)), upstream)
    a0, b1, head_own, head_other = fence(a0, b1, head_own, head_other)

    a0 = fold(a0, lay.p1)
    b1_parts = fold_parts(b1, lay.q, [], range(cut))
    heads_0 = [head_own, *swap(head_other)]
    b0 = grads_call(b0_own, b0_peer, ins_0, peer_0, heads=heads_0, head_rows=small_rows)
    a0, b0, b1, b1_parts = fence(a0, b0, b1, b1_parts)

    a0_done = fold(a0, lay.q, F32)
    b0 = fold(b0, lay.p2)
    a0_done, b0, b1, b1_parts = fence(a0_done, b0, b1, b1_parts)

    b1_done = add_parts(fold_parts(b1, lay.q, b1_parts, range(cut, lay.nq)), F32)
    b0 = fold(b0, lay.p1)
    b1_done, b0 = fence(b1_done, b0)
    b0_done = fold(b0, lay.q, F32)

    grads = [cat(a0_done[:, :lanes], b0_done[:, :lanes]), cat(a1_done, b1_done)]
    heads_done = [close_lanes(done[:, lanes:], small_rows) for done in (b0_done, a0_done)]
    vecs = [h[:, width : width + SMALL] for h in heads_done]
    return (
        output,
        input_grad,
        jnp.stack([v[:, 0:2].reshape(-1) for v in vecs]),
        jnp.stack([v[:, 2:4].reshape(-1) for v in vecs]),
        jnp.stack([g[:, :width].T for g in grads]),
        jnp.stack([h[:, :width].T for h in heads_done]),
        jnp.stack([v[:, 4] for v in vecs]),
        jnp.stack([v[:, 5] for v in vecs]),
        jnp.stack([v[:, 6] for v in vecs]),
        jnp.stack([g[:, 2 * width :].T for g in grads]),
        jnp.stack([g[:, width : 2 * width] for g in grads]),
    )


def solution(mesh):
    lay = Layout(mesh)
    both = ("dp", "seq")
    return jax.shard_map(
        functools.partial(local, lay),
        mesh=mesh,
        in_specs=(
            P(both, None),
            P(None, both),
            P(None, both),
            P(None, None, both),
            P(None, None, both),
            P(None, both),
            P(None, both),
            P(None, both),
            P(None, None, both),
            P(None, both, None),
            P(None, "dp", None),
            P("dp", None),
            P(both, None),
        ),
        out_specs=(
            P(both, None),
            P(both, None),
            P(None, both),
            P(None, both),
            P(None, None, both),
            P(None, None, both),
            P(None, both),
            P(None, both),
            P(None, both),
            P(None, None, both),
            P(None, both, None),
        ),
        check_vma=False,
    )
```

```python
import functools
import itertools
import math

import jax
import jax.numpy as jnp
from jax import lax
from jax.experimental import pallas as pl
from jax.experimental.pallas import tpu as pltpu
from jax.sharding import PartitionSpec as P

LAYERS = 2
JOBS = 2
AXES = ("dp", "seq")
BF = jnp.bfloat16
F32 = jnp.float32
VMEM_LIMIT = 24 << 20
C0 = math.sqrt(2.0 / math.pi)
C1 = 0.044715
SMALL = 7
PAD = 128


class Layout:
    def __init__(self, mesh):
        self.dp, self.seq = mesh.shape["dp"], mesh.shape["seq"]
        self.x, self.c = self.dp // 2, 2
        self.s1 = 4
        self.s0 = self.seq // 4
        self.count = self.dp * self.seq
        self.alt_minor = self.s0 == self.x
        self.swap = self.s0 == self.x or self.s1 == self.x
        if self.alt_minor or not self.swap:
            self.alt, self.nq = self.s0, self.s1
        else:
            self.alt, self.nq = self.s1, self.s0
        self.n1, self.n2 = self.alt, self.x
        self.q = [self.pairs(self.move_q, k) for k in range(self.nq)]
        self.p1 = [self.pairs(self.move_1, k) for k in range(self.n1)]
        self.p2 = [self.pairs(self.move_2, k) for k in range(self.n2)]
        self.core = self.pairs(lambda x, c, a, q, k: (x, c ^ 1, a, q), 0)

    def place(self, x, c, a, q):
        s1, s0 = (q, a) if (self.alt_minor or not self.swap) else (a, q)
        return ((x * 2 + c) * self.s1 + s1) * self.s0 + s0

    def pairs(self, move, k):
        spots = itertools.product(range(self.x), range(2), range(self.alt), range(self.nq))
        return [(self.place(*spot), self.place(*move(*spot, k))) for spot in spots]

    def move_q(self, x, c, a, q, k):
        return (x, c, a, q ^ k)

    def move_1(self, x, c, a, q, k):
        return (x ^ k, c, a, q) if (self.swap and c == 1) else (x, c, a ^ k, q)

    def move_2(self, x, c, a, q, k):
        return (x, c, a ^ k, q) if (self.swap and c == 1) else (x ^ k, c, a, q)

    def natural_rows(self, rows):
        me_dp, me_seq = lax.axis_index("dp"), lax.axis_index("seq")
        mx, mc = me_dp // 2, me_dp % 2
        m1, m0 = me_seq // self.s0, me_seq % self.s0
        minor = self.alt_minor or not self.swap
        ma, mq = (m0, m1) if minor else (m1, m0)
        at = jnp.arange(self.count * rows, dtype=jnp.int32)
        row, at = at % rows, at // rows
        kq, at = at % self.nq, at // self.nq
        k1, at = at % self.n1, at // self.n1
        k2, half = at % self.n2, at // self.n2
        core = mc ^ half
        turned = (core == 1) if self.swap else (core > 1)
        kx = jnp.where(turned, k1, k2)
        ka = jnp.where(turned, k2, k1)
        x, a, q = mx ^ kx, ma ^ ka, mq ^ kq
        s1, s0 = (q, a) if minor else (a, q)
        return (((x * 2 + core) * self.s1 + s1) * self.s0 + s0) * rows + row


def permute(array, pairs):
    return lax.ppermute(array, AXES, pairs)


def cat(*arrays):
    return jnp.concatenate(arrays, axis=0)


def after(array, *others):
    return lax.optimization_barrier((array,) + others)[0]


def fence(*arrays):
    return lax.optimization_barrier(arrays)


def close_lanes(block, rows):
    parts = block.reshape(-1, 3, rows, block.shape[1])
    return jnp.concatenate([parts[:, i] for i in range(3)], axis=-1).reshape(-1, 3 * block.shape[1])


def stage(array, pairs):
    return cat(array, *[permute(array, pairs[k]) for k in range(1, len(pairs))])


def add_parts(parts, dtype):
    total = parts[0].astype(F32)
    for part in parts[1:]:
        total = total + part.astype(F32)
    return total.astype(dtype)


def fold(array, pairs, dtype=None):
    count = len(pairs)
    rows = array.shape[0] // count
    parts = [array[:rows]]
    for k in range(1, count):
        parts.append(permute(array[k * rows : (k + 1) * rows], pairs[k]))
    return add_parts(parts, dtype or array.dtype)


def fold_parts(array, pairs, parts, which):
    rows = array.shape[0] // len(pairs)
    cut = {k: array[k * rows : (k + 1) * rows] for k in which}
    return parts + [permute(cut[k], pairs[k]) if k else cut[k] for k in which]


def dot_nn(a, b):
    return jnp.dot(a, b, preferred_element_type=F32)


def dot_nt(a, b):
    return lax.dot_general(a, b, (((1,), (1,)), ((), ())), preferred_element_type=F32)


def dot_tn(a, b):
    return lax.dot_general(a, b, (((0,), (0,)), ((), ())), preferred_element_type=F32)


def gelu(v):
    return 0.5 * v * (1.0 + jnp.tanh(C0 * (v + C1 * v * v * v)))


def gelu_both(v):
    square = v * v
    t = jnp.tanh(C0 * (v + C1 * v * square))
    half = 0.5 * (1.0 + t)
    slope = half + 0.5 * v * (1.0 - t * t) * (C0 * (1.0 + 3.0 * C1 * square))
    return v * half, slope


def full_spec(shape):
    return pl.BlockSpec(memory_space=pltpu.VMEM)


COST = pl.CostEstimate(flops=1000, bytes_accessed=1000, transcendentals=0)
SCALARS = pl.BlockSpec(memory_space=pltpu.SMEM)
VMEM = pl.BlockSpec(memory_space=pltpu.VMEM)


def one_hot(left, right):
    return jnp.where(left == right, 1.0, 0.0).astype(BF)


def column(count):
    return lax.broadcasted_iota(jnp.int32, (count, 1), 0)


def lane(count):
    return lax.broadcasted_iota(jnp.int32, (1, count), 1)


GAIN, SHIFT, RATE, SCALE, SKIP = range(5)


def params_kernel(key_ref, own_ref, other_ref, wr_ref, rows_ref):
    chan, width = wr_ref.shape[1:]
    half = own_ref.shape[0]
    rows_ref[...] = jnp.zeros_like(rows_ref)
    even = one_hot(2 * column(chan), lane(width))
    odd = one_hot(2 * column(chan) + 1, lane(width))
    same = one_hot(column(chan), lane(chan))
    for layer in range(LAYERS):
        key = key_ref[...] - layer * chan
        whole = dot_nn(one_hot(key[:, :half], column(chan)), own_ref[...])
        whole += dot_nn(one_hot(key[:, half:], column(chan)), other_ref[...])
        whole = whole.astype(BF)
        wr_ref[layer] = whole[:, :width]
        vec = whole[:, width:]
        evens, odds = dot_tn(vec, even), dot_tn(vec, odd)
        turned = dot_tn(vec, same)
        rows_ref[layer, GAIN : GAIN + 1, :] = evens[0:1] + odds[1:2]
        rows_ref[layer, SHIFT : SHIFT + 1, :] = evens[2:3] + odds[3:4]
        for name, k in ((RATE, 4), (SCALE, 5), (SKIP, 6)):
            rows_ref[layer, name : name + 1, :chan] = turned[k : k + 1]


def params_call(key, own, other, width, chan):
    return pl.pallas_call(
        params_kernel,
        out_shape=(
            jax.ShapeDtypeStruct((LAYERS, chan, width), BF),
            jax.ShapeDtypeStruct((LAYERS, 8, width), F32),
        ),
        in_specs=[VMEM] * 3,
        out_specs=(VMEM,) * 2,
        compiler_params=pltpu.CompilerParams(vmem_limit_bytes=VMEM_LIMIT),
        cost_estimate=COST,
        name="params",
    )(key, own, other)


def enter_kernel(starts_n, layer, scal, x_ref, rows_ref, wr_ref, normed_ref, pre_ref, local_ref, last_ref):
    x = x_ref[...].astype(F32)
    centred = x - jnp.mean(x, axis=-1, keepdims=True)
    spread = jnp.mean(centred * centred, axis=-1, keepdims=True)
    gain, shift = rows_ref[layer, GAIN : GAIN + 1, :], rows_ref[layer, SHIFT : SHIFT + 1, :]
    normed = (centred * lax.rsqrt(spread + 1e-05) * gain + shift).astype(BF)
    normed_ref[...] = normed
    pre = dot_nt(normed, wr_ref[layer])
    pre_ref[...] = pre
    rows, chan = pre.shape
    rate = rows_ref[layer, RATE : RATE + 1, :chan]
    state = (1.0 - jnp.exp(-rate)) * gelu(pre)
    row = column(rows)
    k = 1
    while k < rows:
        open_rows = row >= k
        for s in range(starts_n):
            open_rows = open_rows & ~((row >= scal[s]) & (row < scal[s] + k))
        factor = jnp.where(open_rows, jnp.exp(-float(k) * rate), 0.0)
        state = state + factor * pltpu.roll(state, k, 0)
        k *= 2
    local_ref[...] = state
    last_ref[...] = state[rows - 1 :]


def enter_call(layer, starts, x, rows_all, wr_all):
    rows, width = x.shape
    chan = wr_all.shape[1]
    return pl.pallas_call(
        functools.partial(enter_kernel, starts.shape[0], layer),
        out_shape=(
            jax.ShapeDtypeStruct((rows, width), BF),
            jax.ShapeDtypeStruct((rows, chan), F32),
            jax.ShapeDtypeStruct((rows, chan), F32),
            jax.ShapeDtypeStruct((1, chan), F32),
        ),
        in_specs=[SCALARS] + [VMEM] * 3,
        out_specs=(VMEM,) * 4,
        compiler_params=pltpu.CompilerParams(vmem_limit_bytes=VMEM_LIMIT),
        cost_estimate=COST,
        name="enter",
    )(starts, x, rows_all, wr_all)


def mix_kernel(starts_n, layer, scal, hops_ref, lasts_ref, start_ref, rows_ref, pre_ref, local_ref, states_ref, in_ref, mixed_ref):
    rows, chan = pre_ref.shape
    rate = rows_ref[layer, RATE : RATE + 1, :chan]
    hops = hops_ref[...]
    weight = jnp.where(hops >= 0.0, jnp.exp(-jnp.maximum(hops, 0.0) * rate), 0.0)
    many = lasts_ref.shape[0]
    entered = jnp.sum(weight[:many] * lasts_ref[...], axis=0, keepdims=True) + weight[many:] * start_ref[...]
    in_ref[...] = entered
    row = column(rows)
    open_rows = row >= 0
    for s in range(starts_n):
        open_rows = open_rows & ~((row >= scal[s]) & (scal[s] >= 0))
    running = jnp.where(open_rows, jnp.exp(-(row + 1).astype(F32) * rate), 0.0)
    states = local_ref[...] + running * entered
    states_ref[...] = states
    scale, skip = rows_ref[layer, SCALE : SCALE + 1, :chan], rows_ref[layer, SKIP : SKIP + 1, :chan]
    mixed_ref[...] = (scale * states + skip * gelu(pre_ref[...])).astype(BF)


def mix_call(layer, starts, hops, lasts, start_state, rows_all, pre, local_states):
    rows, chan = pre.shape
    return pl.pallas_call(
        functools.partial(mix_kernel, starts.shape[0], layer),
        out_shape=(
            jax.ShapeDtypeStruct((rows, chan), F32),
            jax.ShapeDtypeStruct((1, chan), F32),
            jax.ShapeDtypeStruct((rows, chan), BF),
        ),
        in_specs=[SCALARS] + [VMEM] * 6,
        out_specs=(VMEM,) * 3,
        compiler_params=pltpu.CompilerParams(vmem_limit_bytes=VMEM_LIMIT),
        cost_estimate=COST,
        name="mix",
    )(starts, hops, lasts, start_state, rows_all, pre, local_states)


def back_scan_kernel(starts_n, layer, scal, dmix_ref, rows_ref, local_ref, first_ref):
    rows, chan = dmix_ref.shape
    rate = rows_ref[layer, RATE : RATE + 1, :chan]
    grad = rows_ref[layer, SCALE : SCALE + 1, :chan] * dmix_ref[...]
    row = column(rows)
    k = 1
    while k < rows:
        open_rows = row < rows - k
        for s in range(starts_n):
            open_rows = open_rows & ~((row < scal[s]) & (row >= scal[s] - k))
        factor = jnp.where(open_rows, jnp.exp(-float(k) * rate), 0.0)
        grad = grad + factor * pltpu.roll(grad, rows - k, 0)
        k *= 2
    local_ref[...] = grad
    keep = 1.0
    for s in range(starts_n):
        keep = jnp.where(scal[s] == 0, 0.0, keep)
    first_ref[...] = keep * jnp.exp(-rate) * grad[:1]


def back_scan_call(layer, starts, dmix, rows_all):
    rows, chan = dmix.shape
    return pl.pallas_call(
        functools.partial(back_scan_kernel, starts.shape[0], layer),
        out_shape=(jax.ShapeDtypeStruct((rows, chan), F32), jax.ShapeDtypeStruct((1, chan), F32)),
        in_specs=[SCALARS] + [VMEM] * 2,
        out_specs=(VMEM,) * 2,
        compiler_params=pltpu.CompilerParams(vmem_limit_bytes=VMEM_LIMIT),
        cost_estimate=COST,
        name="back_scan",
    )(starts, dmix, rows_all)


def leave_kernel(
    starts_n,
    layer,
    scal,
    hops_ref,
    firsts_ref,
    key_ref,
    key_col_ref,
    dmix_ref,
    local_ref,
    states_ref,
    in_ref,
    pre_ref,
    normed_ref,
    x_ref,
    rows_ref,
    wr_ref,
    dnorm_ref,
    up_ref,
    up_out_ref,
    low_ref,
    own_ref,
    other_ref,
    small,
):
    rows, chan = dmix_ref.shape
    width = x_ref.shape[1]
    rate = rows_ref[layer, RATE : RATE + 1, :chan]
    decay = jnp.exp(-rate)
    hops = hops_ref[...]
    weight = jnp.where(hops >= 0.0, jnp.exp(-jnp.maximum(hops, 0.0) * rate), 0.0)
    arriving = jnp.sum(weight * firsts_ref[...], axis=0, keepdims=True)
    dmix = dmix_ref[...]
    row = column(rows)
    later = row >= 0
    first = row < 0
    for s in range(starts_n):
        later = later & ~((row < scal[s]) & (scal[s] < rows))
        first = first | (row == scal[s])
    running = jnp.where(later, jnp.exp(-(rows - 1 - row).astype(F32) * rate), 0.0)
    grad = local_ref[...] + running * arriving
    reduced, slope = gelu_both(pre_ref[...])
    states = states_ref[...]
    before = jnp.where(row == 0, in_ref[...], pltpu.roll(states, 1, 0))
    before = jnp.where(first, 0.0, before)
    small[...] = jnp.zeros_like(small)
    small[4:5, :chan] = -decay * jnp.sum(grad * (before - reduced), axis=0, keepdims=True)
    small[5:6, :chan] = jnp.sum(dmix * states, axis=0, keepdims=True)
    small[6:7, :chan] = jnp.sum(dmix * reduced, axis=0, keepdims=True)
    d_reduced = (1.0 - decay) * grad + rows_ref[layer, SKIP : SKIP + 1, :chan] * dmix
    d_pre = (d_reduced * slope).astype(BF)
    d_normed = dnorm_ref[...] + dot_nn(d_pre, wr_ref[layer])
    x = x_ref[...].astype(F32)
    centred = x - jnp.mean(x, axis=-1, keepdims=True)
    spread = jnp.mean(centred * centred, axis=-1, keepdims=True)
    rs = lax.rsqrt(spread + 1e-05)
    xhat = centred * rs
    small[0:1, :] = jnp.sum(d_normed * xhat, axis=0, keepdims=True)
    small[2:3, :] = jnp.sum(d_normed, axis=0, keepdims=True)
    e = d_normed * rows_ref[layer, GAIN : GAIN + 1, :]
    mean_e = jnp.mean(e, axis=-1, keepdims=True)
    mean_ex = jnp.mean(e * xhat, axis=-1, keepdims=True)
    up = up_ref[...].astype(F32) + rs * (e - mean_e - xhat * mean_ex)
    up_out_ref[...] = up
    low_ref[...] = up.astype(BF)
    key = key_ref[...]
    turned = dot_nn(d_pre, one_hot(column(chan), key)).astype(BF)
    grads = dot_tn(turned, normed_ref[...]).astype(BF)
    vecs = small[...].astype(BF)
    key_col = key_col_ref[...]
    pick = column(small.shape[0])
    tail = jnp.zeros((chan, PAD), F32)
    for source, at, spot in ((vecs, 2 * key_col, (0, 2)), (vecs, 2 * key_col + 1, (1, 3))):
        wide = dot_nt(one_hot(at, lane(width)), source)
        tail += dot_nn(wide.astype(BF), one_hot(jnp.where(pick == 0, spot[0], jnp.where(pick == 2, spot[1], -1)), lane(PAD)))
    thin = dot_nt(one_hot(key_col, lane(chan)), vecs[:, :chan])
    tail += dot_nn(thin.astype(BF), one_hot(jnp.where((pick >= 4) & (pick < 7), pick, -1), lane(PAD)))
    half = chan // 2
    own_ref[:, :width] = grads[:half]
    other_ref[:, :width] = grads[half:]
    own_ref[:, width:] = tail[:half].astype(BF)
    other_ref[:, width:] = tail[half:].astype(BF)


def leave_call(layer, starts, hops, firsts, key, dmix, local_grad, kept, rows_all, wr_all, dnorm, up):
    rows, width = kept["stream"].shape
    chan = dmix.shape[1]
    head = jax.ShapeDtypeStruct((chan // 2, width + PAD), BF)
    return pl.pallas_call(
        functools.partial(leave_kernel, starts.shape[0], layer),
        out_shape=(
            jax.ShapeDtypeStruct((rows, width), F32),
            jax.ShapeDtypeStruct((rows, width), BF),
            head,
            head,
        ),
        in_specs=[SCALARS] + [VMEM] * 15,
        out_specs=(VMEM,) * 4,
        scratch_shapes=[pltpu.VMEM((16, width), F32)],
        compiler_params=pltpu.CompilerParams(vmem_limit_bytes=VMEM_LIMIT),
        cost_estimate=COST,
        name="leave",
    )(
        starts,
        hops,
        firsts,
        key.reshape(1, chan),
        key.reshape(chan, 1),
        dmix,
        local_grad,
        kept["states"],
        kept["state_in"],
        kept["pre_reduce"],
        kept["normed"],
        kept["stream"],
        rows_all,
        wr_all,
        dnorm,
        up,
    )


def spread_block(head, count, rows, block):
    at = block * count + column(count)
    slot, group, row = at // (3 * rows), (at // rows) % 3, at % rows
    span = head.shape[1] // 3
    total = None
    for g in range(3):
        source = jnp.where(group == g, slot * rows + row, -1)
        part = dot_nn(one_hot(source, lane(head.shape[0])), head[:, g * span : (g + 1) * span])
        total = part if total is None else total + part
    return total.astype(BF)


def wide_kernel(names, mode, blocks, dims, groups, *refs):
    r = dict(zip(names, (groups,) + refs))
    width, chan = dims
    step = pl.program_id(0)
    forward, backward = mode != "back", mode != "fore"
    pair = "other" in r
    weights = r["weights"] if pair else r["own"]

    def part(low, high):
        if len(weights.shape) == 4:
            return weights[:, 0, :, low:high].reshape(-1, high - low)
        return weights[:, low:high]

    w_gate, w_out, w_expand = [functools.partial(part, *at) for at in ((0, width), (width, 2 * width), (2 * width, 2 * width + chan))]

    @pl.when(step == 0)
    def _():
        if forward:
            r["acc"][...] = r["base"][...].astype(F32)
        if backward:
            r["d_normed"][...] = r["d_normed_in"][...] if "d_normed_in" in r else jnp.zeros_like(r["d_normed"])
            r["d_mixed"][...] = r["d_mixed_in"][...] if "d_mixed_in" in r else jnp.zeros_like(r["d_mixed"])

    if pair:

        @pl.when(step < blocks)
        def _():
            weights[...] = r["own"][...]

        @pl.when(step >= blocks)
        def _():
            weights[...] = r["other"][...]

    normed, mixed = r["normed"][...], r["mixed"][...]
    if forward:
        pre = dot_nt(normed, w_gate())
        expanded = dot_nt(mixed, w_expand())
        if mode == "fore":
            r["pre"][...] = pre
            r["expanded"][...] = expanded
    else:
        pre, expanded = r["pre"][...], r["expanded"][...]
    if backward:
        gate, slope = gelu_both(pre)
    else:
        gate = gelu(pre)
    joined = (expanded * gate).astype(BF)
    if forward:
        r["acc"][...] += dot_nn(joined, w_out())
    if backward:
        low = r["low"][...]
        d_joined = dot_nt(low, w_out())
        d_expanded = (d_joined * gate).astype(BF)
        d_pre = (d_joined * expanded * slope).astype(BF)
        r["d_mixed"][...] += dot_nn(d_expanded, w_expand())
        r["d_normed"][...] += dot_nn(d_pre, w_gate())

        def keep(out):
            out[0], out[1], out[2] = d_pre, joined, d_expanded

        @pl.when(step < blocks)
        def _():
            keep(r["acts_first"])

        @pl.when(step >= blocks)
        def _():
            keep(r["acts_last"])

    if "out" in r:

        @pl.when(step == pl.num_programs(0) - 1)
        def _():
            r["out"][...] = r["acc"][...].astype(r["out"].dtype)


def wide_call(mode, own, other, normed, mixed, base=None, low=None, saved=None, sums=None, out_dtype=F32, job=0, groups=None):
    rows, width = normed.shape
    chan = mixed.shape[1]
    pair = groups is None
    if pair:
        groups = jnp.zeros((1,), jnp.int32)
        blocks, block = 2, own.shape[0] // 2
    else:
        blocks = groups.shape[0] // 2
        block = own.shape[0] * own.shape[2] // groups.shape[0]
    lanes = 2 * width + chan
    forward, backward = mode != "back", mode != "fore"
    ins, outs, scratch = [], [], []
    early = lambda i, _: (jnp.minimum(i, blocks - 1), 0)
    late = lambda i, _: (jnp.maximum(i - blocks, 0), 0)
    if pair:
        ins.append(("own", own, pl.BlockSpec((block, lanes), early)))
        ins.append(("other", other, pl.BlockSpec((block, lanes), late)))
    else:
        deep = (block // own.shape[2], 1, own.shape[2], lanes)
        ins.append(("own", own, pl.BlockSpec(deep, lambda i, at: (at[i], job, 0, 0))))
    ins.append(("normed", normed, full_spec(normed.shape)))
    ins.append(("mixed", mixed, full_spec(mixed.shape)))
    side = pl.BlockSpec((rows, block), lambda i, _: (0, i))
    if forward:
        ins.append(("base", base, full_spec(base.shape)))
    if backward:
        ins.append(("low", low, full_spec(low.shape)))
        if sums is not None:
            ins.append(("d_normed_in", sums[0], full_spec(sums[0].shape)))
            ins.append(("d_mixed_in", sums[1], full_spec(sums[1].shape)))
    if mode == "back":
        ins.append(("pre", saved[0], side))
        ins.append(("expanded", saved[1], side))
    if mode == "fore":
        for name in ("pre", "expanded"):
            outs.append((name, jax.ShapeDtypeStruct((rows, 2 * blocks * block), F32), side))
    if forward:
        if out_dtype == F32:
            outs.append(("acc", jax.ShapeDtypeStruct((rows, width), F32), full_spec((rows, width))))
        else:
            outs.append(("out", jax.ShapeDtypeStruct((rows, width), out_dtype), full_spec((rows, width))))
            scratch.append(("acc", pltpu.VMEM((rows, width), F32)))
    if backward:
        outs.append(("d_normed", jax.ShapeDtypeStruct((rows, width), F32), full_spec((rows, width))))
        outs.append(("d_mixed", jax.ShapeDtypeStruct((rows, chan), F32), full_spec((rows, chan))))
        acts = jax.ShapeDtypeStruct((3, rows, blocks * block), BF)
        for name, at in (("acts_first", early), ("acts_last", late)):
            outs.append((name, acts, pl.BlockSpec((3, rows, block), lambda i, _, at=at: (0, 0, at(i, _)[0]))))
    if pair:
        scratch.append(("weights", pltpu.VMEM((block, lanes), BF)))
    names = ["groups"] + [name for name, _, _ in ins + outs] + [name for name, _ in scratch]
    return pl.pallas_call(
        functools.partial(wide_kernel, names, mode, blocks, (width, chan)),
        grid_spec=pltpu.PrefetchScalarGridSpec(
            num_scalar_prefetch=1,
            grid=(2 * blocks,),
            in_specs=[spec for _, _, spec in ins],
            out_specs=tuple(spec for _, _, spec in outs),
            scratch_shapes=[shape for _, shape in scratch],
        ),
        out_shape=tuple(shape for _, shape, _ in outs),
        compiler_params=pltpu.CompilerParams(vmem_limit_bytes=VMEM_LIMIT),
        cost_estimate=COST,
        name="wide_" + mode,
    )(groups, *[array for _, array, _ in ins])


def grads_kernel(names, head_rows, sub, places, *refs):
    r = dict(zip(names, refs))
    step = pl.program_id(0)
    out = r["grads"] if sub else r["out"]
    at = 0
    for k, name in enumerate(("normed", "low", "mixed")):
        span = r[name].shape[1]
        total = dot_tn(r["acts"][k], r[name][...]) + dot_tn(r["peer_acts"][k], r["peer_" + name][...])
        out[:, at : at + span] = total.astype(BF)
        at += span
    if "head" in r:
        head = (r["head"][...].astype(F32) + r["peer_head"][...].astype(F32)).astype(BF)
        out[:, at:] = spread_block(head, out.shape[0], head_rows, step)
    if sub:
        count = out.shape[0] // sub
        for j in range(count):
            to = pl.multiple_of(places[step * count + j] * sub, 16)
            r["out"][pl.ds(to, sub), :] = out[j * sub : (j + 1) * sub, :]


def grads_call(acts, peer_acts, inputs, peer_inputs, places=None, sub=0, heads=None, head_rows=0):
    rows, span = acts.shape[1:]
    steps = 2
    block = span // steps
    ins = []
    for prefix, array, sides in (("", acts, inputs), ("peer_", peer_acts, peer_inputs)):
        ins.append((prefix + "acts", array, pl.BlockSpec((3, rows, block), lambda i, _: (0, 0, i))))
        for name, side in zip(("normed", "low", "mixed"), sides):
            ins.append((prefix + name, side, full_spec(side.shape)))
    lanes = sum(side.shape[1] for side in inputs)
    if heads is not None:
        ins.append(("head", heads[0], full_spec(heads[0].shape)))
        ins.append(("peer_head", heads[1], full_spec(heads[1].shape)))
        lanes += heads[0].shape[1] // 3
    out_spec = full_spec((span, lanes)) if sub else pl.BlockSpec((block, lanes), lambda i, _: (i, 0))
    names = [name for name, _, _ in ins] + ["out"] + (["grads"] if sub else [])
    return pl.pallas_call(
        functools.partial(grads_kernel, names, head_rows, sub),
        grid_spec=pltpu.PrefetchScalarGridSpec(
            num_scalar_prefetch=1,
            grid=(steps,),
            in_specs=[spec for _, _, spec in ins],
            out_specs=out_spec,
            scratch_shapes=[pltpu.VMEM((block, lanes), BF)] if sub else [],
        ),
        out_shape=jax.ShapeDtypeStruct((span, lanes), BF),
        compiler_params=pltpu.CompilerParams(vmem_limit_bytes=VMEM_LIMIT),
        cost_estimate=COST,
        name="grads",
    )(jnp.zeros((1,), jnp.int32) if places is None else places, *[array for _, array, _ in ins])


def seq_step(lay, held, k):
    pairs = [(d * lay.seq + s, d * lay.seq + (s ^ k)) for d in range(lay.dp) for s in range(lay.seq)]
    return cat(held, permute(held, pairs))


def seq_rest(lay, held):
    k = 2
    while k < lay.seq:
        held = seq_step(lay, held, k)
        k *= 2
    return held


def hops_forward(lay, starts, rows):
    me = lax.axis_index("seq")
    source = jnp.concatenate([me ^ jnp.arange(lay.seq, dtype=jnp.int32), jnp.full((1,), -1, jnp.int32)])
    hops = me - 1 - source
    low, high = (source + 1) * rows, me * rows
    hit = jnp.any((starts[None, :] >= low[:, None]) & (starts[None, :] < high), axis=1)
    return jnp.where((hops >= 0) & ~hit, (hops * rows).astype(F32), -1.0)[:, None]


def hops_backward(lay, starts, rows):
    me = lax.axis_index("seq")
    source = me ^ jnp.arange(lay.seq, dtype=jnp.int32)
    hops = source - me - 1
    low, high = (me + 1) * rows, source * rows
    hit = jnp.any((starts[None, :] >= low) & (starts[None, :] < high[:, None]), axis=1)
    return jnp.where((hops >= 0) & ~hit, (hops * rows).astype(F32), -1.0)[:, None]


def local(
    lay,
    tokens,
    ln_gain,
    ln_shift,
    w_gate,
    w_reduce,
    decay_rate,
    state_scale,
    skip_scale,
    w_expand,
    w_out,
    prev_state,
    item_lengths,
    cotangent,
):
    rows, width = tokens.shape
    chan = w_expand.shape[1]
    small_rows = w_reduce.shape[2]
    ff_rows = w_gate.shape[2]
    job_rows = ff_rows // JOBS
    me_seq = lax.axis_index("seq")
    starts = jnp.cumsum(item_lengths[0])[:-1].astype(jnp.int32)
    near = starts - me_seq * rows
    hops_fore, hops_back = hops_forward(lay, starts, rows), hops_backward(lay, starts, rows)

    def vectors(layer):
        return jnp.concatenate(
            [
                ln_gain[layer].reshape(small_rows, 2),
                ln_shift[layer].reshape(small_rows, 2),
                decay_rate[layer][:, None],
                state_scale[layer][:, None],
                skip_scale[layer][:, None],
                jnp.zeros((small_rows, PAD - SMALL), BF),
            ],
            axis=1,
        )

    head = cat(*[jnp.concatenate([w_reduce[i].T, vectors(i)], axis=1) for i in range(LAYERS)])
    bundles = [jnp.concatenate([w_gate[i].T, w_out[i], w_expand[i].T], axis=1) for i in range(LAYERS)]
    shard_a, shard_b, shard_c, shard_d = [
        bundle[job * job_rows : (job + 1) * job_rows] for bundle in bundles for job in range(JOBS)
    ]
    nature = lay.natural_rows(small_rows)
    lanes = bundles[0].shape[1]
    group = jnp.arange(LAYERS, dtype=jnp.int32)[None, :, None] * chan
    key = (nature.reshape(lay.count, 1, small_rows) + group).reshape(1, -1)

    steps = [list(range(1, lay.nq))[i::3] for i in range(3)]

    def pulls(shard, *which):
        return {k: permute(shard, lay.q[k]) for i in which for k in steps[i]}

    def line_of(shard, pulled):
        return cat(shard, *[pulled[k] for k in range(1, lay.nq)])

    def swap(*arrays):
        return [permute(array, lay.core) for array in arrays]

    line_h = stage(head, lay.q)
    pulled = pulls(shard_a, 0)
    line_h, shard_a, pulled = fence(line_h, shard_a, pulled)
    plane_h = stage(line_h, lay.p1)
    pulled |= pulls(shard_a, 1)
    plane_h, shard_a, pulled = fence(plane_h, shard_a, pulled)
    head_own = stage(plane_h, lay.p2)
    pulled |= pulls(shard_a, 2)
    head_own, line_a, shard_b = fence(head_own, line_of(shard_a, pulled), shard_b)
    (head_other,) = swap(head_own)
    plane_a = stage(line_a, lay.p1)
    pulled = pulls(shard_b, 0)
    head_own, head_other, plane_a, shard_b, pulled = fence(head_own, head_other, plane_a, shard_b, pulled)
    wr_all, rows_all = params_call(key, head_own, head_other, width, chan)
    entered = enter_call(0, near, tokens, rows_all, wr_all)

    def enter(layer, stream, entered, lasts):
        normed, pre_reduce, local_states, _ = entered
        states, state_in, mixed = mix_call(
            layer, near, hops_fore, lasts, prev_state[layer], rows_all, pre_reduce, local_states
        )
        return dict(stream=stream, normed=normed, pre_reduce=pre_reduce, states=states, state_in=state_in, mixed=mixed)

    def leave(layer, kept, sums, reached, upstream):
        upstream, low, *head = leave_call(
            layer, near, hops_back, reached[1], nature, sums[1], reached[0], kept, rows_all, wr_all, sums[0], upstream
        )
        return upstream, low, head

    def both(own, other, base, sums, out_dtype=F32):
        out, d_normed, d_mixed, mine, peers = wide_call(
            "both",
            own,
            other,
            k1["normed"],
            k1["mixed"],
            base=base,
            low=cotangent,
            sums=sums,
            out_dtype=out_dtype,
        )
        return out, [d_normed, d_mixed], mine, peers

    def back(own, other, saved, sums):
        d_normed, d_mixed, mine, peers = wide_call(
            "back", own, other, k0["normed"], k0["mixed"], low=low, saved=saved, sums=sums
        )
        return [d_normed, d_mixed], mine, peers

    a_own = stage(plane_a, lay.p2)
    pulled |= pulls(shard_b, 1, 2)
    a_own, line_b, entered, shard_c = fence(a_own, line_of(shard_b, pulled), entered, shard_c)
    held = seq_step(lay, entered[3], 1)
    (a_other,) = swap(a_own)
    plane_b = stage(after(line_b, held), lay.p1)
    lasts = seq_rest(lay, held)
    pulled = pulls(shard_c, 0)
    a_own, a_other, plane_b, shard_c, pulled, entered, lasts = fence(
        a_own, a_other, plane_b, shard_c, pulled, entered, lasts
    )
    k0 = enter(0, tokens, entered, lasts)
    b_own = stage(plane_b, lay.p2)
    pulled |= pulls(shard_c, 1, 2)
    *save_a, acc = wide_call("fore", a_own, a_other, k0["normed"], k0["mixed"], base=tokens)
    b_own, line_c, acc, shard_d = fence(b_own, line_of(shard_c, pulled), acc, shard_d)
    (b_other,) = swap(b_own)
    plane_c = stage(line_c, lay.p1)
    pulled = pulls(shard_d, 0)
    b_own, b_other, plane_c, shard_d, pulled = fence(b_own, b_other, plane_c, shard_d, pulled)
    c_own = stage(plane_c, lay.p2)
    pulled |= pulls(shard_d, 1, 2)
    *save_b, acc = wide_call("fore", b_own, b_other, k0["normed"], k0["mixed"], base=acc)
    entered = enter_call(1, near, acc, rows_all, wr_all)
    held = seq_step(lay, entered[3], 1)
    c_own, line_d, acc, entered, held = fence(c_own, line_of(shard_d, pulled), acc, entered, held)
    (c_other,) = swap(c_own)
    plane_d = stage(line_d, lay.p1)
    k1 = enter(1, acc, entered, seq_rest(lay, held))
    c_own, c_other, plane_d, k1 = fence(c_own, c_other, plane_d, k1)

    d_own = stage(plane_d, lay.p2)
    ins_1 = (k1["normed"], cotangent, k1["mixed"])
    peer_1 = swap(*ins_1)
    acc, sums, a1_own, a1_peer = both(c_own, c_other, acc, None)
    d_own, acc, sums, a1_own, a1_peer, peer_1 = fence(d_own, acc, sums, a1_own, a1_peer, peer_1)
    (a1_peer,) = swap(a1_peer)
    (d_other,) = swap(d_own)
    a1 = grads_call(a1_own, a1_peer, ins_1, peer_1)
    d_own, d_other, a1 = fence(d_own, d_other, a1)
    a1 = fold(a1, lay.p2)
    output, sums, b1_own, b1_peer = both(d_own, d_other, acc, sums, BF)
    a1, sums, b1_own, b1_peer = fence(a1, sums, b1_own, b1_peer)

    back_local, first_row = back_scan_call(1, near, sums[1], rows_all)
    (b1_peer,) = swap(after(b1_peer, first_row))
    held = seq_step(lay, first_row, 1)
    a1 = fold(after(a1, held), lay.p1)
    b1 = grads_call(b1_own, b1_peer, ins_1, peer_1)
    reached = back_local, seq_rest(lay, after(held, b1))
    upstream, low, head_1 = leave(1, k1, sums, reached, cotangent)
    a1, b1, upstream, low, head_1 = fence(a1, b1, upstream, low, head_1)

    b1 = fold(b1, lay.p2)
    cut = (2 * lay.nq + 2) // 3
    a1_parts = fold_parts(a1, lay.q, [], range(cut))
    peer_0 = swap(k0["normed"], low, k0["mixed"])
    (head_peer,) = swap(head_1[1])
    sums, a0_own, a0_peer = back(a_own, a_other, save_a, None)
    sums, a0_sent, a1, a1_parts = fence(sums, a0_peer, a1, a1_parts)
    a1_done = add_parts(fold_parts(a1, lay.q, a1_parts, range(cut, lay.nq)), F32)
    (a0_peer,) = swap(a0_sent)
    sums, b0_own, b0_peer = back(b_own, b_other, save_b, sums)
    a1_done, b1, peer_0, head_peer, a0_own, a0_peer, sums, b0_own, b0_peer = fence(
        a1_done, b1, peer_0, head_peer, a0_own, a0_peer, sums, b0_own, b0_peer
    )
    ins_0 = (k0["normed"], low, k0["mixed"])
    b1 = fold(b1, lay.p1)
    (b0_peer,) = swap(b0_peer)
    a0 = grads_call(a0_own, a0_peer, ins_0, peer_0, heads=(head_1[0], head_peer), head_rows=small_rows)
    back_local, first_row = back_scan_call(0, near, sums[1], rows_all)
    b1, a0, sums, b0_own, b0_peer, back_local, first_row = fence(
        b1, a0, sums, b0_own, b0_peer, back_local, first_row
    )

    held = seq_step(lay, first_row, 1)
    a0 = fold(after(a0, held), lay.p2)
    _, input_grad, (head_own, head_other) = leave(0, k0, sums, (back_local, seq_rest(lay, held)), upstream)
    (head_peer,) = swap(head_other)
    a0, b1, head_own, head_peer = fence(a0, b1, head_own, head_peer)

    a0 = fold(a0, lay.p1)
    b1_parts = fold_parts(b1, lay.q, [], range(cut))
    b0 = grads_call(b0_own, b0_peer, ins_0, peer_0, heads=(head_own, head_peer), head_rows=small_rows)
    a0, b0, b1, b1_parts = fence(a0, b0, b1, b1_parts)

    a0_done = fold(a0, lay.q, F32)
    b0 = fold(b0, lay.p2)
    a0_done, b0, b1, b1_parts = fence(a0_done, b0, b1, b1_parts)

    b1_done = add_parts(fold_parts(b1, lay.q, b1_parts, range(cut, lay.nq)), F32)
    b0 = fold(b0, lay.p1)
    b1_done, b0 = fence(b1_done, b0)
    b0_done = fold(b0, lay.q, F32)

    grads = [cat(a0_done[:, :lanes], b0_done[:, :lanes]), cat(a1_done, b1_done)]
    heads_done = [close_lanes(done[:, lanes:], small_rows) for done in (b0_done, a0_done)]
    vecs = [h[:, width : width + SMALL] for h in heads_done]
    return (
        output,
        input_grad,
        jnp.stack([v[:, 0:2].reshape(-1) for v in vecs]),
        jnp.stack([v[:, 2:4].reshape(-1) for v in vecs]),
        jnp.stack([g[:, :width].T for g in grads]),
        jnp.stack([h[:, :width].T for h in heads_done]),
        jnp.stack([v[:, 4] for v in vecs]),
        jnp.stack([v[:, 5] for v in vecs]),
        jnp.stack([v[:, 6] for v in vecs]),
        jnp.stack([g[:, 2 * width :].T for g in grads]),
        jnp.stack([g[:, width : 2 * width] for g in grads]),
    )


def solution(mesh):
    lay = Layout(mesh)
    both = ("dp", "seq")
    return jax.shard_map(
        functools.partial(local, lay),
        mesh=mesh,
        in_specs=(
            P(both, None),
            P(None, both),
            P(None, both),
            P(None, None, both),
            P(None, None, both),
            P(None, both),
            P(None, both),
            P(None, both),
            P(None, None, both),
            P(None, both, None),
            P(None, "dp", None),
            P("dp", None),
            P(both, None),
        ),
        out_specs=(
            P(both, None),
            P(both, None),
            P(None, both),
            P(None, both),
            P(None, None, both),
            P(None, None, both),
            P(None, both),
            P(None, both),
            P(None, both),
            P(None, None, both),
            P(None, both, None),
        ),
        check_vma=False,
    )
```

```python
import functools
import itertools
import math

import jax
import jax.numpy as jnp
from jax import lax
from jax.experimental import pallas as pl
from jax.experimental.pallas import tpu as pltpu
from jax.sharding import PartitionSpec as P

LAYERS = 2
JOBS = 2
AXES = ("dp", "seq")
BF = jnp.bfloat16
F32 = jnp.float32
VMEM_LIMIT = 24 << 20
C0 = math.sqrt(2.0 / math.pi)
C1 = 0.044715
SMALL = 7
PAD = 128


class Layout:
    def __init__(self, mesh):
        self.dp, self.seq = mesh.shape["dp"], mesh.shape["seq"]
        self.x, self.c = self.dp // 2, 2
        self.s1 = 4
        self.s0 = self.seq // 4
        self.count = self.dp * self.seq
        self.alt_minor = self.s0 == self.x
        self.swap = self.s0 == self.x or self.s1 == self.x
        if self.alt_minor or not self.swap:
            self.alt, self.nq = self.s0, self.s1
        else:
            self.alt, self.nq = self.s1, self.s0
        self.n1, self.n2 = self.alt, self.x
        self.q = [self.pairs(self.move_q, k) for k in range(self.nq)]
        self.p1 = [self.pairs(self.move_1, k) for k in range(self.n1)]
        self.p2 = [self.pairs(self.move_2, k) for k in range(self.n2)]
        self.core = self.pairs(lambda x, c, a, q, k: (x, c ^ 1, a, q), 0)

    def place(self, x, c, a, q):
        s1, s0 = (q, a) if (self.alt_minor or not self.swap) else (a, q)
        return ((x * 2 + c) * self.s1 + s1) * self.s0 + s0

    def pairs(self, move, k):
        spots = itertools.product(range(self.x), range(2), range(self.alt), range(self.nq))
        return [(self.place(*spot), self.place(*move(*spot, k))) for spot in spots]

    def move_q(self, x, c, a, q, k):
        return (x, c, a, q ^ k)

    def move_1(self, x, c, a, q, k):
        return (x ^ k, c, a, q) if (self.swap and c == 1) else (x, c, a ^ k, q)

    def move_2(self, x, c, a, q, k):
        return (x, c, a ^ k, q) if (self.swap and c == 1) else (x ^ k, c, a, q)

    def natural_rows(self, rows):
        me_dp, me_seq = lax.axis_index("dp"), lax.axis_index("seq")
        mx, mc = me_dp // 2, me_dp % 2
        m1, m0 = me_seq // self.s0, me_seq % self.s0
        minor = self.alt_minor or not self.swap
        ma, mq = (m0, m1) if minor else (m1, m0)
        at = jnp.arange(self.count * rows, dtype=jnp.int32)
        row, at = at % rows, at // rows
        kq, at = at % self.nq, at // self.nq
        k1, at = at % self.n1, at // self.n1
        k2, half = at % self.n2, at // self.n2
        core = mc ^ half
        turned = (core == 1) if self.swap else (core > 1)
        kx = jnp.where(turned, k1, k2)
        ka = jnp.where(turned, k2, k1)
        x, a, q = mx ^ kx, ma ^ ka, mq ^ kq
        s1, s0 = (q, a) if minor else (a, q)
        return (((x * 2 + core) * self.s1 + s1) * self.s0 + s0) * rows + row


def permute(array, pairs):
    return lax.ppermute(array, AXES, pairs)


def cat(*arrays):
    return jnp.concatenate(arrays, axis=0)


def after(array, *others):
    return lax.optimization_barrier((array,) + others)[0]


def fence(*arrays):
    return lax.optimization_barrier(arrays)


def close_lanes(block, rows):
    parts = block.reshape(-1, 3, rows, block.shape[1])
    return jnp.concatenate([parts[:, i] for i in range(3)], axis=-1).reshape(-1, 3 * block.shape[1])


def stage(array, pairs):
    return cat(array, *[permute(array, pairs[k]) for k in range(1, len(pairs))])


def add_parts(parts, dtype):
    total = parts[0].astype(F32)
    for part in parts[1:]:
        total = total + part.astype(F32)
    return total.astype(dtype)


def fold(array, pairs, dtype=None):
    count = len(pairs)
    rows = array.shape[0] // count
    parts = [array[:rows]]
    for k in range(1, count):
        parts.append(permute(array[k * rows : (k + 1) * rows], pairs[k]))
    return add_parts(parts, dtype or array.dtype)


def fold_parts(array, pairs, parts, which):
    rows = array.shape[0] // len(pairs)
    cut = {k: array[k * rows : (k + 1) * rows] for k in which}
    return parts + [permute(cut[k], pairs[k]) if k else cut[k] for k in which]


def dot_nn(a, b):
    return jnp.dot(a, b, preferred_element_type=F32)


def dot_nt(a, b):
    return lax.dot_general(a, b, (((1,), (1,)), ((), ())), preferred_element_type=F32)


def dot_tn(a, b):
    return lax.dot_general(a, b, (((0,), (0,)), ((), ())), preferred_element_type=F32)


def gelu(v):
    return 0.5 * v * (1.0 + jnp.tanh(C0 * (v + C1 * v * v * v)))


def gelu_both(v):
    square = v * v
    t = jnp.tanh(C0 * (v + C1 * v * square))
    half = 0.5 * (1.0 + t)
    slope = half + 0.5 * v * (1.0 - t * t) * (C0 * (1.0 + 3.0 * C1 * square))
    return v * half, slope


def full_spec(shape):
    return pl.BlockSpec(memory_space=pltpu.VMEM)


COST = pl.CostEstimate(flops=1000, bytes_accessed=1000, transcendentals=0)
SCALARS = pl.BlockSpec(memory_space=pltpu.SMEM)
VMEM = pl.BlockSpec(memory_space=pltpu.VMEM)


def one_hot(left, right):
    return jnp.where(left == right, 1.0, 0.0).astype(BF)


def column(count):
    return lax.broadcasted_iota(jnp.int32, (count, 1), 0)


def lane(count):
    return lax.broadcasted_iota(jnp.int32, (1, count), 1)


GAIN, SHIFT, RATE, SCALE, SKIP = range(5)


def params_kernel(key_ref, own_ref, other_ref, wr_ref, rows_ref):
    chan, width = wr_ref.shape[1:]
    half = own_ref.shape[0]
    rows_ref[...] = jnp.zeros_like(rows_ref)
    even = one_hot(2 * column(chan), lane(width))
    odd = one_hot(2 * column(chan) + 1, lane(width))
    same = one_hot(column(chan), lane(chan))
    for layer in range(LAYERS):
        key = key_ref[...] - layer * chan
        whole = dot_nn(one_hot(key[:, :half], column(chan)), own_ref[...])
        whole += dot_nn(one_hot(key[:, half:], column(chan)), other_ref[...])
        whole = whole.astype(BF)
        wr_ref[layer] = whole[:, :width]
        vec = whole[:, width:]
        evens, odds = dot_tn(vec, even), dot_tn(vec, odd)
        turned = dot_tn(vec, same)
        rows_ref[layer, GAIN : GAIN + 1, :] = evens[0:1] + odds[1:2]
        rows_ref[layer, SHIFT : SHIFT + 1, :] = evens[2:3] + odds[3:4]
        for name, k in ((RATE, 4), (SCALE, 5), (SKIP, 6)):
            rows_ref[layer, name : name + 1, :chan] = turned[k : k + 1]


def params_call(key, own, other, width, chan):
    return pl.pallas_call(
        params_kernel,
        out_shape=(
            jax.ShapeDtypeStruct((LAYERS, chan, width), BF),
            jax.ShapeDtypeStruct((LAYERS, 8, width), F32),
        ),
        in_specs=[VMEM] * 3,
        out_specs=(VMEM,) * 2,
        compiler_params=pltpu.CompilerParams(vmem_limit_bytes=VMEM_LIMIT),
        cost_estimate=COST,
        name="params",
    )(key, own, other)


def enter_kernel(starts_n, layer, scal, x_ref, rows_ref, wr_ref, normed_ref, pre_ref, local_ref, last_ref):
    x = x_ref[...].astype(F32)
    centred = x - jnp.mean(x, axis=-1, keepdims=True)
    spread = jnp.mean(centred * centred, axis=-1, keepdims=True)
    gain, shift = rows_ref[layer, GAIN : GAIN + 1, :], rows_ref[layer, SHIFT : SHIFT + 1, :]
    normed = (centred * lax.rsqrt(spread + 1e-05) * gain + shift).astype(BF)
    normed_ref[...] = normed
    pre = dot_nt(normed, wr_ref[layer])
    pre_ref[...] = pre
    rows, chan = pre.shape
    rate = rows_ref[layer, RATE : RATE + 1, :chan]
    state = (1.0 - jnp.exp(-rate)) * gelu(pre)
    row = column(rows)
    k = 1
    while k < rows:
        open_rows = row >= k
        for s in range(starts_n):
            open_rows = open_rows & ~((row >= scal[s]) & (row < scal[s] + k))
        factor = jnp.where(open_rows, jnp.exp(-float(k) * rate), 0.0)
        state = state + factor * pltpu.roll(state, k, 0)
        k *= 2
    local_ref[...] = state
    last_ref[...] = state[rows - 1 :]


def enter_call(layer, starts, x, rows_all, wr_all):
    rows, width = x.shape
    chan = wr_all.shape[1]
    return pl.pallas_call(
        functools.partial(enter_kernel, starts.shape[0], layer),
        out_shape=(
            jax.ShapeDtypeStruct((rows, width), BF),
            jax.ShapeDtypeStruct((rows, chan), F32),
            jax.ShapeDtypeStruct((rows, chan), F32),
            jax.ShapeDtypeStruct((1, chan), F32),
        ),
        in_specs=[SCALARS] + [VMEM] * 3,
        out_specs=(VMEM,) * 4,
        compiler_params=pltpu.CompilerParams(vmem_limit_bytes=VMEM_LIMIT),
        cost_estimate=COST,
        name="enter",
    )(starts, x, rows_all, wr_all)


def mix_kernel(starts_n, layer, scal, hops_ref, lasts_ref, start_ref, rows_ref, pre_ref, local_ref, states_ref, in_ref, mixed_ref):
    rows, chan = pre_ref.shape
    rate = rows_ref[layer, RATE : RATE + 1, :chan]
    hops = hops_ref[...]
    weight = jnp.where(hops >= 0.0, jnp.exp(-jnp.maximum(hops, 0.0) * rate), 0.0)
    many = lasts_ref.shape[0]
    entered = jnp.sum(weight[:many] * lasts_ref[...], axis=0, keepdims=True) + weight[many:] * start_ref[...]
    in_ref[...] = entered
    row = column(rows)
    open_rows = row >= 0
    for s in range(starts_n):
        open_rows = open_rows & ~((row >= scal[s]) & (scal[s] >= 0))
    running = jnp.where(open_rows, jnp.exp(-(row + 1).astype(F32) * rate), 0.0)
    states = local_ref[...] + running * entered
    states_ref[...] = states
    scale, skip = rows_ref[layer, SCALE : SCALE + 1, :chan], rows_ref[layer, SKIP : SKIP + 1, :chan]
    mixed_ref[...] = (scale * states + skip * gelu(pre_ref[...])).astype(BF)


def mix_call(layer, starts, hops, lasts, start_state, rows_all, pre, local_states):
    rows, chan = pre.shape
    return pl.pallas_call(
        functools.partial(mix_kernel, starts.shape[0], layer),
        out_shape=(
            jax.ShapeDtypeStruct((rows, chan), F32),
            jax.ShapeDtypeStruct((1, chan), F32),
            jax.ShapeDtypeStruct((rows, chan), BF),
        ),
        in_specs=[SCALARS] + [VMEM] * 6,
        out_specs=(VMEM,) * 3,
        compiler_params=pltpu.CompilerParams(vmem_limit_bytes=VMEM_LIMIT),
        cost_estimate=COST,
        name="mix",
    )(starts, hops, lasts, start_state, rows_all, pre, local_states)


def back_scan_kernel(starts_n, layer, scal, dmix_ref, rows_ref, local_ref, first_ref):
    rows, chan = dmix_ref.shape
    rate = rows_ref[layer, RATE : RATE + 1, :chan]
    grad = rows_ref[layer, SCALE : SCALE + 1, :chan] * dmix_ref[...]
    row = column(rows)
    k = 1
    while k < rows:
        open_rows = row < rows - k
        for s in range(starts_n):
            open_rows = open_rows & ~((row < scal[s]) & (row >= scal[s] - k))
        factor = jnp.where(open_rows, jnp.exp(-float(k) * rate), 0.0)
        grad = grad + factor * pltpu.roll(grad, rows - k, 0)
        k *= 2
    local_ref[...] = grad
    keep = 1.0
    for s in range(starts_n):
        keep = jnp.where(scal[s] == 0, 0.0, keep)
    first_ref[...] = keep * jnp.exp(-rate) * grad[:1]


def back_scan_call(layer, starts, dmix, rows_all):
    rows, chan = dmix.shape
    return pl.pallas_call(
        functools.partial(back_scan_kernel, starts.shape[0], layer),
        out_shape=(jax.ShapeDtypeStruct((rows, chan), F32), jax.ShapeDtypeStruct((1, chan), F32)),
        in_specs=[SCALARS] + [VMEM] * 2,
        out_specs=(VMEM,) * 2,
        compiler_params=pltpu.CompilerParams(vmem_limit_bytes=VMEM_LIMIT),
        cost_estimate=COST,
        name="back_scan",
    )(starts, dmix, rows_all)


def leave_kernel(
    starts_n,
    layer,
    scal,
    hops_ref,
    firsts_ref,
    key_ref,
    key_col_ref,
    dmix_ref,
    local_ref,
    states_ref,
    in_ref,
    pre_ref,
    normed_ref,
    x_ref,
    rows_ref,
    wr_ref,
    dnorm_ref,
    up_ref,
    up_out_ref,
    low_ref,
    own_ref,
    other_ref,
    small,
):
    rows, chan = dmix_ref.shape
    width = x_ref.shape[1]
    rate = rows_ref[layer, RATE : RATE + 1, :chan]
    decay = jnp.exp(-rate)
    hops = hops_ref[...]
    weight = jnp.where(hops >= 0.0, jnp.exp(-jnp.maximum(hops, 0.0) * rate), 0.0)
    arriving = jnp.sum(weight * firsts_ref[...], axis=0, keepdims=True)
    dmix = dmix_ref[...]
    row = column(rows)
    later = row >= 0
    first = row < 0
    for s in range(starts_n):
        later = later & ~((row < scal[s]) & (scal[s] < rows))
        first = first | (row == scal[s])
    running = jnp.where(later, jnp.exp(-(rows - 1 - row).astype(F32) * rate), 0.0)
    grad = local_ref[...] + running * arriving
    reduced, slope = gelu_both(pre_ref[...])
    states = states_ref[...]
    before = jnp.where(row == 0, in_ref[...], pltpu.roll(states, 1, 0))
    before = jnp.where(first, 0.0, before)
    small[...] = jnp.zeros_like(small)
    small[4:5, :chan] = -decay * jnp.sum(grad * (before - reduced), axis=0, keepdims=True)
    small[5:6, :chan] = jnp.sum(dmix * states, axis=0, keepdims=True)
    small[6:7, :chan] = jnp.sum(dmix * reduced, axis=0, keepdims=True)
    d_reduced = (1.0 - decay) * grad + rows_ref[layer, SKIP : SKIP + 1, :chan] * dmix
    d_pre = (d_reduced * slope).astype(BF)
    d_normed = dnorm_ref[...] + dot_nn(d_pre, wr_ref[layer])
    x = x_ref[...].astype(F32)
    centred = x - jnp.mean(x, axis=-1, keepdims=True)
    spread = jnp.mean(centred * centred, axis=-1, keepdims=True)
    rs = lax.rsqrt(spread + 1e-05)
    xhat = centred * rs
    small[0:1, :] = jnp.sum(d_normed * xhat, axis=0, keepdims=True)
    small[2:3, :] = jnp.sum(d_normed, axis=0, keepdims=True)
    e = d_normed * rows_ref[layer, GAIN : GAIN + 1, :]
    mean_e = jnp.mean(e, axis=-1, keepdims=True)
    mean_ex = jnp.mean(e * xhat, axis=-1, keepdims=True)
    up = up_ref[...].astype(F32) + rs * (e - mean_e - xhat * mean_ex)
    up_out_ref[...] = up
    low_ref[...] = up.astype(BF)
    key = key_ref[...]
    turned = dot_nn(d_pre, one_hot(column(chan), key)).astype(BF)
    grads = dot_tn(turned, normed_ref[...]).astype(BF)
    vecs = small[...].astype(BF)
    key_col = key_col_ref[...]
    pick = column(small.shape[0])
    tail = jnp.zeros((chan, PAD), F32)
    for source, at, spot in ((vecs, 2 * key_col, (0, 2)), (vecs, 2 * key_col + 1, (1, 3))):
        wide = dot_nt(one_hot(at, lane(width)), source)
        tail += dot_nn(wide.astype(BF), one_hot(jnp.where(pick == 0, spot[0], jnp.where(pick == 2, spot[1], -1)), lane(PAD)))
    thin = dot_nt(one_hot(key_col, lane(chan)), vecs[:, :chan])
    tail += dot_nn(thin.astype(BF), one_hot(jnp.where((pick >= 4) & (pick < 7), pick, -1), lane(PAD)))
    half = chan // 2
    own_ref[:, :width] = grads[:half]
    other_ref[:, :width] = grads[half:]
    own_ref[:, width:] = tail[:half].astype(BF)
    other_ref[:, width:] = tail[half:].astype(BF)


def leave_call(layer, starts, hops, firsts, key, dmix, local_grad, kept, rows_all, wr_all, dnorm, up):
    rows, width = kept["stream"].shape
    chan = dmix.shape[1]
    head = jax.ShapeDtypeStruct((chan // 2, width + PAD), BF)
    return pl.pallas_call(
        functools.partial(leave_kernel, starts.shape[0], layer),
        out_shape=(
            jax.ShapeDtypeStruct((rows, width), F32),
            jax.ShapeDtypeStruct((rows, width), BF),
            head,
            head,
        ),
        in_specs=[SCALARS] + [VMEM] * 15,
        out_specs=(VMEM,) * 4,
        scratch_shapes=[pltpu.VMEM((16, width), F32)],
        compiler_params=pltpu.CompilerParams(vmem_limit_bytes=VMEM_LIMIT),
        cost_estimate=COST,
        name="leave",
    )(
        starts,
        hops,
        firsts,
        key.reshape(1, chan),
        key.reshape(chan, 1),
        dmix,
        local_grad,
        kept["states"],
        kept["state_in"],
        kept["pre_reduce"],
        kept["normed"],
        kept["stream"],
        rows_all,
        wr_all,
        dnorm,
        up,
    )


def spread_block(head, count, rows, block):
    at = block * count + column(count)
    slot, group, row = at // (3 * rows), (at // rows) % 3, at % rows
    span = head.shape[1] // 3
    total = None
    for g in range(3):
        source = jnp.where(group == g, slot * rows + row, -1)
        part = dot_nn(one_hot(source, lane(head.shape[0])), head[:, g * span : (g + 1) * span])
        total = part if total is None else total + part
    return total.astype(BF)


def wide_kernel(names, mode, blocks, dims, groups, *refs):
    r = dict(zip(names, (groups,) + refs))
    width, chan = dims
    step = pl.program_id(0)
    forward, backward = mode != "back", mode != "fore"
    pair = "other" in r
    weights = r["weights"] if pair else r["own"]

    def part(low, high):
        if len(weights.shape) == 4:
            return weights[:, 0, :, low:high].reshape(-1, high - low)
        return weights[:, low:high]

    w_gate, w_out, w_expand = [functools.partial(part, *at) for at in ((0, width), (width, 2 * width), (2 * width, 2 * width + chan))]

    @pl.when(step == 0)
    def _():
        if forward:
            r["acc"][...] = r["base"][...].astype(F32)
        if backward:
            r["d_normed"][...] = r["d_normed_in"][...] if "d_normed_in" in r else jnp.zeros_like(r["d_normed"])
            r["d_mixed"][...] = r["d_mixed_in"][...] if "d_mixed_in" in r else jnp.zeros_like(r["d_mixed"])

    if pair:

        @pl.when(step < blocks)
        def _():
            weights[...] = r["own"][...]

        @pl.when(step >= blocks)
        def _():
            weights[...] = r["other"][...]

    normed, mixed = r["normed"][...], r["mixed"][...]
    if forward:
        pre = dot_nt(normed, w_gate())
        expanded = dot_nt(mixed, w_expand())
        if mode == "fore":
            r["pre"][...] = pre
            r["expanded"][...] = expanded
    else:
        pre, expanded = r["pre"][...], r["expanded"][...]
    if backward:
        gate, slope = gelu_both(pre)
    else:
        gate = gelu(pre)
    joined = (expanded * gate).astype(BF)
    if forward:
        r["acc"][...] += dot_nn(joined, w_out())
    if backward:
        low = r["low"][...]
        d_joined = dot_nt(low, w_out())
        d_expanded = (d_joined * gate).astype(BF)
        d_pre = (d_joined * expanded * slope).astype(BF)
        r["d_mixed"][...] += dot_nn(d_expanded, w_expand())
        r["d_normed"][...] += dot_nn(d_pre, w_gate())

        def keep(out):
            out[0], out[1], out[2] = d_pre, joined, d_expanded

        @pl.when(step < blocks)
        def _():
            keep(r["acts_first"])

        @pl.when(step >= blocks)
        def _():
            keep(r["acts_last"])

    if "out" in r:

        @pl.when(step == pl.num_programs(0) - 1)
        def _():
            r["out"][...] = r["acc"][...].astype(r["out"].dtype)


def wide_call(mode, own, other, normed, mixed, base=None, low=None, saved=None, sums=None, out_dtype=F32, job=0, groups=None):
    rows, width = normed.shape
    chan = mixed.shape[1]
    pair = groups is None
    if pair:
        groups = jnp.zeros((1,), jnp.int32)
        blocks, block = 2, own.shape[0] // 2
    else:
        blocks = groups.shape[0] // 2
        block = own.shape[0] * own.shape[2] // groups.shape[0]
    lanes = 2 * width + chan
    forward, backward = mode != "back", mode != "fore"
    ins, outs, scratch = [], [], []
    early = lambda i, _: (jnp.minimum(i, blocks - 1), 0)
    late = lambda i, _: (jnp.maximum(i - blocks, 0), 0)
    if pair:
        ins.append(("own", own, pl.BlockSpec((block, lanes), early)))
        ins.append(("other", other, pl.BlockSpec((block, lanes), late)))
    else:
        deep = (block // own.shape[2], 1, own.shape[2], lanes)
        ins.append(("own", own, pl.BlockSpec(deep, lambda i, at: (at[i], job, 0, 0))))
    ins.append(("normed", normed, full_spec(normed.shape)))
    ins.append(("mixed", mixed, full_spec(mixed.shape)))
    side = pl.BlockSpec((rows, block), lambda i, _: (0, i))
    if forward:
        ins.append(("base", base, full_spec(base.shape)))
    if backward:
        ins.append(("low", low, full_spec(low.shape)))
        if sums is not None:
            ins.append(("d_normed_in", sums[0], full_spec(sums[0].shape)))
            ins.append(("d_mixed_in", sums[1], full_spec(sums[1].shape)))
    if mode == "back":
        ins.append(("pre", saved[0], side))
        ins.append(("expanded", saved[1], side))
    if mode == "fore":
        for name in ("pre", "expanded"):
            outs.append((name, jax.ShapeDtypeStruct((rows, 2 * blocks * block), F32), side))
    if forward:
        if out_dtype == F32:
            outs.append(("acc", jax.ShapeDtypeStruct((rows, width), F32), full_spec((rows, width))))
        else:
            outs.append(("out", jax.ShapeDtypeStruct((rows, width), out_dtype), full_spec((rows, width))))
            scratch.append(("acc", pltpu.VMEM((rows, width), F32)))
    if backward:
        outs.append(("d_normed", jax.ShapeDtypeStruct((rows, width), F32), full_spec((rows, width))))
        outs.append(("d_mixed", jax.ShapeDtypeStruct((rows, chan), F32), full_spec((rows, chan))))
        acts = jax.ShapeDtypeStruct((3, rows, blocks * block), BF)
        for name, at in (("acts_first", early), ("acts_last", late)):
            outs.append((name, acts, pl.BlockSpec((3, rows, block), lambda i, _, at=at: (0, 0, at(i, _)[0]))))
    if pair:
        scratch.append(("weights", pltpu.VMEM((block, lanes), BF)))
    names = ["groups"] + [name for name, _, _ in ins + outs] + [name for name, _ in scratch]
    return pl.pallas_call(
        functools.partial(wide_kernel, names, mode, blocks, (width, chan)),
        grid_spec=pltpu.PrefetchScalarGridSpec(
            num_scalar_prefetch=1,
            grid=(2 * blocks,),
            in_specs=[spec for _, _, spec in ins],
            out_specs=tuple(spec for _, _, spec in outs),
            scratch_shapes=[shape for _, shape in scratch],
        ),
        out_shape=tuple(shape for _, shape, _ in outs),
        compiler_params=pltpu.CompilerParams(vmem_limit_bytes=VMEM_LIMIT),
        cost_estimate=COST,
        name="wide_" + mode,
    )(groups, *[array for _, array, _ in ins])


def grads_kernel(names, head_rows, sub, places, *refs):
    r = dict(zip(names, refs))
    step = pl.program_id(0)
    out = r["grads"] if sub else r["out"]
    at = 0
    for k, name in enumerate(("normed", "low", "mixed")):
        span = r[name].shape[1]
        total = dot_tn(r["acts"][k], r[name][...]) + dot_tn(r["peer_acts"][k], r["peer_" + name][...])
        out[:, at : at + span] = total.astype(BF)
        at += span
    if "head" in r:
        head = (r["head"][...].astype(F32) + r["peer_head"][...].astype(F32)).astype(BF)
        out[:, at:] = spread_block(head, out.shape[0], head_rows, step)
    if sub:
        count = out.shape[0] // sub
        for j in range(count):
            to = pl.multiple_of(places[step * count + j] * sub, 16)
            r["out"][pl.ds(to, sub), :] = out[j * sub : (j + 1) * sub, :]


def grads_call(acts, peer_acts, inputs, peer_inputs, places=None, sub=0, heads=None, head_rows=0):
    rows, span = acts.shape[1:]
    steps = 2
    block = span // steps
    ins = []
    for prefix, array, sides in (("", acts, inputs), ("peer_", peer_acts, peer_inputs)):
        ins.append((prefix + "acts", array, pl.BlockSpec((3, rows, block), lambda i, _: (0, 0, i))))
        for name, side in zip(("normed", "low", "mixed"), sides):
            ins.append((prefix + name, side, full_spec(side.shape)))
    lanes = sum(side.shape[1] for side in inputs)
    if heads is not None:
        ins.append(("head", heads[0], full_spec(heads[0].shape)))
        ins.append(("peer_head", heads[1], full_spec(heads[1].shape)))
        lanes += heads[0].shape[1] // 3
    out_spec = full_spec((span, lanes)) if sub else pl.BlockSpec((block, lanes), lambda i, _: (i, 0))
    names = [name for name, _, _ in ins] + ["out"] + (["grads"] if sub else [])
    return pl.pallas_call(
        functools.partial(grads_kernel, names, head_rows, sub),
        grid_spec=pltpu.PrefetchScalarGridSpec(
            num_scalar_prefetch=1,
            grid=(steps,),
            in_specs=[spec for _, _, spec in ins],
            out_specs=out_spec,
            scratch_shapes=[pltpu.VMEM((block, lanes), BF)] if sub else [],
        ),
        out_shape=jax.ShapeDtypeStruct((span, lanes), BF),
        compiler_params=pltpu.CompilerParams(vmem_limit_bytes=VMEM_LIMIT),
        cost_estimate=COST,
        name="grads",
    )(jnp.zeros((1,), jnp.int32) if places is None else places, *[array for _, array, _ in ins])


def seq_step(lay, held, k):
    pairs = [(d * lay.seq + s, d * lay.seq + (s ^ k)) for d in range(lay.dp) for s in range(lay.seq)]
    return cat(held, permute(held, pairs))


def seq_rest(lay, held):
    k = 2
    while k < lay.seq:
        held = seq_step(lay, held, k)
        k *= 2
    return held


def hops_forward(lay, starts, rows):
    me = lax.axis_index("seq")
    source = jnp.concatenate([me ^ jnp.arange(lay.seq, dtype=jnp.int32), jnp.full((1,), -1, jnp.int32)])
    hops = me - 1 - source
    low, high = (source + 1) * rows, me * rows
    hit = jnp.any((starts[None, :] >= low[:, None]) & (starts[None, :] < high), axis=1)
    return jnp.where((hops >= 0) & ~hit, (hops * rows).astype(F32), -1.0)[:, None]


def hops_backward(lay, starts, rows):
    me = lax.axis_index("seq")
    source = me ^ jnp.arange(lay.seq, dtype=jnp.int32)
    hops = source - me - 1
    low, high = (me + 1) * rows, source * rows
    hit = jnp.any((starts[None, :] >= low) & (starts[None, :] < high[:, None]), axis=1)
    return jnp.where((hops >= 0) & ~hit, (hops * rows).astype(F32), -1.0)[:, None]


def local(
    lay,
    tokens,
    ln_gain,
    ln_shift,
    w_gate,
    w_reduce,
    decay_rate,
    state_scale,
    skip_scale,
    w_expand,
    w_out,
    prev_state,
    item_lengths,
    cotangent,
):
    rows, width = tokens.shape
    chan = w_expand.shape[1]
    small_rows = w_reduce.shape[2]
    ff_rows = w_gate.shape[2]
    job_rows = ff_rows // JOBS
    me_seq = lax.axis_index("seq")
    starts = jnp.cumsum(item_lengths[0])[:-1].astype(jnp.int32)
    near = starts - me_seq * rows
    hops_fore, hops_back = hops_forward(lay, starts, rows), hops_backward(lay, starts, rows)

    def vectors(layer):
        return jnp.concatenate(
            [
                ln_gain[layer].reshape(small_rows, 2),
                ln_shift[layer].reshape(small_rows, 2),
                decay_rate[layer][:, None],
                state_scale[layer][:, None],
                skip_scale[layer][:, None],
                jnp.zeros((small_rows, PAD - SMALL), BF),
            ],
            axis=1,
        )

    head = cat(*[jnp.concatenate([w_reduce[i].T, vectors(i)], axis=1) for i in range(LAYERS)])
    bundles = [jnp.concatenate([w_gate[i].T, w_out[i], w_expand[i].T], axis=1) for i in range(LAYERS)]
    shard_a, shard_b, shard_c, shard_d = [
        bundle[job * job_rows : (job + 1) * job_rows] for bundle in bundles for job in range(JOBS)
    ]
    nature = lay.natural_rows(small_rows)
    lanes = bundles[0].shape[1]
    group = jnp.arange(LAYERS, dtype=jnp.int32)[None, :, None] * chan
    key = (nature.reshape(lay.count, 1, small_rows) + group).reshape(1, -1)

    steps = [list(range(1, lay.nq))[i::3] for i in range(3)]

    def pulls(shard, *which):
        return {k: permute(shard, lay.q[k]) for i in which for k in steps[i]}

    def line_of(shard, pulled):
        return cat(shard, *[pulled[k] for k in range(1, lay.nq)])

    def swap(*arrays):
        return [permute(array, lay.core) for array in arrays]

    line_h = stage(head, lay.q)
    pulled = pulls(shard_a, 0)
    line_h, shard_a, pulled = fence(line_h, shard_a, pulled)
    plane_h = stage(line_h, lay.p1)
    pulled |= pulls(shard_a, 1)
    plane_h, shard_a, pulled = fence(plane_h, shard_a, pulled)
    head_own = stage(plane_h, lay.p2)
    pulled |= pulls(shard_a, 2)
    head_own, line_a, shard_b = fence(head_own, line_of(shard_a, pulled), shard_b)
    (head_other,) = swap(head_own)
    plane_a = stage(line_a, lay.p1)
    pulled = pulls(shard_b, 0)
    head_own, head_other, plane_a, shard_b, pulled = fence(head_own, head_other, plane_a, shard_b, pulled)
    wr_all, rows_all = params_call(key, head_own, head_other, width, chan)
    entered = enter_call(0, near, tokens, rows_all, wr_all)

    def enter(layer, stream, entered, lasts):
        normed, pre_reduce, local_states, _ = entered
        states, state_in, mixed = mix_call(
            layer, near, hops_fore, lasts, prev_state[layer], rows_all, pre_reduce, local_states
        )
        return dict(stream=stream, normed=normed, pre_reduce=pre_reduce, states=states, state_in=state_in, mixed=mixed)

    def leave(layer, kept, sums, reached, upstream):
        upstream, low, *head = leave_call(
            layer, near, hops_back, reached[1], nature, sums[1], reached[0], kept, rows_all, wr_all, sums[0], upstream
        )
        return upstream, low, head

    def both(own, other, base, sums, out_dtype=F32):
        out, d_normed, d_mixed, mine, peers = wide_call(
            "both",
            own,
            other,
            k1["normed"],
            k1["mixed"],
            base=base,
            low=cotangent,
            sums=sums,
            out_dtype=out_dtype,
        )
        return out, [d_normed, d_mixed], mine, peers

    def back(own, other, saved, sums):
        d_normed, d_mixed, mine, peers = wide_call(
            "back", own, other, k0["normed"], k0["mixed"], low=low, saved=saved, sums=sums
        )
        return [d_normed, d_mixed], mine, peers

    a_own = stage(plane_a, lay.p2)
    pulled |= pulls(shard_b, 1, 2)
    a_own, line_b, entered, shard_c = fence(a_own, line_of(shard_b, pulled), entered, shard_c)
    held = seq_step(lay, entered[3], 1)
    (a_other,) = swap(a_own)
    plane_b = stage(after(line_b, held), lay.p1)
    lasts = seq_rest(lay, held)
    pulled = pulls(after(shard_c, lasts), 0)
    k0 = enter(0, tokens, entered, lasts)
    a_own, a_other, plane_b, shard_c, pulled, k0 = fence(a_own, a_other, plane_b, shard_c, pulled, k0)
    b_own = stage(plane_b, lay.p2)
    pulled |= pulls(shard_c, 1, 2)
    *save_a, acc = wide_call("fore", a_own, a_other, k0["normed"], k0["mixed"], base=tokens)
    b_own, line_c, acc, shard_d = fence(b_own, line_of(shard_c, pulled), acc, shard_d)
    (b_other,) = swap(b_own)
    plane_c = stage(line_c, lay.p1)
    pulled = pulls(shard_d, 0)
    b_own, b_other, plane_c, shard_d, pulled = fence(b_own, b_other, plane_c, shard_d, pulled)
    c_own = stage(plane_c, lay.p2)
    pulled |= pulls(shard_d, 1, 2)
    *save_b, acc = wide_call("fore", b_own, b_other, k0["normed"], k0["mixed"], base=acc)
    entered = enter_call(1, near, acc, rows_all, wr_all)
    held = seq_step(lay, entered[3], 1)
    c_own, line_d, acc, entered, held = fence(c_own, line_of(shard_d, pulled), acc, entered, held)
    (c_other,) = swap(c_own)
    plane_d = stage(line_d, lay.p1)
    k1 = enter(1, acc, entered, seq_rest(lay, held))
    c_own, c_other, plane_d, k1 = fence(c_own, c_other, plane_d, k1)

    d_own = stage(plane_d, lay.p2)
    ins_1 = (k1["normed"], cotangent, k1["mixed"])
    peer_1 = swap(*ins_1)
    acc, sums, a1_own, a1_peer = both(c_own, c_other, acc, None)
    d_own, acc, sums, a1_own, a1_peer, peer_1 = fence(d_own, acc, sums, a1_own, a1_peer, peer_1)
    (a1_peer,) = swap(a1_peer)
    (d_other,) = swap(d_own)
    a1 = grads_call(a1_own, a1_peer, ins_1, peer_1)
    d_own, d_other, a1 = fence(d_own, d_other, a1)
    a1 = fold(a1, lay.p2)
    output, sums, b1_own, b1_peer = both(d_own, d_other, acc, sums, BF)
    a1, sums, b1_own, b1_peer = fence(a1, sums, b1_own, b1_peer)

    back_local, first_row = back_scan_call(1, near, sums[1], rows_all)
    (b1_peer,) = swap(after(b1_peer, first_row))
    held = seq_step(lay, first_row, 1)
    a1 = fold(after(a1, held), lay.p1)
    b1 = grads_call(b1_own, b1_peer, ins_1, peer_1)
    reached = back_local, seq_rest(lay, after(held, b1))
    upstream, low, head_1 = leave(1, k1, sums, reached, cotangent)
    a1, b1, upstream, low, head_1 = fence(a1, b1, upstream, low, head_1)

    b1 = fold(b1, lay.p2)
    cut = (2 * lay.nq + 2) // 3
    a1_parts = fold_parts(a1, lay.q, [], range(cut))
    peer_0 = swap(k0["normed"], low, k0["mixed"])
    (head_peer,) = swap(head_1[1])
    sums, a0_own, a0_peer = back(a_own, a_other, save_a, None)
    sums, a0_sent, a1, a1_parts = fence(sums, a0_peer, a1, a1_parts)
    a1_done = add_parts(fold_parts(a1, lay.q, a1_parts, range(cut, lay.nq)), F32)
    (a0_peer,) = swap(a0_sent)
    sums, b0_own, b0_peer = back(b_own, b_other, save_b, sums)
    a1_done, b1, peer_0, head_peer, a0_own, a0_peer, sums, b0_own, b0_peer = fence(
        a1_done, b1, peer_0, head_peer, a0_own, a0_peer, sums, b0_own, b0_peer
    )
    ins_0 = (k0["normed"], low, k0["mixed"])
    b1 = fold(b1, lay.p1)
    (b0_peer,) = swap(b0_peer)
    a0 = grads_call(a0_own, a0_peer, ins_0, peer_0, heads=(head_1[0], head_peer), head_rows=small_rows)
    back_local, first_row = back_scan_call(0, near, sums[1], rows_all)
    b1, a0, sums, b0_own, b0_peer, back_local, first_row = fence(
        b1, a0, sums, b0_own, b0_peer, back_local, first_row
    )

    held = seq_step(lay, first_row, 1)
    a0 = fold(after(a0, held), lay.p2)
    _, input_grad, (head_own, head_other) = leave(0, k0, sums, (back_local, seq_rest(lay, held)), upstream)
    (head_peer,) = swap(head_other)
    a0, b1, head_own, head_peer = fence(a0, b1, head_own, head_peer)

    a0 = fold(a0, lay.p1)
    b1_parts = fold_parts(b1, lay.q, [], range(cut))
    b0 = grads_call(b0_own, b0_peer, ins_0, peer_0, heads=(head_own, head_peer), head_rows=small_rows)
    a0, b0, b1, b1_parts = fence(a0, b0, b1, b1_parts)

    a0_done = fold(a0, lay.q, F32)
    b0 = fold(b0, lay.p2)
    a0_done, b0, b1, b1_parts = fence(a0_done, b0, b1, b1_parts)

    b1_done = add_parts(fold_parts(b1, lay.q, b1_parts, range(cut, lay.nq)), F32)
    b0 = fold(b0, lay.p1)
    b1_done, b0 = fence(b1_done, b0)
    b0_done = fold(b0, lay.q, F32)

    grads = [cat(a0_done[:, :lanes], b0_done[:, :lanes]), cat(a1_done, b1_done)]
    heads_done = [close_lanes(done[:, lanes:], small_rows) for done in (b0_done, a0_done)]
    vecs = [h[:, width : width + SMALL] for h in heads_done]
    return (
        output,
        input_grad,
        jnp.stack([v[:, 0:2].reshape(-1) for v in vecs]),
        jnp.stack([v[:, 2:4].reshape(-1) for v in vecs]),
        jnp.stack([g[:, :width].T for g in grads]),
        jnp.stack([h[:, :width].T for h in heads_done]),
        jnp.stack([v[:, 4] for v in vecs]),
        jnp.stack([v[:, 5] for v in vecs]),
        jnp.stack([v[:, 6] for v in vecs]),
        jnp.stack([g[:, 2 * width :].T for g in grads]),
        jnp.stack([g[:, width : 2 * width] for g in grads]),
    )


def solution(mesh):
    lay = Layout(mesh)
    both = ("dp", "seq")
    return jax.shard_map(
        functools.partial(local, lay),
        mesh=mesh,
        in_specs=(
            P(both, None),
            P(None, both),
            P(None, both),
            P(None, None, both),
            P(None, None, both),
            P(None, both),
            P(None, both),
            P(None, both),
            P(None, None, both),
            P(None, both, None),
            P(None, "dp", None),
            P("dp", None),
            P(both, None),
        ),
        out_specs=(
            P(both, None),
            P(both, None),
            P(None, both),
            P(None, both),
            P(None, None, both),
            P(None, None, both),
            P(None, both),
            P(None, both),
            P(None, both),
            P(None, None, both),
            P(None, both, None),
        ),
        check_vma=False,
    )
```
